32 devices in a mesh: dp: 4 (over x, core), ctx: 8 (over z, y).
Axes of the slice: x: 2, y: 2, z: 4, core: 2. Of those that a mesh axis runs over, the one named last changes fastest.
Arguments:
- hidden_in: bfloat16 [4096, 1024], P(('dp', 'ctx')), may hold values from -6 to 6
- document_index: int32 [4, 1024], P('dp', 'ctx'), may hold values from 0 to 2, never falling along the last dimension, each value on 1 to 768 neighbouring positions
- out_grad: bfloat16 [4096, 1024], P(('dp', 'ctx')), may hold values from -6 to 6
- qkv_weight: bfloat16 [2, 1024, 3072], P(None, ('dp', 'ctx')), may hold values from -0.1875 to 0.1875
- value_bias: bfloat16 [2, 1024], P(None, ('dp', 'ctx')), may hold values from -0.119628906 to 0.119628906
- attention_output_weight: bfloat16 [2, 1024, 1024], P(None, ('dp', 'ctx')), may hold values from -4 to 4
- ffn_in_weight: bfloat16 [2, 1024, 4096], P(None, ('dp', 'ctx')), may hold values from -0.1875 to 0.1875
- ffn_out_weight: bfloat16 [2, 4096, 1024], P(None, ('dp', 'ctx')), may hold values from -0.09375 to 0.09375
- biases: bfloat16 [2, 9216], P(None, ('dp', 'ctx')), may hold values from -1.796875 to 1.796875
- norm_gains: bfloat16 [2, 2048], P(None, ('dp', 'ctx')), may hold values from 0.25 to 1.75
Outputs:
- out: bfloat16 [4096, 1024], P(('dp', 'ctx'))
- input_grad: float32 [4096, 1024], P(('dp', 'ctx'))
- qkv_grad: float32 [2, 1024, 3072], P(None, ('dp', 'ctx'))
- value_bias_grad: float32 [2, 1024], P(None, ('dp', 'ctx'))
- attn_out_grad: float32 [2, 1024, 1024], P(None, ('dp', 'ctx'))
- ffn_in_grad: float32 [2, 1024, 4096], P(None, ('dp', 'ctx'))
- ffn_out_grad: float32 [2, 4096, 1024], P(None, ('dp', 'ctx'))
- bias_grad: float32 [2, 9216], P(None, ('dp', 'ctx'))
- gain_grad: float32 [2, 2048], P(None, ('dp', 'ctx'))
The draws below stay inside these ranges and needn't reach their ends.
Inputs may be any that keep to these rules, and one draw needn't show every extreme that they name: `document_index`: within each packed row the numbers never fall; every document holds 1 to 768 tokens, and one holds exactly 768.
All inputs are finite; a program needn't handle non-finite values.
Results may differ from the reference program's by a relative error of at most 0.03.
Values may be sent and summed in bfloat16 or wider, within the bound.
A program may use at most 256 MiB of HBM per device.

```python
import math
import jax
import jax.numpy as jnp
import numpy as np
from jax import lax

MODEL_WIDTH = 1024
ATTENTION_HEADS = 16
FF = 4096
ENCODER_LAYERS = 2
ROW_DOCUMENTS = 3
ROW_LENGTH = 1024
LONGEST_SEGMENT = 768
TOKENS = 4096
N_DP = 4


def block_levels(rng, shape, pieces, smallest, largest):
    loudness, own = 1.0, jax.random.fold_in(rng, 6)
    for axis_at, parts in pieces:
        draws = jnp.exp(jax.random.uniform(jax.random.fold_in(own, axis_at), (parts,), jnp.float32, smallest / len(pieces), largest / len(pieces)))
        loudness = loudness * jnp.repeat(draws, shape[axis_at] // parts).reshape([-1 if axis == axis_at else 1 for axis in range(len(shape))])
    return loudness


def split_up(number_of, total, bound, skew):
    loads = [(1 << 20) // math.isqrt(rank ** skew) + 1 for rank in range(2, number_of + 1)]
    surplus, counts = total - bound - (number_of - 1), [1] * (number_of - 1)
    while surplus > 0:
        free = [i for i in range(number_of - 1) if counts[i] < bound]
        pool, left = sum([loads[i] for i in free]), surplus
        for i in free:
            extra = min(bound - counts[i], max(1, left * loads[i] // pool), surplus)
            counts[i] = counts[i] + extra
            surplus = surplus - extra
    return np.array([bound] + counts)


def ragged(key, amount, total, bound, skew):
    if amount == 2:
        one = jax.random.randint(key, (), max(1, total - bound), min(bound, total - 1) + 1)
        return jnp.stack([one, total - one])
    tallies = jnp.asarray(split_up(amount, total, bound, skew), jnp.int32)
    couples = (amount - 1) // 2
    donor, taker = tallies[1:1 + 2 * couples:2], tallies[2:2 + 2 * couples:2]
    slack = jnp.minimum(donor - 1, bound - taker)
    passed = jax.random.randint(jax.random.fold_in(key, 1), (couples,), 0, 1 << 20) % (slack + 1)
    tallies = tallies.at[1:1 + 2 * couples:2].set(donor - passed).at[2:2 + 2 * couples:2].set(taker + passed)
    return tallies[jax.random.permutation(jax.random.fold_in(key, 2), amount)]


def bell_draw(own_key, dims, spread, bound, split=(), dtype=jnp.bfloat16):
    loudness = block_levels(own_key, dims, split, -0.22, 0.18) if split else 1.0
    drawn = jax.random.normal(own_key, dims, jnp.float32) * spread * loudness
    return jnp.minimum(jnp.maximum(drawn, -bound), bound).astype(dtype)


def setup_inputs(seed: int = 0) -> dict:
    streams_of = jax.random.split(jax.random.key(seed), 11)
    return {
        "hidden_in": bell_draw(streams_of[0], (TOKENS, MODEL_WIDTH), 1.0, 6.0, ((0, 32),)),
        "document_index": jax.vmap(lambda own: jnp.searchsorted(jnp.cumsum(ragged(own, ROW_DOCUMENTS, ROW_LENGTH, LONGEST_SEGMENT, 0)), jnp.arange(ROW_LENGTH), side="right"))(jax.random.split(streams_of[1], N_DP)).reshape((N_DP, ROW_LENGTH)).astype(jnp.int32),
        "out_grad": bell_draw(streams_of[2], (TOKENS, MODEL_WIDTH), 1.0, 6.0, ((0, 32),)),
        "qkv_weight": bell_draw(streams_of[3], (ENCODER_LAYERS, MODEL_WIDTH, 3 * MODEL_WIDTH), MODEL_WIDTH ** -0.5, 0.1875, ((1, 32),)),
        "value_bias": bell_draw(streams_of[4], (ENCODER_LAYERS, MODEL_WIDTH), 0.02, 0.119628906, ((1, 32),)),
        "attention_output_weight": bell_draw(streams_of[5], (ENCODER_LAYERS, MODEL_WIDTH, MODEL_WIDTH), (max(1, 2 * MODEL_WIDTH // ROW_LENGTH)) ** -0.5, 4.0, ((1, 32),)),
        "ffn_in_weight": bell_draw(streams_of[6], (ENCODER_LAYERS, MODEL_WIDTH, FF), MODEL_WIDTH ** -0.5, 0.1875, ((1, 32),)),
        "ffn_out_weight": bell_draw(streams_of[7], (ENCODER_LAYERS, FF, MODEL_WIDTH), FF ** -0.5, 0.09375, ((1, 32),)),
        "biases": bell_draw(streams_of[8], (ENCODER_LAYERS, 5 * MODEL_WIDTH + FF), 0.3, 1.796875, ((1, 32),)),
        "norm_gains": jnp.clip(1.0 + 0.15 * jax.random.normal(streams_of[9], (ENCODER_LAYERS, 2 * MODEL_WIDTH), jnp.float32), 0.25, 1.75).astype(jnp.bfloat16),
    }


EPS = 1e-12
NEGATIVE = -1e+30
HIGH = lax.Precision.HIGHEST

@jax.custom_vjp
def low(v):
    return lax.optimization_barrier(v.astype(jnp.bfloat16)).astype(jnp.float32)

@jax.custom_vjp
def low_back(v):
    return v

def low_keep(v):
    return (low(v), None)

def low_pass(kept, grad):
    return (grad,)

def back_keep(v):
    return (v, None)

def back_low(kept, grad):
    return (low(grad),)
low.defvjp(low_keep, low_pass)
low_back.defvjp(back_keep, back_low)

def norm_rows(resid, gain, shift):
    mean = lax.optimization_barrier(jnp.mean(resid, axis=-1, keepdims=True))
    centered = resid - mean
    variance = lax.optimization_barrier(jnp.mean(centered * centered, axis=-1, keepdims=True))
    return centered * lax.rsqrt(variance + EPS) * gain + shift

def one_block(query_block, seg_block, split_key_heads, split_value_heads, segment_row):
    scale = (MODEL_WIDTH // ATTENTION_HEADS) ** (-0.5)
    raw = jnp.einsum('qhd,khd->hqk', query_block, split_key_heads, precision=HIGH) * scale
    raw = low_back(raw)
    mask = (seg_block[:, None] == segment_row[None, :])[None]
    probs = jax.nn.softmax(jnp.where(mask, raw, NEGATIVE), axis=-1)
    return jnp.einsum('hqk,khd->qhd', low(probs), split_value_heads, precision=HIGH)

def attend_row(packed):
    query_matrix, key_rows, value_rows, segment_row = packed
    token_block = min(512, ROW_LENGTH)
    head_width = MODEL_WIDTH // ATTENTION_HEADS
    split_key_heads = key_rows.reshape(ROW_LENGTH, ATTENTION_HEADS, head_width)
    split_value_heads = value_rows.reshape(ROW_LENGTH, ATTENTION_HEADS, head_width)
    checked = jax.checkpoint(one_block)
    token_blocks = (query_matrix.reshape(ROW_LENGTH // token_block, token_block, ATTENTION_HEADS, head_width), segment_row.reshape(ROW_LENGTH // token_block, token_block))
    layer_result = lax.map(lambda item: checked(item[0], item[1], split_key_heads, split_value_heads, segment_row), token_blocks)
    return layer_result.reshape(ROW_LENGTH, MODEL_WIDTH)

def forward(state, qkv_weight, value_bias, attention_output_weight, ffn_in_weight, ffn_out_weight, biases, norm_gains, document_index):
    for layer in range(ENCODER_LAYERS):
        bias_all = biases[layer]
        query_bias = bias_all[0:MODEL_WIDTH]
        out_bias = bias_all[MODEL_WIDTH:2 * MODEL_WIDTH]
        inner_bias = bias_all[2 * MODEL_WIDTH:2 * MODEL_WIDTH + FF]
        ffn_bias = bias_all[2 * MODEL_WIDTH + FF:3 * MODEL_WIDTH + FF]
        shift_one = bias_all[3 * MODEL_WIDTH + FF:4 * MODEL_WIDTH + FF]
        shift_two = bias_all[4 * MODEL_WIDTH + FF:5 * MODEL_WIDTH + FF]
        gain_one = norm_gains[layer, 0:MODEL_WIDTH]
        gain_two = norm_gains[layer, MODEL_WIDTH:2 * MODEL_WIDTH]
        state_low = low(state)
        qkv_bias = jnp.concatenate([query_bias, jnp.zeros_like(query_bias), value_bias[layer]])
        query_key_value = low(low_back(jnp.dot(state_low, qkv_weight[layer], precision=HIGH) + qkv_bias))
        query_matrix = query_key_value[:, 0:MODEL_WIDTH].reshape(N_DP, ROW_LENGTH, MODEL_WIDTH)
        key_rows = query_key_value[:, MODEL_WIDTH:2 * MODEL_WIDTH].reshape(N_DP, ROW_LENGTH, MODEL_WIDTH)
        value_rows = query_key_value[:, 2 * MODEL_WIDTH:3 * MODEL_WIDTH].reshape(N_DP, ROW_LENGTH, MODEL_WIDTH)
        context = lax.map(attend_row, (query_matrix, key_rows, value_rows, document_index)).reshape(TOKENS, MODEL_WIDTH)
        context = low(low_back(context))
        branch = low_back(jnp.dot(context, attention_output_weight[layer], precision=HIGH) + out_bias)
        normed = norm_rows(state + branch, gain_one, shift_one)
        pre = low_back(jnp.dot(low(normed), ffn_in_weight[layer], precision=HIGH) + inner_bias)
        inner = low(jax.nn.gelu(pre, approximate=False))
        second = low_back(jnp.dot(inner, ffn_out_weight[layer], precision=HIGH) + ffn_bias)
        state = norm_rows(normed + second, gain_two, shift_two)
    return state

def reference(hidden_in, document_index, out_grad, qkv_weight, value_bias, attention_output_weight, ffn_in_weight, ffn_out_weight, biases, norm_gains):
    inputs = tuple((item.astype(jnp.float32) for item in (hidden_in, qkv_weight, value_bias, attention_output_weight, ffn_in_weight, ffn_out_weight, biases, norm_gains)))

    def run(state, w_qkv, v_bias, w_out, w_in, w_ffo, bias_all, gains):
        return forward(state, w_qkv, v_bias, w_out, w_in, w_ffo, bias_all, gains, document_index)
    layer_result, pull = jax.vjp(run, *inputs)
    grads = pull(out_grad.astype(jnp.float32))
    return (layer_result.astype(jnp.bfloat16), grads[0], grads[1], grads[2], grads[3], grads[4], grads[5], grads[6], grads[7])
```

```python
import math
import types

import jax
import jax.numpy as jnp
from jax import lax
from jax.experimental import pallas as pl
from jax.experimental.pallas import tpu as pltpu
from jax.sharding import PartitionSpec as P

ATTENTION_HEADS = 16


DP, CTX = "dp", "ctx"
BOTH = (DP, CTX)

QUERY_KEY, TO_QUERY, TO_KEY = "qhd,khd->hqk", "hqk,khd->qhd", "hqk,qhd->khd"
EPS = 1e-12
NEGATIVE = -1e30


def norm_rows(resid, gain, shift):
    mean = jnp.mean(resid, axis=-1, keepdims=True)
    centered = resid - mean
    variance = jnp.mean(centered * centered, axis=-1, keepdims=True)
    return centered * lax.rsqrt(variance + EPS) * gain + shift


def exact_gelu(value):
    return jax.nn.gelu(value, approximate=False)


def cross(left, right_operand):
    return lax.dot_general(
        left, right_operand, (((0,), (0,)), ((), ())), preferred_element_type=jnp.float32
    )


def back_product(upstream, weight):
    return lax.dot_general(
        upstream, weight, (((1,), (1,)), ((), ())), preferred_element_type=jnp.float32
    )


def by_blocks(step_fn, carry, pieces, token_block):
    count = pieces[0].shape[0]

    def turn(index, state):
        offset = index * token_block
        parts = tuple((lax.dynamic_slice_in_dim(item, offset, token_block, 0) for item in pieces))
        return step_fn(state, parts, offset)

    return lax.fori_loop(0, count // token_block, turn, carry)


def unpack(fetched, width, inner):
    w_qkv, w_out, w_in, w_ffo, value_vec, bias_all, gains = fetched
    value_vec = value_vec.astype(jnp.float32)
    bias_all = bias_all.astype(jnp.float32)
    gains = gains.astype(jnp.float32)
    query_bias = bias_all[0:width]
    out_bias = bias_all[width : 2 * width]
    inner_bias = bias_all[2 * width : 2 * width + inner]
    ffn_bias = bias_all[2 * width + inner : 3 * width + inner]
    shift_one = bias_all[3 * width + inner : 4 * width + inner]
    shift_two = bias_all[4 * width + inner : 5 * width + inner]
    return (
        w_qkv,
        w_out,
        w_in,
        w_ffo,
        value_vec,
        query_bias,
        out_bias,
        inner_bias,
        ffn_bias,
        shift_one,
        shift_two,
        gains[0:width],
        gains[width : 2 * width],
    )


def masked_scores(query_heads, key_piece, seg_own, segment_row, start, scale):
    count = key_piece.shape[0]
    heads = query_heads.shape[1]
    split_key_heads = key_piece.reshape(count, heads, query_heads.shape[2])
    seg_keys = lax.dynamic_slice_in_dim(segment_row, start, count, 0)
    mask = (seg_own[:, None] == seg_keys[None, :])[None]
    raw = (
        jnp.einsum(QUERY_KEY, query_heads, split_key_heads, preferred_element_type=jnp.float32)
        * scale
    )
    return (jnp.where(mask, raw, NEGATIVE), mask, split_key_heads)


def body(
    hidden_in,
    document_index,
    out_grad,
    qkv_weight,
    value_bias,
    attention_output_weight,
    ffn_in_weight,
    ffn_out_weight,
    biases,
    norm_gains,
):
    layers = qkv_weight.shape[0]
    width = qkv_weight.shape[2] // 3
    inner = ffn_in_weight.shape[2]
    heads = ATTENTION_HEADS
    head_width = width // heads
    scale = head_width ** (-0.5)
    rows = hidden_in.shape[0]
    seg_own = document_index[0]
    segment_row = lax.all_gather(document_index, CTX, axis=1, tiled=True)[0]
    row_len = segment_row.shape[0]
    state = hidden_in.astype(jnp.float32)
    saved = []
    for layer in range(layers):
        fetched = (
            lax.all_gather(qkv_weight[layer], BOTH, axis=0, tiled=True),
            lax.all_gather(attention_output_weight[layer], BOTH, axis=0, tiled=True),
            lax.all_gather(ffn_in_weight[layer], BOTH, axis=0, tiled=True),
            lax.all_gather(ffn_out_weight[layer], BOTH, axis=0, tiled=True),
            lax.all_gather(value_bias[layer], BOTH, axis=0, tiled=True),
            lax.all_gather(biases[layer], BOTH, axis=0, tiled=True),
            lax.all_gather(norm_gains[layer], BOTH, axis=0, tiled=True),
        )
        (
            w_qkv,
            w_out,
            w_in,
            w_ffo,
            value_vec,
            query_bias,
            out_bias,
            inner_bias,
            ffn_bias,
            shift_one,
            shift_two,
            gain_one,
            gain_two,
        ) = unpack(fetched, width, inner)
        state_low = state.astype(jnp.bfloat16)
        qkv_bias = jnp.concatenate([query_bias, jnp.zeros_like(query_bias), value_vec])
        qkv_low = (jnp.dot(state_low, w_qkv, preferred_element_type=jnp.float32) + qkv_bias).astype(
            jnp.bfloat16
        )
        query_heads = qkv_low[:, 0:width].reshape(rows, heads, head_width)
        key_low = qkv_low[:, width : 2 * width]
        value_low = qkv_low[:, 2 * width : 3 * width]

        def stats_step(carry, parts, start):
            top, total = carry
            raw, mask, split_key_heads = masked_scores(
                query_heads, parts[0], seg_own, segment_row, start, scale
            )
            new_top = jnp.maximum(top, jnp.max(raw, axis=-1))
            weights = jnp.where(mask, jnp.exp(raw - new_top[:, :, None]), 0.0)
            return (new_top, total * jnp.exp(top - new_top) + jnp.sum(weights, axis=-1))

        stats_init = (
            jnp.full((heads, rows), NEGATIVE, jnp.float32),
            jnp.zeros((heads, rows), jnp.float32),
        )
        held_pair = None
        top, total = by_blocks(
            stats_step, stats_init, (lax.all_gather(key_low, CTX, axis=0, tiled=True),), rows
        )
        log_total = top + jnp.log(total)

        def value_step(carry, parts, start):
            context_acc, exact_acc = carry
            raw, mask, split_key_heads = masked_scores(
                query_heads, parts[0], seg_own, segment_row, start, scale
            )
            split_value_heads = parts[1].reshape(parts[1].shape[0], heads, head_width)
            probs = jnp.where(mask, jnp.exp(raw - log_total[:, :, None]), 0.0)
            probs_low = probs.astype(jnp.bfloat16)
            residue_low = (probs - probs_low.astype(jnp.float32)).astype(jnp.bfloat16)
            part_low = jnp.einsum(
                TO_QUERY, probs_low, split_value_heads, preferred_element_type=jnp.float32
            )
            part_fix = jnp.einsum(
                TO_QUERY, residue_low, split_value_heads, preferred_element_type=jnp.float32
            )
            return (context_acc + part_low, exact_acc + part_fix)

        value_init = (
            jnp.zeros((rows, heads, head_width), jnp.float32),
            jnp.zeros((rows, heads, head_width), jnp.float32),
        )
        context, correction = by_blocks(
            value_step,
            value_init,
            (
                lax.all_gather(key_low, CTX, axis=0, tiled=True),
                lax.all_gather(value_low, CTX, axis=0, tiled=True),
            ),
            rows,
        )
        context_exact = (context + correction).reshape(rows, width)
        context = context.reshape(rows, width)
        context_low = context.astype(jnp.bfloat16)
        resid_one = (
            state + jnp.dot(context_low, w_out, preferred_element_type=jnp.float32) + out_bias
        )
        normed = norm_rows(resid_one, gain_one, shift_one)
        normed_low = normed.astype(jnp.bfloat16)
        pre = jnp.dot(normed_low, w_in, preferred_element_type=jnp.float32) + inner_bias
        inner_low = exact_gelu(pre).astype(jnp.bfloat16)
        resid_two = (
            normed + jnp.dot(inner_low, w_ffo, preferred_element_type=jnp.float32) + ffn_bias
        )
        saved.append(
            (
                fetched,
                state_low,
                qkv_low,
                log_total,
                context_exact,
                context_low,
                resid_one,
                normed_low,
                pre,
                inner_low,
                resid_two,
                held_pair,
            )
        )
        state = norm_rows(resid_two, gain_two, shift_two)
    upstream = out_grad.astype(jnp.float32)
    per_layer = []
    for layer in reversed(range(layers)):
        (
            fetched,
            state_low,
            qkv_low,
            log_total,
            context_exact,
            context_low,
            resid_one,
            normed_low,
            pre,
            inner_low,
            resid_two,
            held_pair,
        ) = saved[layer]
        weights_now = (
            lax.all_gather(qkv_weight[layer], BOTH, axis=0, tiled=True),
            lax.all_gather(attention_output_weight[layer], BOTH, axis=0, tiled=True),
            lax.all_gather(ffn_in_weight[layer], BOTH, axis=0, tiled=True),
            lax.all_gather(ffn_out_weight[layer], BOTH, axis=0, tiled=True),
            lax.all_gather(value_bias[layer], BOTH, axis=0, tiled=True),
            lax.all_gather(biases[layer], BOTH, axis=0, tiled=True),
            lax.all_gather(norm_gains[layer], BOTH, axis=0, tiled=True),
        )
        (
            w_qkv,
            w_out,
            w_in,
            w_ffo,
            value_vec,
            query_bias,
            out_bias,
            inner_bias,
            ffn_bias,
            shift_one,
            shift_two,
            gain_one,
            gain_two,
        ) = unpack(weights_now, width, inner)
        query_low = qkv_low[:, 0:width]
        query_heads = query_low.reshape(rows, heads, head_width)
        key_low = qkv_low[:, width : 2 * width]
        value_low = qkv_low[:, 2 * width : 3 * width]
        unused_two, pull_two = jax.vjp(norm_rows, resid_two, gain_two, shift_two)
        back_two, back_gain_two, back_shift_two = pull_two(upstream)
        back_second = back_two.astype(jnp.bfloat16)
        grad_second = cross(inner_low, back_second)
        back_inner = back_product(back_second, w_ffo)
        unused_pre, pull_gelu = jax.vjp(exact_gelu, pre)
        back_pre = pull_gelu(back_inner)[0].astype(jnp.bfloat16)
        grad_first = cross(normed_low, back_pre)
        back_normed = back_two + back_product(back_pre, w_in)
        normed_again, pull_one = jax.vjp(norm_rows, resid_one, gain_one, shift_one)
        back_one, back_gain_one, back_shift_one = pull_one(back_normed)
        back_branch = back_one.astype(jnp.bfloat16)
        grad_out_proj = cross(context_low, back_branch)
        back_context = back_product(back_branch, w_out).astype(jnp.bfloat16)
        context_heads_back = back_context.reshape(rows, heads, head_width)
        delta = jnp.sum(
            (back_context.astype(jnp.float32) * context_exact).reshape(rows, heads, head_width),
            axis=-1,
        ).T

        def grad_step(carry, parts, start):
            query_sum, key_sums, value_sums = carry
            count = parts[0].shape[0]
            raw, mask, split_key_heads = masked_scores(
                query_heads, parts[0], seg_own, segment_row, start, scale
            )
            split_value_heads = parts[1].reshape(count, heads, head_width)
            probs = jnp.where(mask, jnp.exp(raw - log_total[:, :, None]), 0.0)
            back_probs = jnp.einsum(
                QUERY_KEY,
                context_heads_back,
                split_value_heads,
                preferred_element_type=jnp.float32,
            )
            back_scores = (probs * (back_probs - delta[:, :, None])).astype(jnp.bfloat16)
            query_part = (
                jnp.einsum(
                    TO_QUERY, back_scores, split_key_heads, preferred_element_type=jnp.float32
                )
                * scale
            )
            key_part = (
                jnp.einsum(
                    TO_KEY, back_scores, query_heads, preferred_element_type=jnp.float32
                ).reshape(count, width)
                * scale
            )
            value_part = jnp.einsum(
                TO_KEY,
                probs.astype(jnp.bfloat16),
                context_heads_back,
                preferred_element_type=jnp.float32,
            ).reshape(count, width)
            key_sums = lax.dynamic_update_slice_in_dim(
                key_sums, lax.dynamic_slice_in_dim(key_sums, start, count, 0) + key_part, start, 0
            )
            value_sums = lax.dynamic_update_slice_in_dim(
                value_sums,
                lax.dynamic_slice_in_dim(value_sums, start, count, 0) + value_part,
                start,
                0,
            )
            return (query_sum + query_part, key_sums, value_sums)

        query_init = jnp.zeros((rows, heads, head_width), jnp.float32)
        grad_init = (
            query_init,
            jnp.zeros((row_len, width), jnp.float32),
            jnp.zeros((row_len, width), jnp.float32),
        )
        folded = by_blocks(
            grad_step,
            grad_init,
            (
                lax.all_gather(key_low, CTX, axis=0, tiled=True),
                lax.all_gather(value_low, CTX, axis=0, tiled=True),
            ),
            rows,
        )
        query_sum, key_sums, value_sums = folded
        key_own, value_own = (
            lax.psum_scatter(
                key_sums.astype(jnp.bfloat16), CTX, scatter_dimension=0, tiled=True
            ).astype(jnp.float32),
            lax.psum_scatter(
                value_sums.astype(jnp.bfloat16), CTX, scatter_dimension=0, tiled=True
            ).astype(jnp.float32),
        )
        back_qkv = jnp.concatenate(
            [query_sum.reshape(rows, width), key_own, value_own], axis=1
        ).astype(jnp.bfloat16)
        grad_qkv = cross(state_low, back_qkv)
        back_qkv_float = back_qkv.astype(jnp.float32)
        grad_value_bias = jnp.sum(back_qkv_float[:, 2 * width : 3 * width], axis=0)
        grad_bias = jnp.concatenate(
            [
                jnp.sum(back_qkv_float[:, 0:width], axis=0),
                jnp.sum(back_branch.astype(jnp.float32), axis=0),
                jnp.sum(back_pre.astype(jnp.float32), axis=0),
                jnp.sum(back_second.astype(jnp.float32), axis=0),
                back_shift_one,
                back_shift_two,
            ]
        )
        grad_gain = jnp.concatenate([back_gain_one, back_gain_two])
        upstream = back_one + back_product(back_qkv, w_qkv)
        shards = (
            lax.psum_scatter(grad_qkv, BOTH, scatter_dimension=0, tiled=True),
            lax.psum_scatter(grad_value_bias, BOTH, scatter_dimension=0, tiled=True),
            lax.psum_scatter(grad_out_proj, BOTH, scatter_dimension=0, tiled=True),
            lax.psum_scatter(grad_first, BOTH, scatter_dimension=0, tiled=True),
            lax.psum_scatter(grad_second, BOTH, scatter_dimension=0, tiled=True),
            lax.psum_scatter(grad_bias, BOTH, scatter_dimension=0, tiled=True),
            lax.psum_scatter(grad_gain, BOTH, scatter_dimension=0, tiled=True),
        )
        per_layer.append(shards)
    ordered = per_layer[::-1]
    stacked = tuple((jnp.stack([item[member] for item in ordered]) for member in range(7)))
    return (
        state.astype(jnp.bfloat16),
        upstream,
        stacked[0],
        stacked[1],
        stacked[2],
        stacked[3],
        stacked[4],
        stacked[5],
        stacked[6],
    )


MESH = pl.DeviceIdType.MESH
F32 = jnp.float32
BF16 = jnp.bfloat16
VMEM = pltpu.VMEM
ANY = pl.ANY
VMEM_LIMIT = 56 * 2**20
OWN, XN, YN, DIAG = range(4)


def dot_nn(a, b):
    return lax.dot_general(a, b, (((1,), (0,)), ((), ())), preferred_element_type=F32)


def dot_nt(a, b):
    return lax.dot_general(a, b, (((1,), (1,)), ((), ())), preferred_element_type=F32)


def dot_tn(a, b):
    return lax.dot_general(a, b, (((0,), (0,)), ((), ())), preferred_element_type=F32)


def place():
    d, t = lax.axis_index(DP), lax.axis_index(CTX)
    x, c = lax.div(d, 2), lax.rem(d, 2)
    z, y = lax.div(t, 2), lax.rem(t, 2)
    w = types.SimpleNamespace(d=d, x=x, c=c, z=z, y=y)
    w.part = d * 2 + y
    w.group = (x * 2 + y, (1 - x) * 2 + y, x * 2 + 1 - y, (1 - x) * 2 + 1 - y)
    w.xn, w.yn, w.sib = ((1 - x) * 2 + c, t), (d, z * 2 + 1 - y), (x * 2 + 1 - c, t)
    w.zs = [(d, lax.rem(z + k, 4) * 2 + y) for k in (1, 2, 3)]
    w.plane = []
    for bits in range(1, 8):
        xx = 1 - x if bits & 4 else x
        cc = 1 - c if bits & 2 else c
        yy = 1 - y if bits & 1 else y
        w.plane.append(((xx * 2 + cc, z * 2 + yy), (xx * 2 + cc) * 2 + yy))
    w.swap = (z, d * 2 + y)
    return w


class Net:
    def __init__(self, ssem, rsem, lsem):
        self.ssem, self.rsem, self.lsem = ssem, rsem, lsem
        self.sent, self.kept, self.swaps = [], [], []
        self.at = 0

    def greet(self, devices, w, swap=False):
        barrier = pltpu.get_barrier_semaphore()
        for device in devices:
            pl.semaphore_signal(barrier, inc=1, device_id=device, device_id_type=MESH)
        more = 0
        if swap:
            more = jnp.where(w.d != w.z, 1, 0)

            @pl.when(w.d != w.z)
            def _():
                pl.semaphore_signal(barrier, inc=1, device_id=w.swap, device_id_type=MESH)

        pl.semaphore_wait(barrier, len(devices) + more)

    def make(self, src, dst, device):
        copy = pltpu.make_async_remote_copy(
            src_ref=src,
            dst_ref=dst,
            send_sem=self.ssem.at[self.at],
            recv_sem=self.rsem.at[self.at],
            device_id=device,
            device_id_type=MESH,
        )
        self.at += 1
        return copy

    def send(self, src, dst, device):
        copy = self.make(src, dst, device)
        copy.start()
        self.sent.append(copy)
        return copy

    def local(self, src, dst):
        copy = pltpu.make_async_copy(src, dst, self.lsem.at[len(self.kept)])
        copy.start()
        self.kept.append(copy)
        return copy

    def swap(self, w, src, dst):
        far = self.make(src, dst, w.swap)
        near = pltpu.make_async_copy(src, dst, self.lsem.at[len(self.kept)])
        self.kept.append(None)

        @pl.when(w.d != w.z)
        def _():
            far.start()

        @pl.when(w.d == w.z)
        def _():
            near.start()

        def wait():
            @pl.when(w.d != w.z)
            def _():
                far.wait()

            @pl.when(w.d == w.z)
            def _():
                near.wait()

        return wait

    def z_gather(self, w, src, at):
        copies = [self.send(src, at(w.z), device) for device in w.zs]
        own = self.local(src, at(w.z))

        def wait():
            own.wait()
            for copy in copies:
                copy.wait_recv()

        return wait

    def z_scatter(self, w, at, land):
        copies = [
            self.send(at(lax.rem(w.z + k + 1, 4)), land.at[k], device)
            for k, device in enumerate(w.zs)
        ]
        own = self.local(at(w.z), land.at[3])

        def wait():
            own.wait()
            for copy in copies:
                copy.wait_recv()

        return wait

    def plane_swap(self, w, at, to):
        copies = [self.send(at(part), to(w.part), device) for device, part in w.plane]
        own = self.local(at(w.part), to(w.part))

        def wait():
            own.wait()
            for copy in copies:
                copy.wait_recv()

        return wait

    def finish(self):
        for copy in self.sent:
            copy.wait_send()


def gather(net, w, buf, on_group, after_start):
    def half(group, h):
        return buf.at[pl.ds(pl.multiple_of((group * 2 + w.c) * 128 + h * 64, 64), 64)]

    def put(group, h, device):
        ref = half(group, h)
        return net.send(ref, ref, device)

    own, xn, yn, diag = w.group
    x0 = put(own, 0, w.xn)
    y1 = put(own, 1, w.yn)
    whole = buf.at[pl.ds(pl.multiple_of((own * 2 + w.c) * 128, 128), 128)]
    c0 = net.send(whole, whole, w.sib)
    x1 = put(own, 1, w.xn)
    y0 = put(own, 0, w.yn)
    after_start()
    c0.wait_recv()
    on_group(OWN)
    x0.wait_recv()
    d0 = put(xn, 0, w.yn)
    cx0 = put(xn, 0, w.sib)
    y1.wait_recv()
    d1 = put(yn, 1, w.xn)
    cy1 = put(yn, 1, w.sib)
    x1.wait_recv()
    cx1 = put(xn, 1, w.sib)
    y0.wait_recv()
    cy0 = put(yn, 0, w.sib)
    cx0.wait_recv()
    cx1.wait_recv()
    on_group(XN)
    cy0.wait_recv()
    cy1.wait_recv()
    on_group(YN)
    d0.wait_recv()
    cd0 = put(diag, 0, w.sib)
    d1.wait_recv()
    cd1 = put(diag, 1, w.sib)
    cd0.wait_recv()
    cd1.wait_recv()
    on_group(DIAG)


class Reduce:
    def __init__(self, net, w, r, part):
        self.net, self.w, self.r, self.part = net, w, r, part
        self.cores = dict()

    def produce(self, kind):
        w, r, k = self.w, self.r, kind
        group = w.group[kind]
        r.core_out[k] = self.part(group * 2 + 1 - w.c).astype(BF16)
        self.cores[kind] = self.net.send(r.core_out.at[k], r.core_in.at[k], w.sib)
        r.keep[k] = self.part(group * 2 + w.c)

    def diag(self):
        w, r = self.w, self.r
        self.cores[DIAG].wait_recv()
        r.far[...] = (r.keep[3] + r.core_in[3].astype(F32)).astype(BF16)
        self.fy = self.net.send(r.far.at[pl.ds(0, 64)], r.via_y, w.yn)
        self.fx = self.net.send(r.far.at[pl.ds(64, 64)], r.via_x, w.xn)

    def first(self):
        w, r = self.w, self.r
        self.cores[XN].wait_recv()
        r.out_x[64:128] = (r.keep[1, 64:128] + r.core_in[1, 64:128].astype(F32)).astype(BF16)
        self.x1 = self.net.send(r.out_x.at[pl.ds(64, 64)], r.in_x.at[pl.ds(64, 64)], w.xn)
        self.cores[YN].wait_recv()
        r.out_y[0:64] = (r.keep[2, 0:64] + r.core_in[2, 0:64].astype(F32)).astype(BF16)
        self.y0 = self.net.send(r.out_y.at[pl.ds(0, 64)], r.in_y.at[pl.ds(0, 64)], w.yn)

    def second(self):
        w, r = self.w, self.r
        self.fy.wait_recv()
        r.out_x[0:64] = (
            r.keep[1, 0:64] + r.core_in[1, 0:64].astype(F32) + r.via_y[...].astype(F32)
        ).astype(BF16)
        self.x0 = self.net.send(r.out_x.at[pl.ds(0, 64)], r.in_x.at[pl.ds(0, 64)], w.xn)
        self.fx.wait_recv()
        r.out_y[64:128] = (
            r.keep[2, 64:128] + r.core_in[2, 64:128].astype(F32) + r.via_x[...].astype(F32)
        ).astype(BF16)
        self.y1 = self.net.send(r.out_y.at[pl.ds(64, 64)], r.in_y.at[pl.ds(64, 64)], w.yn)

    def total(self):
        r = self.r
        self.cores[OWN].wait_recv()
        for copy in (self.x1, self.y0, self.x0, self.y1):
            copy.wait_recv()
        return (
            r.keep[0] + r.core_in[0].astype(F32) + r.in_x[...].astype(F32) + r.in_y[...].astype(F32)
        )


def reduce_scratch(width):
    return dict(
        core_out=VMEM((4, 128, width), BF16),
        core_in=VMEM((4, 128, width), BF16),
        keep=VMEM((4, 128, width), F32),
        far=VMEM((128, width), BF16),
        via_x=VMEM((64, width), BF16),
        via_y=VMEM((64, width), BF16),
        out_x=VMEM((128, width), BF16),
        out_y=VMEM((128, width), BF16),
        in_x=VMEM((128, width), BF16),
        in_y=VMEM((128, width), BF16),
    )


def run(body, ins, outs, scratch, number, flops=0):
    names = [*ins, *outs, *scratch]

    def kernel(*refs):
        r = types.SimpleNamespace(**dict(zip(names, refs)))
        net = Net(*refs[len(names) :])
        body(net, place(), r)
        net.finish()

    results = pl.pallas_call(
        kernel,
        out_shape=[jax.ShapeDtypeStruct(shape, dtype) for shape, dtype, _ in outs.values()],
        in_specs=[pl.BlockSpec(memory_space=memory) for _, memory in ins.values()],
        out_specs=[pl.BlockSpec(memory_space=memory) for _, _, memory in outs.values()],
        scratch_shapes=[
            *scratch.values(),
            pltpu.SemaphoreType.DMA((80,)),
            pltpu.SemaphoreType.DMA((80,)),
            pltpu.SemaphoreType.DMA((16,)),
        ],
        compiler_params=pltpu.CompilerParams(
            collective_id=number, has_side_effects=True, vmem_limit_bytes=VMEM_LIMIT
        ),
        cost_estimate=pl.CostEstimate(flops=flops, bytes_accessed=8 * 2**20, transcendentals=0),
    )(*[array for array, _ in ins.values()])
    return types.SimpleNamespace(**dict(zip(outs, results)))


def neighbours(w):
    return [w.xn, w.yn, w.sib, *w.zs]


def bringing(**items):
    every = dict(swap=None, qkv=None, out=None, plane=None, inner=None, ffo=None)
    return types.SimpleNamespace(**dict(every, **items))


def rows_of(group, n=256):
    return pl.ds(pl.multiple_of(group * n, n), n)


def norm_parts(resid):
    mean = jnp.mean(resid, axis=-1, keepdims=True)
    centered = resid - mean
    variance = jnp.mean(centered * centered, axis=-1, keepdims=True)
    root = lax.rsqrt(variance + EPS)
    return centered * root, root


def norm_back(grad, hat, root, gain):
    scaled = grad * gain
    return root * (
        scaled
        - jnp.mean(scaled, axis=-1, keepdims=True)
        - hat * jnp.mean(scaled * hat, axis=-1, keepdims=True)
    )


def column_sum(value):
    return jnp.sum(value, axis=0, keepdims=True)


def of_head(value, h):
    lanes = lax.broadcasted_iota(jnp.int32, value.shape, 1)
    keep = lanes < 64 if h == 0 else lanes >= 64
    return jnp.where(keep, value, jnp.zeros_like(value))


G1, S1, BO, G2, S2, B2 = range(6)


def start_kernel(sent, number):
    layers = 2
    three, ff = sent.qkv.shape[-1], sent.inner.shape[-1]
    width = sent.hidden.shape[1]

    def body(net, w, r):
        net.greet([dev for dev, _ in w.plane] + w.zs, w, swap=True)
        hidden = net.swap(w, r.hidden, r.hidden_row)
        docs = net.swap(w, r.docs, r.docs_own)
        first = net.plane_swap(w, lambda p: r.qkv.at[0, p], lambda p: r.qkv_zero.at[p])
        vec = net.z_gather(w, r.vec, lambda z: r.vec_z.at[z])
        out = net.z_gather(w, r.out, lambda z: r.out_all.at[z])
        vec()
        vec_all = net.plane_swap(w, lambda p: r.vec_z, lambda p: r.vec_all.at[p])
        first()
        copies = [
            net.send(r.qkv_zero.at[pl.ds(2 * k, 2)], r.qkv_all.at[k, w.z], device)
            for device in w.zs
            for k in range(4)
        ]
        own = [net.local(r.qkv_zero.at[pl.ds(2 * k, 2)], r.qkv_all.at[k, w.z]) for k in range(4)]
        later = [net.plane_swap(w, lambda p: r.qkv.at[1, p], lambda p: r.qkv_one.at[p])]
        for layer in range(layers):
            later.append(
                net.plane_swap(
                    w,
                    lambda p, layer=layer: r.inner.at[layer, p],
                    lambda p, layer=layer: r.inner_z.at[layer, p],
                )
            )
        docs()
        spread = net.plane_swap(w, lambda p: r.docs_own, lambda p: r.docs_all.at[p])
        hidden()
        for wait in later:
            wait()
        out()
        vec_all()
        spread()
        for copy in own:
            copy.wait()
        for copy in copies:
            copy.wait_recv()

    return run(
        body,
        dict(
            hidden=(sent.hidden, ANY),
            docs=(sent.docs, VMEM),
            vec=(sent.vec, VMEM),
            qkv=(sent.qkv, ANY),
            inner=(sent.inner, ANY),
            out=(sent.out, ANY),
        ),
        dict(
            hidden_row=((128, width), BF16, ANY),
            docs_all=((8, 8, 128), jnp.int32, ANY),
            vec_all=((8, 4, 16, 128), BF16, ANY),
            qkv_one=((8, 32, three), BF16, ANY),
            inner_z=((layers, 8, 32, ff), BF16, ANY),
            qkv_all=((4, 4, 2, 32, three), BF16, ANY),
            out_all=((4, 32, width), BF16, ANY),
        ),
        dict(
            docs_own=VMEM((8, 128), jnp.int32),
            vec_z=VMEM((4, 16, 128), BF16),
            qkv_zero=VMEM((8, 32, three), BF16),
        ),
        number,
    )


def attend_kernel(state, low, weights, out_z, docs, vec, tpb, bring, number):
    width = low.shape[1]
    scale = (width // ATTENTION_HEADS) ** (-0.5)

    def body(net, w, r):
        net.greet(neighbours(w), w)
        r.all_low[pl.ds(pl.multiple_of((w.group[OWN] * 2 + w.c) * 128, 128), 128)] = r.low[...]
        waits = []
        extra = types.SimpleNamespace()

        def after_start():
            extra.out = net.send(
                r.out_z.at[pl.ds(2 * (1 - w.y), 2)], r.out_w.at[:, w.y], w.yn
            )
            extra.own = net.local(r.out_z.at[pl.ds(2 * w.y, 2)], r.out_w.at[:, w.y])
            waits.append(
                net.z_gather(w, r.b_inner, lambda z: r.inner_all.at[:, z])
            )
            waits.append(net.z_gather(w, r.b_ffo, lambda z: r.ffo_all.at[z]))

        bias = r.tpb[0:1, 0 : r.weights.shape[1]]

        def on_group(kind):
            rows = rows_of(w.group[kind])
            r.qkv[rows] = (dot_nn(r.all_low[rows], r.weights[...]) + bias).astype(BF16)

        gather(net, w, r.all_low, on_group, after_start)
        value = r.qkv[:, 256:384]
        for h in range(2):
            r.split_v[h] = of_head(value, h)
        extra.out.wait_recv()
        extra.own.wait()

        def attend(kind):
            def block(i, carry):
                rows = pl.ds(pl.multiple_of(w.group[kind] * 256 + i * 128, 128), 128)
                query = r.qkv[rows, 0:128]
                mask = r.docs_col[rows, 0:1] == r.docs_row[0:1, :]
                total, logs = None, []
                for h in range(2):
                    raw = dot_nt(of_head(query, h), r.qkv[:, 128:256]) * scale
                    raw = jnp.where(mask, raw, NEGATIVE)
                    top = jnp.max(raw, axis=-1, keepdims=True)
                    weight = jnp.exp(raw - top)
                    mass = jnp.sum(weight, axis=-1, keepdims=True)
                    probs = (weight * (1.0 / mass)).astype(BF16)
                    piece = dot_nn(probs, r.split_v[h])
                    total = piece if total is None else total + piece
                    logs.append(top + jnp.log(mass))
                r.context[rows] = total.astype(BF16)
                lanes = lax.broadcasted_iota(jnp.int32, (128, 128), 1)
                r.logs[rows] = jnp.where(lanes < 64, logs[0], logs[1])
                return carry

            lax.fori_loop(0, 2, block, 0)

        out_w = r.out_w

        def part(slot):
            return dot_nn(r.context[rows_of(slot, 128)], out_w[...].reshape(128, width))

        reduce = Reduce(net, w, r, part)
        for kind in (DIAG, XN):
            attend(kind)
            reduce.produce(kind)
        reduce.diag()
        attend(YN)
        reduce.produce(YN)
        reduce.first()
        attend(OWN)
        reduce.produce(OWN)
        reduce.second()
        before = r.low[...].astype(F32) if state is None else r.state[...]
        hat, root = norm_parts(before + reduce.total() + r.vec[BO : BO + 1])
        normed = hat * r.vec[G1 : G1 + 1] + r.vec[S1 : S1 + 1]
        r.normed[...] = normed
        r.normed_low[...] = normed.astype(BF16)
        r.hat[...] = hat
        r.root[...] = jnp.broadcast_to(root, (128, 128))
        for wait in waits:
            wait()

    ff = bring.inner.shape[-1]
    ins = dict(
        low=(low, VMEM),
        weights=(weights, VMEM),
        out_z=(out_z, VMEM),
        docs_row=(docs[0], VMEM),
        docs_col=(docs[1], VMEM),
        vec=(vec, VMEM),
        tpb=(tpb, VMEM),
        b_inner=(bring.inner, ANY),
        b_ffo=(bring.ffo, ANY),
    )
    if state is not None:
        ins.update(state=(state, VMEM))
    return run(
        body,
        ins,
        dict(
            all_low=((1024, width), BF16, VMEM),
            qkv=((1024, 384), BF16, VMEM),
            context=((1024, 128), BF16, VMEM),
            logs=((1024, 128), F32, VMEM),
            out_w=((2, 2, 32, width), BF16, VMEM),
            normed=((128, width), F32, VMEM),
            normed_low=((128, width), BF16, VMEM),
            hat=((128, width), F32, VMEM),
            root=((128, 128), F32, VMEM),
            inner_all=((4, 4, 64, ff), BF16, ANY),
            ffo_all=((4, 128, width), BF16, ANY),
        ),
        dict(split_v=VMEM((2, 1024, 128), BF16), **reduce_scratch(width)),
        number,
    )


def feed_kernel(normed, low, w_in, w_ffo, vec, tpb, bring, number):
    width, ff = low.shape[1], w_in.shape[1]

    def body(net, w, r):
        net.greet(neighbours(w), w, swap=bring.swap is not None)
        r.all_low[pl.ds(pl.multiple_of((w.group[OWN] * 2 + w.c) * 128, 128), 128)] = r.low[...]
        waits = []

        def after_start():
            if bring.swap is not None:
                waits.append(net.swap(w, r.b_swap, r.swapped))
            if bring.qkv is not None:
                waits.append(net.z_gather(w, r.b_out, lambda z: r.out_all.at[z]))
                waits.append(net.z_gather(w, r.b_qkv, lambda z: r.qkv_all.at[:, z]))

        bias = r.tpb[1:2, 0:ff]

        def part(slot):
            return dot_nn(r.inner[rows_of(slot, 128)], r.w_ffo[...])

        reduce = Reduce(net, w, r, part)

        def on_group(kind):
            r.pre[...] = dot_nn(r.all_low[rows_of(w.group[kind])], r.w_in[...]) + bias

            def block(i, carry):
                here = pl.ds(pl.multiple_of(i * 32, 32), 32)
                there = pl.ds(pl.multiple_of(w.group[kind] * 256 + i * 32, 32), 32)
                pre = r.pre[here]
                cdf = 0.5 * (1.0 + lax.erf(pre * (0.5**0.5)))
                r.inner[there] = (pre * cdf).astype(BF16)
                bell = jnp.exp(pre * pre * (-0.5)) * ((2.0 * math.pi) ** (-0.5))
                r.slope[there] = cdf + pre * bell
                return carry

            lax.fori_loop(0, 8, block, 0)
            reduce.produce(kind)
            if kind == YN:
                reduce.first()

        gather(net, w, r.all_low, on_group, after_start)
        reduce.diag()
        reduce.second()
        hat, root = norm_parts(r.normed[...] + reduce.total() + r.vec[B2 : B2 + 1])
        state = hat * r.vec[G2 : G2 + 1] + r.vec[S2 : S2 + 1]
        r.state[...] = state
        r.state_low[...] = state.astype(BF16)
        r.hat[...] = hat
        r.root[...] = jnp.broadcast_to(root, (128, 128))
        for wait in waits:
            wait()

    ins = dict(
        normed=(normed, VMEM),
        low=(low, VMEM),
        w_in=(w_in, VMEM),
        w_ffo=(w_ffo, VMEM),
        vec=(vec, VMEM),
        tpb=(tpb, VMEM),
    )
    outs = dict(
        all_low=((1024, width), BF16, VMEM),
        inner=((1024, ff), BF16, VMEM),
        slope=((1024, ff), F32, VMEM),
        state=((128, width), F32, VMEM),
        state_low=((128, width), BF16, VMEM),
        hat=((128, width), F32, VMEM),
        root=((128, 128), F32, VMEM),
    )
    if bring.swap is not None:
        ins.update(b_swap=(bring.swap, ANY))
        outs.update(swapped=((128, width), BF16, ANY))
    if bring.qkv is not None:
        ins.update(b_out=(bring.out, ANY))
        ins.update(b_qkv=(bring.qkv, ANY))
        outs.update(out_all=((4, 32, width), BF16, ANY))
        outs.update(qkv_all=((4, 4, 64, bring.qkv.shape[-1]), BF16, ANY))
    return run(body, ins, outs, dict(pre=VMEM((256, ff), F32), **reduce_scratch(width)), number)


def feed_back_kernel(grad, saved, hat_one, root_one, w_in, w_ffo, vec, bring, number):
    width, ff = hat_one.shape[1], w_in.shape[1]

    def body(net, w, r):
        plane = bring.plane is not None
        net.greet(
            [dev for dev, _ in w.plane] + w.zs if plane else neighbours(w), w, swap=bring.swap is not None
        )
        grad = r.grad[...].astype(F32)
        hat = r.hat_two[...]
        back_two = norm_back(grad, hat, r.root_two[:, 0:1], r.vec[G2 : G2 + 1])
        second = back_two.astype(BF16)
        r.back_two[...] = back_two
        r.all_back[pl.ds(pl.multiple_of((w.group[OWN] * 2 + w.c) * 128, 128), 128)] = second
        r.sums[...] = jnp.zeros_like(r.sums)
        r.sums[G2 : G2 + 1, :] = column_sum(grad * hat)
        r.sums[S2 : S2 + 1, :] = column_sum(grad)
        r.sums[B2 : B2 + 1, :] = column_sum(second.astype(F32))
        waits = []

        def after_start():
            if bring.swap is not None:
                waits.append(net.swap(w, r.b_swap, r.swapped))
            if bring.qkv is not None:
                waits.append(net.z_scatter(w, lambda z: r.b_out.at[z], r.land_out))
                waits.append(net.z_scatter(w, lambda z: r.b_qkv.at[:, z], r.land_qkv))
            if plane:
                waits.append(
                    net.plane_swap(w, lambda p: r.b_plane.at[p], lambda p: r.plane_all.at[p])
                )

        def part(slot):
            return dot_nt(r.back_pre[rows_of(slot, 128)], r.w_in[...])

        reduce = Reduce(net, w, r, part)

        def on_group(kind):
            rows = rows_of(w.group[kind])
            back_inner = dot_nt(r.all_back[rows], r.w_ffo[...])
            r.back_pre[rows] = (back_inner * r.slope[rows]).astype(BF16)
            reduce.produce(kind)
            if kind == YN:
                reduce.first()

        gather(net, w, r.all_back, on_group, after_start)
        reduce.diag()

        def ffo_block(i, carry):
            lanes = pl.ds(pl.multiple_of(i * 128, 128), 128)
            r.g_ffo[lanes] = dot_tn(r.inner[:, lanes], r.all_back[...]).astype(BF16)
            return carry

        lax.fori_loop(0, ff // 128, ffo_block, 0)
        reduce.second()

        def in_block(i, carry):
            lanes = pl.ds(pl.multiple_of(i * 128, 128), 128)
            r.g_in[lanes] = dot_tn(r.all_low[:, lanes], r.back_pre[...]).astype(BF16)
            return carry

        lax.fori_loop(0, width // 128, in_block, 0)
        r.sums[6:7, 256 : 256 + ff] = column_sum(r.back_pre[...].astype(F32))
        grad_one = r.back_two[...] + reduce.total()
        hat = r.hat_one[...]
        back_one = norm_back(grad_one, hat, r.root_one[:, 0:1], r.vec[G1 : G1 + 1])
        branch = back_one.astype(BF16)
        r.back_one[...] = back_one
        r.branch[...] = branch
        r.sums[G1 : G1 + 1, :] = column_sum(grad_one * hat)
        r.sums[S1 : S1 + 1, :] = column_sum(grad_one)
        r.sums[BO : BO + 1, :] = column_sum(branch.astype(F32))
        for wait in waits:
            wait()
        if bring.qkv is not None:
            r.red_out[...] = sum(r.land_out[k].astype(F32) for k in range(4))
            r.red_qkv[...] = sum(r.land_qkv[k].astype(F32) for k in range(4)).astype(BF16)

    ins = dict(
        grad=(grad, VMEM),
        hat_two=(saved.hat, VMEM),
        root_two=(saved.root, VMEM),
        all_low=(saved.all_low, VMEM),
        inner=(saved.inner, VMEM),
        slope=(saved.slope, VMEM),
        hat_one=(hat_one, VMEM),
        root_one=(root_one, VMEM),
        w_in=(w_in, VMEM),
        w_ffo=(w_ffo, VMEM),
        vec=(vec, VMEM),
    )
    outs = dict(
        g_ffo=((ff, width), BF16, VMEM),
        g_in=((width, ff), BF16, VMEM),
        back_one=((128, width), F32, VMEM),
        branch=((128, width), BF16, VMEM),
        sums=((8, width), F32, VMEM),
    )
    scratch = dict(
        all_back=VMEM((1024, width), BF16),
        back_two=VMEM((128, width), F32),
        back_pre=VMEM((1024, ff), BF16),
        **reduce_scratch(width),
    )
    if bring.swap is not None:
        ins.update(b_swap=(bring.swap, ANY))
        outs.update(swapped=((128, width), BF16, ANY))
    if bring.qkv is not None:
        ins.update(b_out=(bring.out, ANY))
        ins.update(b_qkv=(bring.qkv, ANY))
        outs.update(red_out=((32, width), F32, VMEM))
        outs.update(red_qkv=((4, 64, 384), BF16, VMEM))
        scratch.update(land_out=VMEM((4, 32, width), BF16))
        scratch.update(land_qkv=VMEM((4, 4, 64, 384), BF16))
    if bring.plane is not None:
        ins.update(b_plane=(bring.plane, ANY))
        outs.update(plane_all=(bring.plane.shape, BF16, ANY))
    return run(body, ins, outs, scratch, number)


def attend_back_kernel(back_one, branch, saved, weights, docs, bring, number):
    width = branch.shape[1]
    ff = bring.inner.shape[-1]
    scale = (width // ATTENTION_HEADS) ** (-0.5)

    def body(net, w, r):
        plane = bring.plane is not None
        net.greet([dev for dev, _ in w.plane] + w.zs if plane else neighbours(w), w)
        r.all_back[pl.ds(pl.multiple_of((w.group[OWN] * 2 + w.c) * 128, 128), 128)] = r.branch[...]
        r.sum_k[...] = jnp.zeros_like(r.sum_k)
        r.sum_v[...] = jnp.zeros_like(r.sum_v)
        key = r.qkv[:, 128:256]
        for h in range(2):
            r.split_k[h] = of_head(key, h)
        waits = []

        def after_start():
            waits.append(net.z_scatter(w, lambda z: r.b_ffo.at[z], r.land_ffo))
            waits.append(net.z_scatter(w, lambda z: r.b_inner.at[:, z], r.land_in))
            if plane:
                waits.append(
                    net.plane_swap(w, lambda p: r.b_plane.at[p], lambda p: r.plane_all.at[p])
                )

        def on_group(kind):
            rows = rows_of(w.group[kind])
            r.back_context[rows] = dot_nt(r.all_back[rows], r.out_w[...].reshape(128, width)).astype(BF16)

            def block(i, carry):
                here = pl.ds(pl.multiple_of(w.group[kind] * 256 + i * 128, 128), 128)
                query = r.qkv[here, 0:128]
                upstream = r.back_context[here]
                mask = r.docs_col[here, 0:1] == r.docs_row[0:1, :]
                total = None
                for h in range(2):
                    query_h, upstream_h = of_head(query, h), of_head(upstream, h)
                    raw = dot_nt(query_h, r.qkv[:, 128:256]) * scale
                    raw = jnp.where(mask, raw, NEGATIVE)
                    probs = jnp.exp(raw - r.logs[here, h * 64 : h * 64 + 1])
                    back = dot_nt(upstream_h, r.qkv[:, 256:384])
                    delta = jnp.sum(probs * back, axis=-1, keepdims=True)
                    scores = (probs * (back - delta)).astype(BF16)
                    piece = dot_nn(scores, r.split_k[h])
                    total = piece if total is None else total + piece
                    r.sum_k[...] += dot_tn(scores, query_h)
                    r.sum_v[...] += dot_tn(probs.astype(BF16), upstream_h)
                r.back_qkv[here, 0:128] = (total * scale).astype(BF16)
                return carry

            lax.fori_loop(0, 2, block, 0)

        gather(net, w, r.all_back, on_group, after_start)
        r.back_qkv[:, 128:256] = (r.sum_k[...] * scale).astype(BF16)
        r.back_qkv[:, 256:384] = r.sum_v[...].astype(BF16)

        def part(slot):
            return dot_nt(r.back_qkv[rows_of(slot, 128)], r.weights[...])

        reduce = Reduce(net, w, r, part)
        reduce.produce(DIAG)
        reduce.produce(XN)
        reduce.diag()
        reduce.produce(YN)
        reduce.first()
        reduce.produce(OWN)
        r.g_out[...] = dot_tn(r.context[...], r.all_back[...]).astype(BF16).reshape(2, 2, 32, width)
        cross_y = net.send(r.g_out.at[:, 1 - w.y], r.g_out_z.at[pl.ds(2 * w.y, 2)], w.yn)
        kept = net.local(r.g_out.at[:, w.y], r.g_out_z.at[pl.ds(2 * w.y, 2)])
        reduce.second()

        def qkv_block(i, carry):
            lanes = pl.ds(pl.multiple_of(i * 128, 128), 128)
            r.g_qkv[lanes] = dot_tn(r.all_low[:, lanes], r.back_qkv[...]).astype(BF16)
            return carry

        lax.fori_loop(0, width // 128, qkv_block, 0)
        r.sums[...] = jnp.zeros_like(r.sums)
        r.sums[0:1, 0:384] = column_sum(r.back_qkv[...].astype(F32))
        r.grad[...] = r.back_one[...] + reduce.total()
        for wait in waits:
            wait()
        kept.wait()
        cross_y.wait_recv()
        r.red_ffo[...] = sum(r.land_ffo[k].astype(F32) for k in range(4))
        r.red_in[...] = sum(r.land_in[k].astype(F32) for k in range(4)).astype(BF16)

    ins = dict(
        back_one=(back_one, VMEM),
        branch=(branch, VMEM),
        qkv=(saved.qkv, VMEM),
        context=(saved.context, VMEM),
        logs=(saved.logs, VMEM),
        all_low=(saved.all_low, VMEM),
        out_w=(saved.out_w, VMEM),
        weights=(weights, VMEM),
        docs_row=(docs[0], VMEM),
        docs_col=(docs[1], VMEM),
        b_ffo=(bring.ffo, ANY),
        b_inner=(bring.inner, ANY),
    )
    outs = dict(
        grad=((128, width), F32, VMEM),
        g_qkv=((width, 384), BF16, VMEM),
        g_out_z=((4, 32, width), BF16, VMEM),
        sums=((8, 384), F32, VMEM),
        red_ffo=((128, width), F32, VMEM),
        red_in=((4, 64, ff), BF16, VMEM),
    )
    scratch = dict(
        all_back=VMEM((1024, width), BF16),
        sum_k=VMEM((1024, 128), F32),
        sum_v=VMEM((1024, 128), F32),
        split_k=VMEM((2, 1024, 128), BF16),
        back_context=VMEM((1024, 128), BF16),
        back_qkv=VMEM((1024, 384), BF16),
        g_out=VMEM((2, 2, 32, width), BF16),
        land_ffo=VMEM((4, 128, width), BF16),
        land_in=VMEM((4, 4, 64, ff), BF16),
        **reduce_scratch(width),
    )
    if bring.plane is not None:
        ins.update(b_plane=(bring.plane, ANY))
        outs.update(plane_all=(bring.plane.shape, BF16, ANY))
    return run(body, ins, outs, scratch, number)


def end_kernel(grad_low, g_qkv, g_out, red_in, vecs, number):
    width, ff = grad_low.shape[1], red_in.shape[-1]

    def body(net, w, r):
        net.greet([dev for dev, _ in w.plane] + w.zs, w, swap=True)
        qkv = net.z_scatter(w, lambda z: r.qkv.at[:, z], r.land_qkv)
        out = net.z_scatter(w, lambda z: r.out.at[z], r.land_out)
        vec = net.z_scatter(w, lambda z: r.vecs, r.land_vec)
        grad = net.swap(w, r.grad_low, r.grad)
        inner = net.plane_swap(w, lambda p: r.inner.at[p], lambda p: r.g_in.at[p])
        vec()
        r.vec_z[...] = r.land_vec[0] + r.land_vec[1] + r.land_vec[2] + r.land_vec[3]
        spread = net.plane_swap(w, lambda p: r.vec_z, lambda p: r.vec_all.at[p])
        qkv()
        r.qkv_z[...] = sum(r.land_qkv[k].astype(F32) for k in range(4)).astype(BF16).reshape(8, 32, 384)
        last = net.plane_swap(w, lambda p: r.qkv_z.at[p], lambda p: r.g_qkv.at[p])
        out()
        r.g_out[...] = sum(r.land_out[k].astype(F32) for k in range(4))
        spread()
        r.vec_sum[...] = sum(r.vec_all[p] for p in range(8))
        for p in range(8):
            r.vec_part[p] = r.vec_all[p, 16:24]
        inner()
        last()
        grad()

    return run(
        body,
        dict(
            grad_low=(grad_low, ANY),
            qkv=(g_qkv, ANY),
            out=(g_out, ANY),
            inner=(red_in, ANY),
            vecs=(vecs, VMEM),
        ),
        dict(
            grad=((128, width), BF16, ANY),
            g_qkv=((8, 32, 384), BF16, ANY),
            g_in=((8, 32, ff), BF16, ANY),
            g_out=((32, width), F32, VMEM),
            vec_sum=((24, width), F32, VMEM),
            vec_part=((8, 8, width), F32, VMEM),
        ),
        dict(
            land_qkv=VMEM((4, 4, 64, 384), BF16),
            land_out=VMEM((4, 32, width), BF16),
            land_vec=VMEM((4, 24, width), F32),
            vec_z=VMEM((24, width), F32),
            vec_all=VMEM((8, 24, width), F32),
            qkv_z=VMEM((8, 32, 384), BF16),
        ),
        number,
    )


def plane_body(
    hidden_in,
    document_index,
    out_grad,
    qkv_weight,
    value_bias,
    attention_output_weight,
    ffn_in_weight,
    ffn_out_weight,
    biases,
    norm_gains,
):
    layers = qkv_weight.shape[0]
    width = hidden_in.shape[1]
    inner = ffn_in_weight.shape[2]
    share = inner // 8
    d, t = lax.axis_index(DP), lax.axis_index(CTX)
    y = lax.rem(t, 2)
    part = d * 2 + y
    packed = jnp.concatenate([biases, norm_gains, value_bias], axis=1).reshape(-1)
    per_owner = packed.shape[0] // layers
    n_bias, n_gain = biases.shape[1], norm_gains.shape[1]
    sent = types.SimpleNamespace(
        hidden=hidden_in,
        docs=jnp.broadcast_to(document_index, (8, 128)),
        vec=jnp.pad(packed, (0, 2048 - packed.shape[0])).reshape(16, 128),
        qkv=qkv_weight.reshape(layers, 32, 3, 8, width // 8)
        .transpose(0, 3, 1, 2, 4)
        .reshape(layers, 8, 32, 3 * width // 8),
        inner=ffn_in_weight.reshape(layers, 32, 4, 4, 2, share // 4)
        .transpose(0, 2, 4, 1, 3, 5)
        .reshape(layers, 8, 32, share),
        out=attention_output_weight[0],
    )
    got = start_kernel(sent, 0)
    docs = got.docs_all[:, 0].reshape(2, 2, 2, 128).transpose(0, 2, 1, 3).reshape(1024)
    docs = (jnp.broadcast_to(docs[None], (8, 1024)), jnp.broadcast_to(docs[:, None], (1024, 128)))
    vec = (
        got.vec_all.reshape(4, 2, 4, 2048)
        .transpose(0, 2, 1, 3)
        .reshape(32, 2048)[:, : layers * per_owner]
        .astype(F32)
    )
    owned = vec.reshape(32, layers, per_owner)
    bias = owned[:, :, :n_bias].transpose(1, 0, 2).reshape(layers, -1)
    gain = owned[:, :, n_bias : n_bias + n_gain].transpose(1, 0, 2).reshape(layers, -1)
    v_bias = owned[:, :, n_bias + n_gain :].transpose(1, 0, 2).reshape(layers, -1)
    vecs, tpbs = [], []
    for layer in range(layers):
        row = bias[layer]
        after = 2 * width + inner
        vecs.append(
            jnp.stack(
                [
                    gain[layer, :width],
                    row[after + width : after + 2 * width],
                    row[width : 2 * width],
                    gain[layer, width:],
                    row[after + 2 * width : after + 3 * width],
                    row[after : after + width],
                    jnp.zeros((width,), F32),
                    jnp.zeros((width,), F32),
                ]
            )
        )
        head = lax.dynamic_slice_in_dim(row, part * 128, 128)
        head_v = lax.dynamic_slice_in_dim(v_bias[layer], part * 128, 128)
        units = lax.dynamic_index_in_dim(
            row[2 * width : after].reshape(4, 4, 2, share // 4).transpose(0, 2, 1, 3).reshape(8, share),
            part,
            0,
            keepdims=False,
        )
        first = jnp.concatenate([head, jnp.zeros((128,), F32), head_v, jnp.zeros((width - 384,), F32)])
        tpbs.append(
            jnp.concatenate(
                [first[None], jnp.pad(units, (0, width - share))[None], jnp.zeros((6, width), F32)]
            )
        )
    state, low = None, got.hidden_row
    w_qkv, out_z = got.qkv_all.reshape(width, 384), got.out_all
    kept, number = [], 1
    for layer in range(layers):
        bring = bringing(
            inner=got.inner_z[layer].reshape(4, 64, share),
            ffo=ffn_out_weight[layer],
        )
        att = attend_kernel(state, low, w_qkv, out_z, docs, vecs[layer], tpbs[layer], bring, number)
        w_in, w_ffo = att.inner_all.reshape(width, share), att.ffo_all.reshape(share, width)
        if layer + 1 < layers:
            bring = bringing(
                qkv=got.qkv_one.reshape(4, 64, 384),
                out=attention_output_weight[layer + 1],
            )
        else:
            bring = bringing(swap=out_grad)
        feed = feed_kernel(
            att.normed, att.normed_low, w_in, w_ffo, vecs[layer], tpbs[layer], bring, number + 1
        )
        number += 2
        kept.append((att, feed, w_qkv, w_in, w_ffo))
        state, low = feed.state, feed.state_low
        if layer + 1 < layers:
            w_qkv, out_z = feed.qkv_all.reshape(width, 384), feed.out_all
    grad = feed.swapped
    qkv_done, in_done = [None] * layers, [None] * layers
    out_done, ffo_done = [None] * layers, [None] * layers
    sums = []
    bring = bringing(swap=low)
    red_qkv = None
    for layer in reversed(range(layers)):
        att, feed, w_qkv, w_in, w_ffo = kept[layer]
        back = feed_back_kernel(grad, feed, att.hat, att.root, w_in, w_ffo, vecs[layer], bring, number)
        if layer + 1 == layers:
            out = back.swapped
        else:
            out_done[layer + 1] = back.red_out
            in_done[layer + 1] = back.plane_all
            red_qkv = back.red_qkv
        bring = bringing(
            ffo=back.g_ffo.reshape(4, 128, width),
            inner=back.g_in.reshape(4, 4, 64, share),
        )
        if red_qkv is not None:
            bring.plane = red_qkv.reshape(8, 32, 384)
        turn = attend_back_kernel(back.back_one, back.branch, att, w_qkv, docs, bring, number + 1)
        number += 2
        if red_qkv is not None:
            qkv_done[layer + 1] = turn.plane_all
        ffo_done[layer] = turn.red_ffo
        sums.append((back.sums, turn.sums))
        grad = turn.grad
        red_in = turn.red_in.reshape(8, 32, share)
        bring = bringing(qkv=turn.g_qkv.reshape(4, 4, 64, 384), out=turn.g_out_z, plane=red_in)
    packed = [back.at[6, 0:128].set(turn[0, 0:128]).at[6, 128:256].set(turn[0, 256:384]) for back, turn in sums]
    packed = jnp.concatenate(
        [packed[1][0:6], jnp.zeros((2, width), F32), packed[0][0:6], jnp.zeros((2, width), F32)]
        + [packed[1][6:7], packed[0][6:7], jnp.zeros((6, width), F32)]
    )
    end = end_kernel(
        grad.astype(BF16), turn.g_qkv.reshape(4, 4, 64, 384), turn.g_out_z, red_in, packed, number
    )
    out_done[0], in_done[0], qkv_done[0] = end.g_out, end.g_in, end.g_qkv
    index = d * 8 + t
    bias_all, gain_all, value_all = [], [], []
    for layer in range(layers):
        rows = end.vec_sum[8 * layer : 8 * layer + 8]
        parts = end.vec_part[:, layer]
        bias_all.append(
            jnp.concatenate(
                [
                    parts[:, 0:128].reshape(-1),
                    rows[BO],
                    parts[:, 256 : 256 + share].reshape(4, 2, 4, share // 4).transpose(0, 2, 1, 3).reshape(-1),
                    rows[B2],
                    rows[S1],
                    rows[S2],
                ]
            )
        )
        gain_all.append(jnp.concatenate([rows[G1], rows[G2]]))
        value_all.append(parts[:, 128:256].reshape(-1))

    def own(items, size):
        return lax.dynamic_slice_in_dim(jnp.stack(items), index * size, size, 1)

    return (
        out,
        end.grad.astype(F32),
        jnp.stack(
            [
                item.reshape(8, 32, 3, 128).transpose(1, 2, 0, 3).reshape(32, 3 * width).astype(F32)
                for item in qkv_done
            ]
        ),
        own(value_all, width // 32),
        jnp.stack(out_done),
        jnp.stack(
            [
                item.reshape(4, 2, 32, 4, share // 4).transpose(2, 0, 3, 1, 4).reshape(32, inner).astype(F32)
                for item in in_done
            ]
        ),
        jnp.stack(ffo_done),
        own(bias_all, n_bias),
        own(gain_all, n_gain),
    )


def fits_plane(mesh):
    return mesh.shape[DP] == 4 and mesh.shape[CTX] == 8


def solution(mesh):
    return jax.shard_map(
        plane_body if fits_plane(mesh) else body,
        mesh=mesh,
        in_specs=(
            P(BOTH, None),
            P(DP, CTX),
            P(BOTH, None),
            P(None, BOTH, None),
            P(None, BOTH),
            P(None, BOTH, None),
            P(None, BOTH, None),
            P(None, BOTH, None),
            P(None, BOTH),
            P(None, BOTH),
        ),
        out_specs=(
            P(BOTH, None),
            P(BOTH, None),
            P(None, BOTH, None),
            P(None, BOTH),
            P(None, BOTH, None),
            P(None, BOTH, None),
            P(None, BOTH, None),
            P(None, BOTH),
            P(None, BOTH),
        ),
        check_vma=False,
    )
```

```python
import math
import types

import jax
import jax.numpy as jnp
from jax import lax
from jax.experimental import pallas as pl
from jax.experimental.pallas import tpu as pltpu
from jax.sharding import PartitionSpec as P

ATTENTION_HEADS = 16


DP, CTX = "dp", "ctx"
BOTH = (DP, CTX)

QUERY_KEY, TO_QUERY, TO_KEY = "qhd,khd->hqk", "hqk,khd->qhd", "hqk,qhd->khd"
EPS = 1e-12
NEGATIVE = -1e30


def norm_rows(resid, gain, shift):
    mean = jnp.mean(resid, axis=-1, keepdims=True)
    centered = resid - mean
    variance = jnp.mean(centered * centered, axis=-1, keepdims=True)
    return centered * lax.rsqrt(variance + EPS) * gain + shift


def exact_gelu(value):
    return jax.nn.gelu(value, approximate=False)


def cross(left, right_operand):
    return lax.dot_general(
        left, right_operand, (((0,), (0,)), ((), ())), preferred_element_type=jnp.float32
    )


def back_product(upstream, weight):
    return lax.dot_general(
        upstream, weight, (((1,), (1,)), ((), ())), preferred_element_type=jnp.float32
    )


def by_blocks(step_fn, carry, pieces, token_block):
    count = pieces[0].shape[0]

    def turn(index, state):
        offset = index * token_block
        parts = tuple((lax.dynamic_slice_in_dim(item, offset, token_block, 0) for item in pieces))
        return step_fn(state, parts, offset)

    return lax.fori_loop(0, count // token_block, turn, carry)


def unpack(fetched, width, inner):
    w_qkv, w_out, w_in, w_ffo, value_vec, bias_all, gains = fetched
    value_vec = value_vec.astype(jnp.float32)
    bias_all = bias_all.astype(jnp.float32)
    gains = gains.astype(jnp.float32)
    query_bias = bias_all[0:width]
    out_bias = bias_all[width : 2 * width]
    inner_bias = bias_all[2 * width : 2 * width + inner]
    ffn_bias = bias_all[2 * width + inner : 3 * width + inner]
    shift_one = bias_all[3 * width + inner : 4 * width + inner]
    shift_two = bias_all[4 * width + inner : 5 * width + inner]
    return (
        w_qkv,
        w_out,
        w_in,
        w_ffo,
        value_vec,
        query_bias,
        out_bias,
        inner_bias,
        ffn_bias,
        shift_one,
        shift_two,
        gains[0:width],
        gains[width : 2 * width],
    )


def masked_scores(query_heads, key_piece, seg_own, segment_row, start, scale):
    count = key_piece.shape[0]
    heads = query_heads.shape[1]
    split_key_heads = key_piece.reshape(count, heads, query_heads.shape[2])
    seg_keys = lax.dynamic_slice_in_dim(segment_row, start, count, 0)
    mask = (seg_own[:, None] == seg_keys[None, :])[None]
    raw = (
        jnp.einsum(QUERY_KEY, query_heads, split_key_heads, preferred_element_type=jnp.float32)
        * scale
    )
    return (jnp.where(mask, raw, NEGATIVE), mask, split_key_heads)


def body(
    hidden_in,
    document_index,
    out_grad,
    qkv_weight,
    value_bias,
    attention_output_weight,
    ffn_in_weight,
    ffn_out_weight,
    biases,
    norm_gains,
):
    layers = qkv_weight.shape[0]
    width = qkv_weight.shape[2] // 3
    inner = ffn_in_weight.shape[2]
    heads = ATTENTION_HEADS
    head_width = width // heads
    scale = head_width ** (-0.5)
    rows = hidden_in.shape[0]
    seg_own = document_index[0]
    segment_row = lax.all_gather(document_index, CTX, axis=1, tiled=True)[0]
    row_len = segment_row.shape[0]
    state = hidden_in.astype(jnp.float32)
    saved = []
    for layer in range(layers):
        fetched = (
            lax.all_gather(qkv_weight[layer], BOTH, axis=0, tiled=True),
            lax.all_gather(attention_output_weight[layer], BOTH, axis=0, tiled=True),
            lax.all_gather(ffn_in_weight[layer], BOTH, axis=0, tiled=True),
            lax.all_gather(ffn_out_weight[layer], BOTH, axis=0, tiled=True),
            lax.all_gather(value_bias[layer], BOTH, axis=0, tiled=True),
            lax.all_gather(biases[layer], BOTH, axis=0, tiled=True),
            lax.all_gather(norm_gains[layer], BOTH, axis=0, tiled=True),
        )
        (
            w_qkv,
            w_out,
            w_in,
            w_ffo,
            value_vec,
            query_bias,
            out_bias,
            inner_bias,
            ffn_bias,
            shift_one,
            shift_two,
            gain_one,
            gain_two,
        ) = unpack(fetched, width, inner)
        state_low = state.astype(jnp.bfloat16)
        qkv_bias = jnp.concatenate([query_bias, jnp.zeros_like(query_bias), value_vec])
        qkv_low = (jnp.dot(state_low, w_qkv, preferred_element_type=jnp.float32) + qkv_bias).astype(
            jnp.bfloat16
        )
        query_heads = qkv_low[:, 0:width].reshape(rows, heads, head_width)
        key_low = qkv_low[:, width : 2 * width]
        value_low = qkv_low[:, 2 * width : 3 * width]

        def stats_step(carry, parts, start):
            top, total = carry
            raw, mask, split_key_heads = masked_scores(
                query_heads, parts[0], seg_own, segment_row, start, scale
            )
            new_top = jnp.maximum(top, jnp.max(raw, axis=-1))
            weights = jnp.where(mask, jnp.exp(raw - new_top[:, :, None]), 0.0)
            return (new_top, total * jnp.exp(top - new_top) + jnp.sum(weights, axis=-1))

        stats_init = (
            jnp.full((heads, rows), NEGATIVE, jnp.float32),
            jnp.zeros((heads, rows), jnp.float32),
        )
        held_pair = None
        top, total = by_blocks(
            stats_step, stats_init, (lax.all_gather(key_low, CTX, axis=0, tiled=True),), rows
        )
        log_total = top + jnp.log(total)

        def value_step(carry, parts, start):
            context_acc, exact_acc = carry
            raw, mask, split_key_heads = masked_scores(
                query_heads, parts[0], seg_own, segment_row, start, scale
            )
            split_value_heads = parts[1].reshape(parts[1].shape[0], heads, head_width)
            probs = jnp.where(mask, jnp.exp(raw - log_total[:, :, None]), 0.0)
            probs_low = probs.astype(jnp.bfloat16)
            residue_low = (probs - probs_low.astype(jnp.float32)).astype(jnp.bfloat16)
            part_low = jnp.einsum(
                TO_QUERY, probs_low, split_value_heads, preferred_element_type=jnp.float32
            )
            part_fix = jnp.einsum(
                TO_QUERY, residue_low, split_value_heads, preferred_element_type=jnp.float32
            )
            return (context_acc + part_low, exact_acc + part_fix)

        value_init = (
            jnp.zeros((rows, heads, head_width), jnp.float32),
            jnp.zeros((rows, heads, head_width), jnp.float32),
        )
        context, correction = by_blocks(
            value_step,
            value_init,
            (
                lax.all_gather(key_low, CTX, axis=0, tiled=True),
                lax.all_gather(value_low, CTX, axis=0, tiled=True),
            ),
            rows,
        )
        context_exact = (context + correction).reshape(rows, width)
        context = context.reshape(rows, width)
        context_low = context.astype(jnp.bfloat16)
        resid_one = (
            state + jnp.dot(context_low, w_out, preferred_element_type=jnp.float32) + out_bias
        )
        normed = norm_rows(resid_one, gain_one, shift_one)
        normed_low = normed.astype(jnp.bfloat16)
        pre = jnp.dot(normed_low, w_in, preferred_element_type=jnp.float32) + inner_bias
        inner_low = exact_gelu(pre).astype(jnp.bfloat16)
        resid_two = (
            normed + jnp.dot(inner_low, w_ffo, preferred_element_type=jnp.float32) + ffn_bias
        )
        saved.append(
            (
                fetched,
                state_low,
                qkv_low,
                log_total,
                context_exact,
                context_low,
                resid_one,
                normed_low,
                pre,
                inner_low,
                resid_two,
                held_pair,
            )
        )
        state = norm_rows(resid_two, gain_two, shift_two)
    upstream = out_grad.astype(jnp.float32)
    per_layer = []
    for layer in reversed(range(layers)):
        (
            fetched,
            state_low,
            qkv_low,
            log_total,
            context_exact,
            context_low,
            resid_one,
            normed_low,
            pre,
            inner_low,
            resid_two,
            held_pair,
        ) = saved[layer]
        weights_now = (
            lax.all_gather(qkv_weight[layer], BOTH, axis=0, tiled=True),
            lax.all_gather(attention_output_weight[layer], BOTH, axis=0, tiled=True),
            lax.all_gather(ffn_in_weight[layer], BOTH, axis=0, tiled=True),
            lax.all_gather(ffn_out_weight[layer], BOTH, axis=0, tiled=True),
            lax.all_gather(value_bias[layer], BOTH, axis=0, tiled=True),
            lax.all_gather(biases[layer], BOTH, axis=0, tiled=True),
            lax.all_gather(norm_gains[layer], BOTH, axis=0, tiled=True),
        )
        (
            w_qkv,
            w_out,
            w_in,
            w_ffo,
            value_vec,
            query_bias,
            out_bias,
            inner_bias,
            ffn_bias,
            shift_one,
            shift_two,
            gain_one,
            gain_two,
        ) = unpack(weights_now, width, inner)
        query_low = qkv_low[:, 0:width]
        query_heads = query_low.reshape(rows, heads, head_width)
        key_low = qkv_low[:, width : 2 * width]
        value_low = qkv_low[:, 2 * width : 3 * width]
        unused_two, pull_two = jax.vjp(norm_rows, resid_two, gain_two, shift_two)
        back_two, back_gain_two, back_shift_two = pull_two(upstream)
        back_second = back_two.astype(jnp.bfloat16)
        grad_second = cross(inner_low, back_second)
        back_inner = back_product(back_second, w_ffo)
        unused_pre, pull_gelu = jax.vjp(exact_gelu, pre)
        back_pre = pull_gelu(back_inner)[0].astype(jnp.bfloat16)
        grad_first = cross(normed_low, back_pre)
        back_normed = back_two + back_product(back_pre, w_in)
        normed_again, pull_one = jax.vjp(norm_rows, resid_one, gain_one, shift_one)
        back_one, back_gain_one, back_shift_one = pull_one(back_normed)
        back_branch = back_one.astype(jnp.bfloat16)
        grad_out_proj = cross(context_low, back_branch)
        back_context = back_product(back_branch, w_out).astype(jnp.bfloat16)
        context_heads_back = back_context.reshape(rows, heads, head_width)
        delta = jnp.sum(
            (back_context.astype(jnp.float32) * context_exact).reshape(rows, heads, head_width),
            axis=-1,
        ).T

        def grad_step(carry, parts, start):
            query_sum, key_sums, value_sums = carry
            count = parts[0].shape[0]
            raw, mask, split_key_heads = masked_scores(
                query_heads, parts[0], seg_own, segment_row, start, scale
            )
            split_value_heads = parts[1].reshape(count, heads, head_width)
            probs = jnp.where(mask, jnp.exp(raw - log_total[:, :, None]), 0.0)
            back_probs = jnp.einsum(
                QUERY_KEY,
                context_heads_back,
                split_value_heads,
                preferred_element_type=jnp.float32,
            )
            back_scores = (probs * (back_probs - delta[:, :, None])).astype(jnp.bfloat16)
            query_part = (
                jnp.einsum(
                    TO_QUERY, back_scores, split_key_heads, preferred_element_type=jnp.float32
                )
                * scale
            )
            key_part = (
                jnp.einsum(
                    TO_KEY, back_scores, query_heads, preferred_element_type=jnp.float32
                ).reshape(count, width)
                * scale
            )
            value_part = jnp.einsum(
                TO_KEY,
                probs.astype(jnp.bfloat16),
                context_heads_back,
                preferred_element_type=jnp.float32,
            ).reshape(count, width)
            key_sums = lax.dynamic_update_slice_in_dim(
                key_sums, lax.dynamic_slice_in_dim(key_sums, start, count, 0) + key_part, start, 0
            )
            value_sums = lax.dynamic_update_slice_in_dim(
                value_sums,
                lax.dynamic_slice_in_dim(value_sums, start, count, 0) + value_part,
                start,
                0,
            )
            return (query_sum + query_part, key_sums, value_sums)

        query_init = jnp.zeros((rows, heads, head_width), jnp.float32)
        grad_init = (
            query_init,
            jnp.zeros((row_len, width), jnp.float32),
            jnp.zeros((row_len, width), jnp.float32),
        )
        folded = by_blocks(
            grad_step,
            grad_init,
            (
                lax.all_gather(key_low, CTX, axis=0, tiled=True),
                lax.all_gather(value_low, CTX, axis=0, tiled=True),
            ),
            rows,
        )
        query_sum, key_sums, value_sums = folded
        key_own, value_own = (
            lax.psum_scatter(
                key_sums.astype(jnp.bfloat16), CTX, scatter_dimension=0, tiled=True
            ).astype(jnp.float32),
            lax.psum_scatter(
                value_sums.astype(jnp.bfloat16), CTX, scatter_dimension=0, tiled=True
            ).astype(jnp.float32),
        )
        back_qkv = jnp.concatenate(
            [query_sum.reshape(rows, width), key_own, value_own], axis=1
        ).astype(jnp.bfloat16)
        grad_qkv = cross(state_low, back_qkv)
        back_qkv_float = back_qkv.astype(jnp.float32)
        grad_value_bias = jnp.sum(back_qkv_float[:, 2 * width : 3 * width], axis=0)
        grad_bias = jnp.concatenate(
            [
                jnp.sum(back_qkv_float[:, 0:width], axis=0),
                jnp.sum(back_branch.astype(jnp.float32), axis=0),
                jnp.sum(back_pre.astype(jnp.float32), axis=0),
                jnp.sum(back_second.astype(jnp.float32), axis=0),
                back_shift_one,
                back_shift_two,
            ]
        )
        grad_gain = jnp.concatenate([back_gain_one, back_gain_two])
        upstream = back_one + back_product(back_qkv, w_qkv)
        shards = (
            lax.psum_scatter(grad_qkv, BOTH, scatter_dimension=0, tiled=True),
            lax.psum_scatter(grad_value_bias, BOTH, scatter_dimension=0, tiled=True),
            lax.psum_scatter(grad_out_proj, BOTH, scatter_dimension=0, tiled=True),
            lax.psum_scatter(grad_first, BOTH, scatter_dimension=0, tiled=True),
            lax.psum_scatter(grad_second, BOTH, scatter_dimension=0, tiled=True),
            lax.psum_scatter(grad_bias, BOTH, scatter_dimension=0, tiled=True),
            lax.psum_scatter(grad_gain, BOTH, scatter_dimension=0, tiled=True),
        )
        per_layer.append(shards)
    ordered = per_layer[::-1]
    stacked = tuple((jnp.stack([item[member] for item in ordered]) for member in range(7)))
    return (
        state.astype(jnp.bfloat16),
        upstream,
        stacked[0],
        stacked[1],
        stacked[2],
        stacked[3],
        stacked[4],
        stacked[5],
        stacked[6],
    )


MESH = pl.DeviceIdType.MESH
F32 = jnp.float32
BF16 = jnp.bfloat16
VMEM = pltpu.VMEM
VMEM_LIMIT = 62 * 2**20
COPIES = 420
OWN, XN, YN, DIAG = range(4)
G1, S1, BO, G2, S2, B2 = range(6)


def dot_nn(a, b):
    return lax.dot_general(a, b, (((1,), (0,)), ((), ())), preferred_element_type=F32)


def dot_nt(a, b):
    return lax.dot_general(a, b, (((1,), (1,)), ((), ())), preferred_element_type=F32)


def dot_tn(a, b):
    return lax.dot_general(a, b, (((0,), (0,)), ((), ())), preferred_element_type=F32)


def turned(two_bits):
    return lax.rem(two_bits, 2) * 2 + lax.div(two_bits, 2)


def place():
    d, t = lax.axis_index(DP), lax.axis_index(CTX)
    x, c = lax.div(d, 2), lax.rem(d, 2)
    z, y = lax.div(t, 2), lax.rem(t, 2)
    w = types.SimpleNamespace(d=d, x=x, c=c, z=z, y=y)
    w.part = d * 2 + y
    w.group = (x * 2 + y, (1 - x) * 2 + y, x * 2 + 1 - y, (1 - x) * 2 + 1 - y)
    w.slot = w.group[OWN] * 2 + c
    w.xn, w.yn, w.sib = ((1 - x) * 2 + c, t), (d, z * 2 + 1 - y), (x * 2 + 1 - c, t)
    w.plane = []
    for bits in range(1, 8):
        xx = 1 - x if bits & 4 else x
        cc = 1 - c if bits & 2 else c
        yy = 1 - y if bits & 1 else y
        w.plane.append(((xx * 2 + cc, z * 2 + yy), (xx * 2 + cc) * 2 + yy))
    w.zs = [(d, lax.rem(z + k, 4) * 2 + y) for k in (1, 2, 3)]
    w.far = lax.rem(z + 2, 4)
    w.up, w.down, w.over = (d, (z + 1) * 2 + y), (d, (z - 1) * 2 + y), (d, w.far * 2 + y)
    w.middle = (z == 1) | (z == 2)
    w.edge = (z == 0) | (z == 3)
    w.end = jnp.where(z == 1, 0, 3)
    w.near_end = (d, w.end * 2 + y)
    w.inside = jnp.where(z == 0, 1, 2)
    w.near_middle = (d, w.inside * 2 + y)
    w.opposite = 3 - z
    w.away = d != turned(z)
    w.home = d == turned(z)
    w.swap = (turned(z), turned(d) * 2 + y)
    return w


class Maybe:
    def __init__(self, copy, sends, receives):
        self.copy, self.sends, self.receives = copy, sends, receives

    def start(self):
        pl.when(self.sends)(self.copy.start)

    def wait_send(self):
        pl.when(self.sends)(self.copy.wait_send)

    def wait_recv(self):
        pl.when(self.receives)(self.copy.wait_recv)


class Net:
    def __init__(self, ssem, rsem, lsem):
        self.ssem, self.rsem, self.lsem = ssem, rsem, lsem
        self.sent, self.slow, self.scatters, self.at, self.near = [], [], [], 0, 0

    def greet(self, w):
        barrier = pltpu.get_barrier_semaphore()
        devices = [device for device, _ in w.plane] + w.zs
        for device in devices:
            pl.semaphore_signal(barrier, inc=1, device_id=device, device_id_type=MESH)

        @pl.when(w.away)
        def _():
            pl.semaphore_signal(barrier, inc=1, device_id=w.swap, device_id_type=MESH)

        pl.semaphore_wait(barrier, len(devices) + jnp.where(w.away, 1, 0))

    def make(self, src, dst, device):
        copy = pltpu.make_async_remote_copy(
            src_ref=src,
            dst_ref=dst,
            send_sem=self.ssem.at[self.at],
            recv_sem=self.rsem.at[self.at],
            device_id=device,
            device_id_type=MESH,
        )
        self.at += 1
        return copy

    def maybe(self, src, dst, device, sends, receives):
        copy = Maybe(self.make(src, dst, device), sends, receives)
        self.slow.append(copy)
        return copy

    def send(self, src, dst, device, slow=False):
        copy = self.make(src, dst, device)
        copy.start()
        (self.slow if slow else self.sent).append(copy)
        return copy

    def local(self, src, dst):
        copy = pltpu.make_async_copy(src, dst, self.lsem.at[self.near])
        self.near += 1
        return copy

    def swap(self, w, src, dst):
        far = Maybe(self.make(src, dst, w.swap), w.away, w.away)
        near = self.local(src, dst)
        far.start()
        pl.when(w.home)(near.start)

        def wait():
            far.wait_recv()
            far.wait_send()
            pl.when(w.home)(near.wait)

        return wait

    def plane_swap(self, w, at, to):
        copies = [self.send(at(part), to(w.part), device, True) for device, part in w.plane]
        own = self.local(at(w.part), to(w.part))
        own.start()

        def wait():
            own.wait()
            for copy in copies:
                copy.wait_recv()

        return wait

    def z_spread(self, w, src, land):
        copies = [self.send(src, land.at[k], device, True) for k, device in enumerate(w.zs)]

        def wait():
            for copy in copies:
                copy.wait_recv()

        return wait

    def drain(self):
        for copy in self.sent:
            copy.wait_send()
        self.sent = []

    def settle(self):
        self.drain()
        for copy in self.slow:
            copy.wait_send()
        self.slow = []
        for scatter in self.scatters:
            scatter.settle()


class ZGather:
    def __init__(self, net, w, src, at):
        self.w, here = w, at(w.z)
        self.over = net.send(src, here, w.over, True)
        self.up = net.maybe(src, here, w.up, w.z < 3, w.z > 0)
        self.down = net.maybe(src, here, w.down, w.z > 0, w.z < 3)
        far = at(w.far)
        self.on = net.maybe(far, far, w.near_end, w.middle, w.edge)
        self.own = net.local(src, here)
        self.up.start()
        self.down.start()
        self.own.start()

    def poll(self):
        pl.when(self.w.middle)(self.over.wait_recv)
        self.on.start()

    def wait(self):
        pl.when(self.w.edge)(self.over.wait_recv)
        self.own.wait()
        for copy in (self.up, self.down, self.on):
            copy.wait_recv()


class ZScatter:
    def __init__(self, net, w, at, land):
        self.w, self.at, self.land = w, at, land
        self.on = net.maybe(at(w.opposite), land.at[3], w.near_middle, w.edge, w.middle)
        self.on.start()
        self.up = net.maybe(at(lax.rem(w.z + 1, 4)), land.at[0], w.up, w.z < 3, w.z > 0)
        self.down = net.maybe(at(lax.rem(w.z + 3, 4)), land.at[1], w.down, w.z > 0, w.z < 3)
        self.end_over = net.maybe(at(w.far), land.at[2], w.over, w.edge, w.middle)
        self.mid_over = net.maybe(land.at[3], land.at[2], w.over, w.middle, w.edge)
        self.sends = (self.on, self.up, self.down, self.end_over, self.mid_over)
        net.slow = [copy for copy in net.slow if copy not in self.sends]
        net.scatters.append(self)
        for copy in (self.end_over, self.up, self.down):
            copy.start()

        @pl.when(w.z == 0)
        def _():
            land[0] = jnp.zeros(land.shape[1:], BF16)

        @pl.when(w.z == 3)
        def _():
            land[1] = jnp.zeros(land.shape[1:], BF16)

    def poll(self):
        @pl.when(self.w.middle)
        def _():
            self.on.copy.wait_recv()
            own = self.at(self.w.far)[...].astype(F32)
            self.land[3] = (self.land[3].astype(F32) + own).astype(BF16)

        self.mid_over.start()

    def settle(self):
        for copy in self.sends:
            copy.wait_send()
        self.sends = ()

    def total(self):
        for copy in (self.up, self.down, self.end_over, self.mid_over):
            copy.wait_recv()
        land = self.land
        return (
            self.at(self.w.z)[...].astype(F32)
            + land[0].astype(F32)
            + land[1].astype(F32)
            + land[2].astype(F32)
        )


def gather(net, w, buf, on_group, after_start):
    def half(group, h):
        return buf.at[pl.ds(pl.multiple_of((group * 2 + w.c) * 128 + h * 64, 64), 64)]

    def put(group, h, device):
        ref = half(group, h)
        return net.send(ref, ref, device)

    own, xn, yn, diag = w.group
    x0 = put(own, 0, w.xn)
    y1 = put(own, 1, w.yn)
    whole = buf.at[rows_of(w.slot, 128)]
    c0 = net.send(whole, whole, w.sib)
    x1 = put(own, 1, w.xn)
    y0 = put(own, 0, w.yn)
    after_start()
    c0.wait_recv()
    on_group(OWN)
    x0.wait_recv()
    d0 = put(xn, 0, w.yn)
    cx0 = put(xn, 0, w.sib)
    y1.wait_recv()
    d1 = put(yn, 1, w.xn)
    cy1 = put(yn, 1, w.sib)
    x1.wait_recv()
    cx1 = put(xn, 1, w.sib)
    y0.wait_recv()
    cy0 = put(yn, 0, w.sib)
    cx0.wait_recv()
    cx1.wait_recv()
    on_group(XN)
    cy0.wait_recv()
    cy1.wait_recv()
    on_group(YN)
    d0.wait_recv()
    cd0 = put(diag, 0, w.sib)
    d1.wait_recv()
    cd1 = put(diag, 1, w.sib)
    cd0.wait_recv()
    cd1.wait_recv()
    on_group(DIAG)


class Reduce:
    def __init__(self, net, w, r, part):
        self.net, self.w, self.r, self.part = net, w, r, part
        self.cores = [None] * 4

    def produce(self, kind):
        w, r = self.w, self.r
        group = w.group[kind]
        r.core_out[kind] = self.part(group * 2 + 1 - w.c).astype(BF16)
        self.cores[kind] = self.net.send(r.core_out.at[kind], r.core_in.at[kind], w.sib)
        r.keep[kind] = self.part(group * 2 + w.c)

    def both(self, kind, rows):
        return self.r.keep[kind, rows] + self.r.core_in[kind, rows].astype(F32)

    def diag(self):
        w, r = self.w, self.r
        self.cores[DIAG].wait_recv()
        r.across[...] = self.both(DIAG, slice(0, 128)).astype(BF16)
        self.fy = self.net.send(r.across.at[pl.ds(0, 64)], r.via_y, w.yn)
        self.fx = self.net.send(r.across.at[pl.ds(64, 64)], r.via_x, w.xn)

    def first(self):
        w, r = self.w, self.r
        self.cores[XN].wait_recv()
        r.out_x[64:128] = self.both(XN, slice(64, 128)).astype(BF16)
        self.x1 = self.net.send(r.out_x.at[pl.ds(64, 64)], r.in_x.at[pl.ds(64, 64)], w.xn)
        self.cores[YN].wait_recv()
        r.out_y[0:64] = self.both(YN, slice(0, 64)).astype(BF16)
        self.y0 = self.net.send(r.out_y.at[pl.ds(0, 64)], r.in_y.at[pl.ds(0, 64)], w.yn)

    def second(self):
        w, r = self.w, self.r
        self.fy.wait_recv()
        r.out_x[0:64] = (self.both(XN, slice(0, 64)) + r.via_y[...].astype(F32)).astype(BF16)
        self.x0 = self.net.send(r.out_x.at[pl.ds(0, 64)], r.in_x.at[pl.ds(0, 64)], w.xn)
        self.fx.wait_recv()
        r.out_y[64:128] = (self.both(YN, slice(64, 128)) + r.via_x[...].astype(F32)).astype(BF16)
        self.y1 = self.net.send(r.out_y.at[pl.ds(64, 64)], r.in_y.at[pl.ds(64, 64)], w.yn)

    def total(self):
        r = self.r
        self.cores[OWN].wait_recv()
        for copy in (self.x1, self.y0, self.x0, self.y1):
            copy.wait_recv()
        return self.both(OWN, slice(0, 128)) + r.in_x[...].astype(F32) + r.in_y[...].astype(F32)


def rows_of(group, n=256):
    return pl.ds(pl.multiple_of(group * n, n), n)


def norm_parts(resid):
    mean = jnp.mean(resid, axis=-1, keepdims=True)
    centered = resid - mean
    variance = jnp.mean(centered * centered, axis=-1, keepdims=True)
    root = lax.rsqrt(variance + EPS)
    return centered * root, root


def norm_back(grad, hat, root, gain):
    scaled = grad * gain
    return root * (
        scaled
        - jnp.mean(scaled, axis=-1, keepdims=True)
        - hat * jnp.mean(scaled * hat, axis=-1, keepdims=True)
    )


def column_sum(value):
    return jnp.sum(value, axis=0, keepdims=True)


def of_head(value, h):
    lanes = lax.broadcasted_iota(jnp.int32, value.shape, 1)
    keep = lanes < 64 if h == 0 else lanes >= 64
    return jnp.where(keep, value, jnp.zeros_like(value))


def attend_forward(net, w, r, s, before, started, gathered, late):
    width = r.width
    net_scale = (width // ATTENTION_HEADS) ** (-0.5)
    cross = types.SimpleNamespace()

    def after_start():
        started()

    def on_group(kind):
        rows = rows_of(w.group[kind])
        if kind == OWN:
            gathered()
        weights = s.w_qkv[...].reshape(width, 384)
        s.qkv[rows] = (dot_nn(s.all_x[rows], weights) + s.part_bias[0:1, 0:384]).astype(BF16)

    gather(net, w, s.all_x, on_group, after_start)
    cross.out = net.send(s.out_z.at[pl.ds(2 * (1 - w.y), 2)], s.w_out.at[:, w.y], w.yn)
    cross.own = net.local(s.out_z.at[pl.ds(2 * w.y, 2)], s.w_out.at[:, w.y])
    cross.own.start()
    value = s.qkv[:, 256:384]
    for h in range(2):
        r.split[h] = of_head(value, h)
    late(0)

    def attend(kind):
        def block(i, carry):
            rows = pl.ds(pl.multiple_of(w.group[kind] * 256 + i * 128, 128), 128)
            query = s.qkv[rows, 0:128]
            mask = r.docs_col[rows, 0:1] == r.docs_row[0:1, :]
            total, logs = None, []
            for h in range(2):
                raw = dot_nt(of_head(query, h), s.qkv[:, 128:256]) * net_scale
                raw = jnp.where(mask, raw, NEGATIVE)
                top = jnp.max(raw, axis=-1, keepdims=True)
                weight = jnp.exp(raw - top)
                mass = jnp.sum(weight, axis=-1, keepdims=True)
                probs = (weight * (1.0 / mass)).astype(BF16)
                piece = dot_nn(probs, r.split[h])
                total = piece if total is None else total + piece
                logs.append(top + jnp.log(mass))
            s.context[rows] = total.astype(BF16)
            lanes = lax.broadcasted_iota(jnp.int32, (128, 128), 1)
            s.logs[rows] = jnp.where(lanes < 64, logs[0], logs[1])
            return carry

        lax.fori_loop(0, 2, block, 0)

    def part(slot):
        return dot_nn(s.context[rows_of(slot, 128)], s.w_out[...].reshape(128, width))

    reduce = Reduce(net, w, r, part)
    attend(DIAG)
    cross.out.wait_recv()
    cross.own.wait()
    reduce.produce(DIAG)
    attend(XN)
    reduce.produce(XN)
    reduce.diag()
    attend(YN)
    reduce.produce(YN)
    reduce.first()
    attend(OWN)
    reduce.produce(OWN)
    reduce.second()
    late(1)
    hat, root = norm_parts(before() + reduce.total() + s.vec[BO : BO + 1])
    normed = hat * s.vec[G1 : G1 + 1] + s.vec[S1 : S1 + 1]
    r.normed[...] = normed
    s.all_n[rows_of(w.slot, 128)] = normed.astype(BF16)
    s.hat_one[...] = hat
    s.root_one[...] = jnp.broadcast_to(root, (128, 128))
    net.drain()


def feed_forward(net, w, r, s, started, ready_in, ready_ffo, late):
    def part(slot):
        return dot_nn(s.inner[rows_of(slot, 128)], s.w_ffo[...].reshape(r.share, r.width))

    reduce = Reduce(net, w, r, part)

    def on_group(kind):
        if kind == OWN:
            ready_in()
        weights = s.w_in[...].reshape(r.width, r.share)
        r.pre[...] = dot_nn(s.all_n[rows_of(w.group[kind])], weights) + s.part_bias[1:2, 0 : r.share]

        def block(i, carry):
            here = pl.ds(pl.multiple_of(i * 32, 32), 32)
            there = pl.ds(pl.multiple_of(w.group[kind] * 256 + i * 32, 32), 32)
            pre = r.pre[here]
            cdf = 0.5 * (1.0 + lax.erf(pre * (0.5**0.5)))
            s.inner[there] = (pre * cdf).astype(BF16)
            bell = jnp.exp(pre * pre * (-0.5)) * ((2.0 * math.pi) ** (-0.5))
            s.slope[there] = (cdf + pre * bell).astype(BF16)
            return carry

        lax.fori_loop(0, 8, block, 0)
        if kind == OWN:
            ready_ffo()
        reduce.produce(kind)
        if kind == YN:
            reduce.first()

    gather(net, w, s.all_n, on_group, started)
    reduce.diag()
    late(0)
    reduce.second()
    late(1)
    hat, root = norm_parts(r.normed[...] + reduce.total() + s.vec[B2 : B2 + 1])
    s.hat_two[...] = hat
    s.root_two[...] = jnp.broadcast_to(root, (128, 128))
    net.drain()
    return hat * s.vec[G2 : G2 + 1] + s.vec[S2 : S2 + 1]


def put_row(ref, row, value):
    for k in range(value.shape[1] // 128):
        ref[row + k : row + k + 1, :] = value[:, k * 128 : (k + 1) * 128]


def feed_backward(net, w, r, s, grad, started, free, late):
    hat = s.hat_two[...]
    back_two = norm_back(grad, hat, s.root_two[:, 0:1], s.vec[G2 : G2 + 1])
    second = back_two.astype(BF16)
    r.normed[...] = back_two
    r.all_second[rows_of(w.slot, 128)] = second

    def part(slot):
        return dot_nt(r.back_pre[rows_of(slot, 128)], s.w_in[...].reshape(r.width, r.share))

    reduce = Reduce(net, w, r, part)

    def after_start():
        put_row(s.sums, 8 * G2, column_sum(grad * hat))
        put_row(s.sums, 8 * S2, column_sum(grad))
        put_row(s.sums, 8 * B2, column_sum(second.astype(F32)))
        started()

    def on_group(kind):
        rows = rows_of(w.group[kind])
        back_inner = dot_nt(r.all_second[rows], s.w_ffo[...].reshape(r.share, r.width))
        r.back_pre[rows] = (back_inner * s.slope[rows].astype(F32)).astype(BF16)
        reduce.produce(kind)
        if kind == YN:
            reduce.first()

    gather(net, w, r.all_second, on_group, after_start)
    reduce.diag()
    free()

    for z in range(4):
        r.g_ffo[z] = dot_tn(s.inner[:, z * 128 : (z + 1) * 128], r.all_second[...]).astype(BF16)
    s.z_ffo = ZScatter(net, w, lambda z: r.g_ffo.at[z], s.land_ffo)
    reduce.second()
    late(0)

    def in_block(i, carry):
        lanes = pl.ds(pl.multiple_of(i * 256, 256), 256)
        piece = dot_tn(s.all_n[:, lanes], r.back_pre[...]).astype(BF16)
        r.g_in[i] = piece.reshape(4, 64, r.share)
        return carry

    lax.fori_loop(0, 4, in_block, 0)
    s.z_in = ZScatter(net, w, lambda z: r.g_in.at[:, z], s.land_in)
    put_row(s.sums, 50, column_sum(r.back_pre[...].astype(F32)))
    late(1)
    grad_one = r.normed[...] + reduce.total()
    hat = s.hat_one[...]
    back_one = norm_back(grad_one, hat, s.root_one[:, 0:1], s.vec[G1 : G1 + 1])
    branch = back_one.astype(BF16)
    r.back_one[...] = back_one
    r.all_branch[rows_of(w.slot, 128)] = branch
    put_row(s.sums, 8 * G1, column_sum(grad_one * hat))
    put_row(s.sums, 8 * S1, column_sum(grad_one))
    put_row(s.sums, 8 * BO, column_sum(branch.astype(F32)))


def attend_backward(net, w, r, s, started, late):
    width = r.width
    scale = (width // ATTENTION_HEADS) ** (-0.5)

    def after_start():
        r.sum_k[...] = jnp.zeros_like(r.sum_k)
        r.sum_v[...] = jnp.zeros_like(r.sum_v)
        key = s.qkv[:, 128:256]
        for h in range(2):
            r.split[h] = of_head(key, h)
        started()

    def on_group(kind):
        rows = rows_of(w.group[kind])
        out_w = s.w_out[...].reshape(128, width)
        r.back_context[rows] = dot_nt(r.all_branch[rows], out_w).astype(BF16)

        def block(i, carry):
            here = pl.ds(pl.multiple_of(w.group[kind] * 256 + i * 128, 128), 128)
            query = s.qkv[here, 0:128]
            upstream = r.back_context[here]
            mask = r.docs_col[here, 0:1] == r.docs_row[0:1, :]
            total = None
            for h in range(2):
                query_h, upstream_h = of_head(query, h), of_head(upstream, h)
                raw = dot_nt(query_h, s.qkv[:, 128:256]) * scale
                raw = jnp.where(mask, raw, NEGATIVE)
                probs = jnp.exp(raw - s.logs[here, h * 64 : h * 64 + 1])
                back = dot_nt(upstream_h, s.qkv[:, 256:384])
                delta = jnp.sum(probs * back, axis=-1, keepdims=True)
                scores = (probs * (back - delta)).astype(BF16)
                piece = dot_nn(scores, r.split[h])
                total = piece if total is None else total + piece
                r.sum_k[...] += dot_tn(scores, query_h)
                r.sum_v[...] += dot_tn(probs.astype(BF16), upstream_h)
            r.back_qkv[here, 0:128] = (total * scale).astype(BF16)
            return carry

        lax.fori_loop(0, 2, block, 0)

    gather(net, w, r.all_branch, on_group, after_start)
    r.back_qkv[:, 128:256] = (r.sum_k[...] * scale).astype(BF16)
    r.back_qkv[:, 256:384] = r.sum_v[...].astype(BF16)

    def part(slot):
        return dot_nt(r.back_qkv[rows_of(slot, 128)], s.w_qkv[...].reshape(width, 384))

    reduce = Reduce(net, w, r, part)
    reduce.produce(DIAG)
    reduce.produce(XN)
    reduce.diag()
    reduce.produce(YN)
    reduce.first()
    reduce.produce(OWN)
    late(0)

    def qkv_block(i, carry):
        lanes = pl.ds(pl.multiple_of(i * 256, 256), 256)
        piece = dot_tn(s.all_x[:, lanes], r.back_qkv[...]).astype(BF16)
        s.g_qkv[i] = piece.reshape(4, 2, 32, 384)
        return carry

    lax.fori_loop(0, 4, qkv_block, 0)
    s.z_qkv = ZScatter(net, w, lambda z: s.g_qkv.at[:, z], s.land_qkv)
    reduce.second()
    r.g_out[...] = dot_tn(s.context[...], r.all_branch[...]).astype(BF16).reshape(2, 2, 32, width)
    cross = net.send(r.g_out.at[:, 1 - w.y], s.g_out_z.at[pl.ds(2 * w.y, 2)], w.yn)
    kept = net.local(r.g_out.at[:, w.y], s.g_out_z.at[pl.ds(2 * w.y, 2)])
    kept.start()
    put_row(s.sums, 48, column_sum(r.back_qkv[:, 0:128].astype(F32)))
    put_row(s.sums, 49, column_sum(r.back_qkv[:, 256:384].astype(F32)))
    late(1)
    grad = r.back_one[...] + reduce.total()
    kept.wait()
    cross.wait_recv()
    s.z_out = ZScatter(net, w, lambda z: s.g_out_z.at[z], s.land_out)
    return grad


FLAT_ROWS = 96


def whole_kernel(r):
    net = Net(r.ssem, r.rsem, r.lsem)
    w = place()
    layers = len(r.layer)
    first, last = r.layer[0], r.layer[-1]
    width, share = r.width, r.share
    unit = share // 4
    r.docs_mine[...] = jnp.broadcast_to(r.docs[...], (8, 128)).astype(F32)

    def pack_qkv(layer):
        for p in range(8):
            for k in range(3):
                lanes = slice(k * width + p * 128, k * width + (p + 1) * 128)
                r.layer[layer].qkv_parts[p // 2, p % 2, :, k * 128 : (k + 1) * 128] = r.qkv_in[layer, :, lanes]

    def pack_inner(layer):
        for p in range(8):
            for z in range(4):
                at = ((p // 2) * 8 + z * 2 + p % 2) * unit
                r.layer[layer].in_parts[p // 2, p % 2, :, z * unit : (z + 1) * unit] = r.inner_in[
                    layer, :, at : at + unit
                ]

    def of_part(ref):
        return lambda p: ref.at[lax.div(p, 2), lax.rem(p, 2)]

    pack_qkv(0)
    net.greet(w)
    hidden = net.swap(w, r.hidden, r.hidden_row)
    docs = net.swap(w, r.docs_mine, r.docs_own)
    parts = net.plane_swap(w, of_part(first.qkv_parts), of_part(first.qkv_piece))
    vec = net.z_spread(w, r.vec_in, r.vec_z)
    first.zg_out = ZGather(net, w, r.out_in.at[0], lambda z: first.out_z.at[z])
    for layer in range(layers):
        pack_inner(layer)
        if layer:
            pack_qkv(layer)
    parts()
    first.zg_qkv = ZGather(net, w, first.qkv_piece, lambda z: first.w_qkv.at[:, z])
    more = []
    for layer in range(layers):
        s = r.layer[layer]
        more.append(net.plane_swap(w, of_part(s.in_parts), of_part(s.in_piece)))
        if layer:
            more.append(net.plane_swap(w, of_part(s.qkv_parts), of_part(s.qkv_piece)))
    vec()
    r.vec_own[...] = (
        r.vec_in[...].astype(F32)
        + r.vec_z[0].astype(F32)
        + r.vec_z[1].astype(F32)
        + r.vec_z[2].astype(F32)
    ).astype(BF16)
    spread = net.plane_swap(w, lambda p: r.vec_own, lambda p: r.vec_all.at[p])
    docs()
    docs = net.plane_swap(w, lambda p: r.docs_own, lambda p: r.docs_all.at[p])
    hidden()
    first.all_x[rows_of(w.slot, 128)] = r.hidden_row[...]

    def unpack():
        spread()
        total = r.vec_all[0].astype(F32)
        for p in range(1, 8):
            total = total + r.vec_all[p].astype(F32)
        r.flat[...] = total
        for layer in range(layers):
            s, base = r.layer[layer], layer * FLAT_ROWS
            for row, name in ((G1, 72), (S1, 56), (BO, 8), (G2, 80), (S2, 64), (B2, 48)):
                for k in range(8):
                    s.vec[row : row + 1, k * 128 : (k + 1) * 128] = r.flat[
                        base + name + k : base + name + k + 1, :
                    ]
            s.part_bias[...] = jnp.zeros_like(s.part_bias)
            s.part_bias[0:1, 0:128] = r.flat[pl.ds(base + w.part, 1), :]
            s.part_bias[0:1, 256:384] = r.flat[pl.ds(base + 88 + w.part, 1), :]
            for z in range(4):
                s.part_bias[1:2, z * unit : (z + 1) * unit] = r.flat[
                    pl.ds(base + 16 + 8 * w.d + 2 * z + w.y, 1), :
                ]
        docs()
        for p in range(8):
            slot = (p // 4) * 4 + (p % 2) * 2 + (p // 2) % 2
            numbers = r.docs_all[p]
            r.docs_row[:, slot * 128 : (slot + 1) * 128] = numbers
            r.docs_col[slot * 128 : (slot + 1) * 128, :] = jnp.broadcast_to(numbers[0:1], (128, 128)).T

    def weights_next(layer, at):
        s = r.layer[layer]
        if at == 0:
            s.zg_in = ZGather(net, w, s.in_piece, lambda z: s.w_in.at[:, z])
        elif at == 1:
            s.zg_in.poll()
            s.zg_ffo = ZGather(net, w, r.ffo_in.at[layer], lambda z: s.w_ffo.at[z])

    swaps = types.SimpleNamespace()
    for layer in range(layers):
        s = r.layer[layer]

        def started(layer=layer, s=s):
            if layer == 0:
                unpack()
                s.zg_out.poll()
                s.zg_qkv.poll()
                for wait in more:
                    wait()

        def gathered(s=s):
            s.zg_qkv.wait()
            s.zg_out.wait()

        def before(layer=layer):
            return r.hidden_row[...].astype(F32) if layer == 0 else r.state[...]

        attend_forward(
            net, w, r, s, before, started, gathered, lambda at, layer=layer: weights_next(layer, at)
        )

        def ready_in(s=s):
            s.zg_in.wait()

        def ready_ffo(s=s):
            s.zg_ffo.poll()
            s.zg_ffo.wait()

        def late(at, layer=layer):
            if layer + 1 < layers:
                n = r.layer[layer + 1]
                if at == 0:
                    n.zg_out = ZGather(net, w, r.out_in.at[layer + 1], lambda z: n.out_z.at[z])
                    n.zg_qkv = ZGather(net, w, n.qkv_piece, lambda z: n.w_qkv.at[:, z])
                else:
                    n.zg_out.poll()
                    n.zg_qkv.poll()
            elif at == 0:
                swaps.grad = net.swap(w, r.out_grad, r.grad_row)

        state = feed_forward(net, w, r, s, lambda: None, ready_in, ready_ffo, late)
        r.state[...] = state
        if layer + 1 < layers:
            r.layer[layer + 1].all_x[rows_of(w.slot, 128)] = state.astype(BF16)
        else:
            r.state_low[...] = state.astype(BF16)
    swaps.grad()
    net.settle()
    swaps.out = net.swap(w, r.state_low, r.out)
    grad = r.grad_row[...].astype(F32)

    def vectors_out(s):
        return net.z_spread(w, s.sums, s.sums_z)

    def vectors_plane(s, wait):
        wait()
        s.sums_own[...] = s.sums[...] + s.sums_z[0] + s.sums_z[1] + s.sums_z[2]
        return net.plane_swap(w, lambda p: s.sums_own, lambda p: s.sums_all.at[p])

    def vectors_in(layer, s, wait):
        wait()
        base = layer * FLAT_ROWS
        for row, name in ((G1, 72), (S1, 56), (BO, 8), (G2, 80), (S2, 64), (B2, 48)):
            total = s.sums_all[0, 8 * row : 8 * row + 8]
            for p in range(1, 8):
                total = total + s.sums_all[p, 8 * row : 8 * row + 8]
            r.vectors[base + name : base + name + 8, :] = total
        for p in range(8):
            r.vectors[base + p : base + p + 1, :] = s.sums_all[p, 48:49]
            r.vectors[base + 88 + p : base + 89 + p, :] = s.sums_all[p, 49:50]
            for z in range(4):
                at = base + 16 + 8 * (p // 2) + 2 * z + p % 2
                r.vectors[at : at + 1, :] = s.sums_all[p, 50 + z : 51 + z]

    def send_inner(s):
        s.in_parts[...] = s.z_in.total().astype(BF16).reshape(4, 2, 32, share)
        return net.plane_swap(w, of_part(s.in_parts), of_part(s.in_piece))

    def send_qkv(s):
        s.qkv_parts[...] = s.z_qkv.total().astype(BF16)
        return net.plane_swap(w, of_part(s.qkv_parts), of_part(s.qkv_piece))

    def place_inner(layer, s, wait):
        wait()
        for p in range(8):
            for z in range(4):
                at = ((p // 2) * 8 + z * 2 + p % 2) * unit
                r.in_grad[layer, :, at : at + unit] = s.in_piece[
                    p // 2, p % 2, :, z * unit : (z + 1) * unit
                ].astype(F32)

    def place_qkv(layer, s, wait):
        wait()
        for p in range(8):
            for k in range(3):
                lanes = slice(k * width + p * 128, k * width + (p + 1) * 128)
                r.qkv_grad[layer, :, lanes] = s.qkv_piece[
                    p // 2, p % 2, :, k * 128 : (k + 1) * 128
                ].astype(F32)

    for layer in reversed(range(layers)):
        s = r.layer[layer]
        a = r.layer[layer + 1] if layer + 1 < layers else None
        s.sums[...] = jnp.zeros_like(s.sums)

        def feed_started(a=a):
            if a is not None:
                a.z_qkv.poll()
                a.z_out.poll()

        def feed_late(at, layer=layer, a=a):
            if a is None:
                return
            if at == 0:
                a.vec_wait = vectors_plane(a, a.vec_wait)
                a.qkv_wait = send_qkv(a)
            else:
                r.out_grad_w[layer + 1] = a.z_out.total()

        def free(a=a):
            if a is not None:
                a.z_ffo.settle()
                a.z_in.settle()

        feed_backward(net, w, r, s, grad, feed_started, free, feed_late)
        if layer + 1 == layers:
            swaps.out()
        net.drain()

        def back_started(layer=layer, s=s, a=a):
            if a is not None:
                place_qkv(layer + 1, a, a.qkv_wait)
                vectors_in(layer + 1, a, a.vec_wait)

        def back_late(at, layer=layer, s=s):
            if at == 0:
                s.z_ffo.poll()
                s.z_in.poll()
            else:
                r.ffo_grad[layer] = s.z_ffo.total()
                s.in_wait = send_inner(s)

        grad = attend_backward(net, w, r, s, back_started, back_late)
        s.vec_wait = vectors_out(s)
        if layer:
            r.state[...] = grad
            grad = r.state[...]
            place_inner(layer, s, s.in_wait)
            net.drain()
    r.state_low[...] = grad.astype(BF16)
    swaps.back = net.swap(w, r.state_low, r.grad_row)
    first.z_qkv.poll()
    first.z_out.poll()
    place_inner(0, first, first.in_wait)
    first.vec_wait = vectors_plane(first, first.vec_wait)
    first.qkv_wait = send_qkv(first)
    r.out_grad_w[0] = first.z_out.total()
    vectors_in(0, first, first.vec_wait)
    swaps.back()
    r.input_grad[...] = r.grad_row[...].astype(F32)
    place_qkv(0, first, first.qkv_wait)
    net.settle()


def plane_body(
    hidden_in,
    document_index,
    out_grad,
    qkv_weight,
    value_bias,
    attention_output_weight,
    ffn_in_weight,
    ffn_out_weight,
    biases,
    norm_gains,
):
    layers = qkv_weight.shape[0]
    width = hidden_in.shape[1]
    inner = ffn_in_weight.shape[2]
    share = inner // 8
    index = lax.axis_index(DP) * 8 + lax.axis_index(CTX)
    n_bias, n_gain, n_value = biases.shape[1], norm_gains.shape[1], value_bias.shape[1]

    def spread(items):
        size = items.shape[1]
        return lax.dynamic_update_slice(
            jnp.zeros((layers, size * 32), items.dtype), items, (0, index * size)
        )

    flat = jnp.concatenate([spread(biases), spread(norm_gains), spread(value_bias)], axis=1)
    flat = flat.reshape(layers * FLAT_ROWS, 128)
    ins = dict(
        hidden=hidden_in,
        docs=document_index,
        out_grad=out_grad,
        qkv_in=qkv_weight,
        out_in=attention_output_weight,
        inner_in=ffn_in_weight,
        ffo_in=ffn_out_weight,
        vec_in=flat,
    )
    outs = dict(
        out=((128, width), BF16),
        input_grad=((128, width), F32),
        qkv_grad=(qkv_weight.shape, F32),
        out_grad_w=(attention_output_weight.shape, F32),
        in_grad=(ffn_in_weight.shape, F32),
        ffo_grad=(ffn_out_weight.shape, F32),
        vectors=((layers * FLAT_ROWS, 128), F32),
    )
    far = dict(hidden=1, out_grad=1, ffo_in=1, out_in=1)
    whole = (1024, width)
    shared = dict(
        hidden_row=((128, width), BF16),
        grad_row=((128, width), BF16),
        docs_mine=((8, 128), F32),
        docs_own=((8, 128), F32),
        docs_all=((8, 8, 128), F32),
        docs_row=((8, 1024), F32),
        docs_col=((1024, 128), F32),
        vec_z=((3, *flat.shape), BF16),
        vec_own=(flat.shape, BF16),
        vec_all=((8, *flat.shape), BF16),
        flat=(flat.shape, F32),
        normed=((128, width), F32),
        state=((128, width), F32),
        state_low=((128, width), BF16),
        back_one=((128, width), F32),
        split=((2, 1024, 128), BF16),
        pre=((256, share), F32),
        all_second=(whole, BF16),
        all_branch=(whole, BF16),
        back_pre=((1024, share), BF16),
        back_context=((1024, 128), BF16),
        back_qkv=((1024, 384), BF16),
        sum_k=((1024, 128), F32),
        sum_v=((1024, 128), F32),
        g_out=((2, 2, 32, width), BF16),
        g_ffo=((4, 128, width), BF16),
        g_in=((4, 4, 64, share), BF16),
        core_out=((4, 128, width), BF16),
        core_in=((4, 128, width), BF16),
        keep=((4, 128, width), F32),
        across=((128, width), BF16),
        via_x=((64, width), BF16),
        via_y=((64, width), BF16),
        out_x=((128, width), BF16),
        out_y=((128, width), BF16),
        in_x=((128, width), BF16),
        in_y=((128, width), BF16),
    )
    each = dict(
        qkv_parts=((4, 2, 32, 384), BF16),
        qkv_piece=((4, 2, 32, 384), BF16),
        in_parts=((4, 2, 32, share), BF16),
        in_piece=((4, 2, 32, share), BF16),
        w_qkv=((4, 4, 2, 32, 384), BF16),
        w_in=((4, 4, 2, 32, share), BF16),
        w_ffo=((4, 128, width), BF16),
        out_z=((4, 32, width), BF16),
        w_out=((2, 2, 32, width), BF16),
        vec=((8, width), F32),
        part_bias=((8, width), F32),
        all_x=(whole, BF16),
        qkv=((1024, 384), BF16),
        context=((1024, 128), BF16),
        logs=((1024, 128), F32),
        all_n=(whole, BF16),
        inner=((1024, share), BF16),
        slope=((1024, share), BF16),
        hat_one=((128, width), F32),
        root_one=((128, 128), F32),
        hat_two=((128, width), F32),
        root_two=((128, 128), F32),
        g_qkv=((4, 4, 2, 32, 384), BF16),
        g_out_z=((4, 32, width), BF16),
        land_ffo=((4, 128, width), BF16),
        land_in=((4, 4, 64, share), BF16),
        land_qkv=((4, 4, 2, 32, 384), BF16),
        land_out=((4, 32, width), BF16),
        sums=((56, 128), F32),
        sums_z=((3, 56, 128), F32),
        sums_own=((56, 128), F32),
        sums_all=((8, 56, 128), F32),
    )

    def kernel(*refs):
        refs = list(refs)

        def take(names):
            return dict(zip(names, [refs.pop(0) for _ in names]))

        r = types.SimpleNamespace(width=width, share=share, **take(ins), **take(outs), **take(shared))
        r.layer = [types.SimpleNamespace(**take(each)) for _ in range(layers)]
        r.ssem, r.rsem, r.lsem = refs
        whole_kernel(r)

    def held(items):
        return [VMEM(shape, dtype) for shape, dtype in items.values()]

    results = pl.pallas_call(
        kernel,
        out_shape=[jax.ShapeDtypeStruct(shape, dtype) for shape, dtype in outs.values()],
        in_specs=[pl.BlockSpec(memory_space=pl.ANY if name in far else VMEM) for name in ins],
        out_specs=[pl.BlockSpec(memory_space=VMEM)] * len(outs),
        scratch_shapes=[
            *held(shared),
            *(held(each) * layers),
            pltpu.SemaphoreType.DMA((COPIES,)),
            pltpu.SemaphoreType.DMA((COPIES,)),
            pltpu.SemaphoreType.DMA((64,)),
        ],
        compiler_params=pltpu.CompilerParams(
            collective_id=0, has_side_effects=True, vmem_limit_bytes=VMEM_LIMIT
        ),
    )(*ins.values())
    out, input_grad, g_qkv, g_out, g_in, g_ffo, vectors = results
    vectors = vectors.reshape(layers, FLAT_ROWS * 128)

    def own(begin, size):
        return lax.dynamic_slice_in_dim(vectors, begin * 128 + index * size, size, 1)

    return (out, input_grad, g_qkv, own(88, n_value), g_out, g_in, g_ffo, own(0, n_bias), own(72, n_gain))


def fits_plane(mesh):
    return mesh.shape[DP] == 4 and mesh.shape[CTX] == 8


def solution(mesh):
    return jax.shard_map(
        plane_body if fits_plane(mesh) else body,
        mesh=mesh,
        in_specs=(
            P(BOTH, None),
            P(DP, CTX),
            P(BOTH, None),
            P(None, BOTH, None),
            P(None, BOTH),
            P(None, BOTH, None),
            P(None, BOTH, None),
            P(None, BOTH, None),
            P(None, BOTH),
            P(None, BOTH),
        ),
        out_specs=(
            P(BOTH, None),
            P(BOTH, None),
            P(None, BOTH, None),
            P(None, BOTH),
            P(None, BOTH, None),
            P(None, BOTH, None),
            P(None, BOTH, None),
            P(None, BOTH),
            P(None, BOTH),
        ),
        check_vma=False,
    )
```

```python
import math
import types

import jax
import jax.numpy as jnp
from jax import lax
from jax.experimental import pallas as pl
from jax.experimental.pallas import tpu as pltpu
from jax.sharding import PartitionSpec as P

ATTENTION_HEADS = 16


DP, CTX = "dp", "ctx"
BOTH = (DP, CTX)

QUERY_KEY, TO_QUERY, TO_KEY = "qhd,khd->hqk", "hqk,khd->qhd", "hqk,qhd->khd"
EPS = 1e-12
NEGATIVE = -1e30


def norm_rows(resid, gain, shift):
    mean = jnp.mean(resid, axis=-1, keepdims=True)
    centered = resid - mean
    variance = jnp.mean(centered * centered, axis=-1, keepdims=True)
    return centered * lax.rsqrt(variance + EPS) * gain + shift


def exact_gelu(value):
    return jax.nn.gelu(value, approximate=False)


def cross(left, right_operand):
    return lax.dot_general(
        left, right_operand, (((0,), (0,)), ((), ())), preferred_element_type=jnp.float32
    )


def back_product(upstream, weight):
    return lax.dot_general(
        upstream, weight, (((1,), (1,)), ((), ())), preferred_element_type=jnp.float32
    )


def by_blocks(step_fn, carry, pieces, token_block):
    count = pieces[0].shape[0]

    def turn(index, state):
        offset = index * token_block
        parts = tuple((lax.dynamic_slice_in_dim(item, offset, token_block, 0) for item in pieces))
        return step_fn(state, parts, offset)

    return lax.fori_loop(0, count // token_block, turn, carry)


def unpack(fetched, width, inner):
    w_qkv, w_out, w_in, w_ffo, value_vec, bias_all, gains = fetched
    value_vec = value_vec.astype(jnp.float32)
    bias_all = bias_all.astype(jnp.float32)
    gains = gains.astype(jnp.float32)
    query_bias = bias_all[0:width]
    out_bias = bias_all[width : 2 * width]
    inner_bias = bias_all[2 * width : 2 * width + inner]
    ffn_bias = bias_all[2 * width + inner : 3 * width + inner]
    shift_one = bias_all[3 * width + inner : 4 * width + inner]
    shift_two = bias_all[4 * width + inner : 5 * width + inner]
    return (
        w_qkv,
        w_out,
        w_in,
        w_ffo,
        value_vec,
        query_bias,
        out_bias,
        inner_bias,
        ffn_bias,
        shift_one,
        shift_two,
        gains[0:width],
        gains[width : 2 * width],
    )


def masked_scores(query_heads, key_piece, seg_own, segment_row, start, scale):
    count = key_piece.shape[0]
    heads = query_heads.shape[1]
    split_key_heads = key_piece.reshape(count, heads, query_heads.shape[2])
    seg_keys = lax.dynamic_slice_in_dim(segment_row, start, count, 0)
    mask = (seg_own[:, None] == seg_keys[None, :])[None]
    raw = (
        jnp.einsum(QUERY_KEY, query_heads, split_key_heads, preferred_element_type=jnp.float32)
        * scale
    )
    return (jnp.where(mask, raw, NEGATIVE), mask, split_key_heads)


def body(
    hidden_in,
    document_index,
    out_grad,
    qkv_weight,
    value_bias,
    attention_output_weight,
    ffn_in_weight,
    ffn_out_weight,
    biases,
    norm_gains,
):
    layers = qkv_weight.shape[0]
    width = qkv_weight.shape[2] // 3
    inner = ffn_in_weight.shape[2]
    heads = ATTENTION_HEADS
    head_width = width // heads
    scale = head_width ** (-0.5)
    rows = hidden_in.shape[0]
    seg_own = document_index[0]
    segment_row = lax.all_gather(document_index, CTX, axis=1, tiled=True)[0]
    row_len = segment_row.shape[0]
    state = hidden_in.astype(jnp.float32)
    saved = []
    for layer in range(layers):
        fetched = (
            lax.all_gather(qkv_weight[layer], BOTH, axis=0, tiled=True),
            lax.all_gather(attention_output_weight[layer], BOTH, axis=0, tiled=True),
            lax.all_gather(ffn_in_weight[layer], BOTH, axis=0, tiled=True),
            lax.all_gather(ffn_out_weight[layer], BOTH, axis=0, tiled=True),
            lax.all_gather(value_bias[layer], BOTH, axis=0, tiled=True),
            lax.all_gather(biases[layer], BOTH, axis=0, tiled=True),
            lax.all_gather(norm_gains[layer], BOTH, axis=0, tiled=True),
        )
        (
            w_qkv,
            w_out,
            w_in,
            w_ffo,
            value_vec,
            query_bias,
            out_bias,
            inner_bias,
            ffn_bias,
            shift_one,
            shift_two,
            gain_one,
            gain_two,
        ) = unpack(fetched, width, inner)
        state_low = state.astype(jnp.bfloat16)
        qkv_bias = jnp.concatenate([query_bias, jnp.zeros_like(query_bias), value_vec])
        qkv_low = (jnp.dot(state_low, w_qkv, preferred_element_type=jnp.float32) + qkv_bias).astype(
            jnp.bfloat16
        )
        query_heads = qkv_low[:, 0:width].reshape(rows, heads, head_width)
        key_low = qkv_low[:, width : 2 * width]
        value_low = qkv_low[:, 2 * width : 3 * width]

        def stats_step(carry, parts, start):
            top, total = carry
            raw, mask, split_key_heads = masked_scores(
                query_heads, parts[0], seg_own, segment_row, start, scale
            )
            new_top = jnp.maximum(top, jnp.max(raw, axis=-1))
            weights = jnp.where(mask, jnp.exp(raw - new_top[:, :, None]), 0.0)
            return (new_top, total * jnp.exp(top - new_top) + jnp.sum(weights, axis=-1))

        stats_init = (
            jnp.full((heads, rows), NEGATIVE, jnp.float32),
            jnp.zeros((heads, rows), jnp.float32),
        )
        held_pair = None
        top, total = by_blocks(
            stats_step, stats_init, (lax.all_gather(key_low, CTX, axis=0, tiled=True),), rows
        )
        log_total = top + jnp.log(total)

        def value_step(carry, parts, start):
            context_acc, exact_acc = carry
            raw, mask, split_key_heads = masked_scores(
                query_heads, parts[0], seg_own, segment_row, start, scale
            )
            split_value_heads = parts[1].reshape(parts[1].shape[0], heads, head_width)
            probs = jnp.where(mask, jnp.exp(raw - log_total[:, :, None]), 0.0)
            probs_low = probs.astype(jnp.bfloat16)
            residue_low = (probs - probs_low.astype(jnp.float32)).astype(jnp.bfloat16)
            part_low = jnp.einsum(
                TO_QUERY, probs_low, split_value_heads, preferred_element_type=jnp.float32
            )
            part_fix = jnp.einsum(
                TO_QUERY, residue_low, split_value_heads, preferred_element_type=jnp.float32
            )
            return (context_acc + part_low, exact_acc + part_fix)

        value_init = (
            jnp.zeros((rows, heads, head_width), jnp.float32),
            jnp.zeros((rows, heads, head_width), jnp.float32),
        )
        context, correction = by_blocks(
            value_step,
            value_init,
            (
                lax.all_gather(key_low, CTX, axis=0, tiled=True),
                lax.all_gather(value_low, CTX, axis=0, tiled=True),
            ),
            rows,
        )
        context_exact = (context + correction).reshape(rows, width)
        context = context.reshape(rows, width)
        context_low = context.astype(jnp.bfloat16)
        resid_one = (
            state + jnp.dot(context_low, w_out, preferred_element_type=jnp.float32) + out_bias
        )
        normed = norm_rows(resid_one, gain_one, shift_one)
        normed_low = normed.astype(jnp.bfloat16)
        pre = jnp.dot(normed_low, w_in, preferred_element_type=jnp.float32) + inner_bias
        inner_low = exact_gelu(pre).astype(jnp.bfloat16)
        resid_two = (
            normed + jnp.dot(inner_low, w_ffo, preferred_element_type=jnp.float32) + ffn_bias
        )
        saved.append(
            (
                fetched,
                state_low,
                qkv_low,
                log_total,
                context_exact,
                context_low,
                resid_one,
                normed_low,
                pre,
                inner_low,
                resid_two,
                held_pair,
            )
        )
        state = norm_rows(resid_two, gain_two, shift_two)
    upstream = out_grad.astype(jnp.float32)
    per_layer = []
    for layer in reversed(range(layers)):
        (
            fetched,
            state_low,
            qkv_low,
            log_total,
            context_exact,
            context_low,
            resid_one,
            normed_low,
            pre,
            inner_low,
            resid_two,
            held_pair,
        ) = saved[layer]
        weights_now = (
            lax.all_gather(qkv_weight[layer], BOTH, axis=0, tiled=True),
            lax.all_gather(attention_output_weight[layer], BOTH, axis=0, tiled=True),
            lax.all_gather(ffn_in_weight[layer], BOTH, axis=0, tiled=True),
            lax.all_gather(ffn_out_weight[layer], BOTH, axis=0, tiled=True),
            lax.all_gather(value_bias[layer], BOTH, axis=0, tiled=True),
            lax.all_gather(biases[layer], BOTH, axis=0, tiled=True),
            lax.all_gather(norm_gains[layer], BOTH, axis=0, tiled=True),
        )
        (
            w_qkv,
            w_out,
            w_in,
            w_ffo,
            value_vec,
            query_bias,
            out_bias,
            inner_bias,
            ffn_bias,
            shift_one,
            shift_two,
            gain_one,
            gain_two,
        ) = unpack(weights_now, width, inner)
        query_low = qkv_low[:, 0:width]
        query_heads = query_low.reshape(rows, heads, head_width)
        key_low = qkv_low[:, width : 2 * width]
        value_low = qkv_low[:, 2 * width : 3 * width]
        unused_two, pull_two = jax.vjp(norm_rows, resid_two, gain_two, shift_two)
        back_two, back_gain_two, back_shift_two = pull_two(upstream)
        back_second = back_two.astype(jnp.bfloat16)
        grad_second = cross(inner_low, back_second)
        back_inner = back_product(back_second, w_ffo)
        unused_pre, pull_gelu = jax.vjp(exact_gelu, pre)
        back_pre = pull_gelu(back_inner)[0].astype(jnp.bfloat16)
        grad_first = cross(normed_low, back_pre)
        back_normed = back_two + back_product(back_pre, w_in)
        normed_again, pull_one = jax.vjp(norm_rows, resid_one, gain_one, shift_one)
        back_one, back_gain_one, back_shift_one = pull_one(back_normed)
        back_branch = back_one.astype(jnp.bfloat16)
        grad_out_proj = cross(context_low, back_branch)
        back_context = back_product(back_branch, w_out).astype(jnp.bfloat16)
        context_heads_back = back_context.reshape(rows, heads, head_width)
        delta = jnp.sum(
            (back_context.astype(jnp.float32) * context_exact).reshape(rows, heads, head_width),
            axis=-1,
        ).T

        def grad_step(carry, parts, start):
            query_sum, key_sums, value_sums = carry
            count = parts[0].shape[0]
            raw, mask, split_key_heads = masked_scores(
                query_heads, parts[0], seg_own, segment_row, start, scale
            )
            split_value_heads = parts[1].reshape(count, heads, head_width)
            probs = jnp.where(mask, jnp.exp(raw - log_total[:, :, None]), 0.0)
            back_probs = jnp.einsum(
                QUERY_KEY,
                context_heads_back,
                split_value_heads,
                preferred_element_type=jnp.float32,
            )
            back_scores = (probs * (back_probs - delta[:, :, None])).astype(jnp.bfloat16)
            query_part = (
                jnp.einsum(
                    TO_QUERY, back_scores, split_key_heads, preferred_element_type=jnp.float32
                )
                * scale
            )
            key_part = (
                jnp.einsum(
                    TO_KEY, back_scores, query_heads, preferred_element_type=jnp.float32
                ).reshape(count, width)
                * scale
            )
            value_part = jnp.einsum(
                TO_KEY,
                probs.astype(jnp.bfloat16),
                context_heads_back,
                preferred_element_type=jnp.float32,
            ).reshape(count, width)
            key_sums = lax.dynamic_update_slice_in_dim(
                key_sums, lax.dynamic_slice_in_dim(key_sums, start, count, 0) + key_part, start, 0
            )
            value_sums = lax.dynamic_update_slice_in_dim(
                value_sums,
                lax.dynamic_slice_in_dim(value_sums, start, count, 0) + value_part,
                start,
                0,
            )
            return (query_sum + query_part, key_sums, value_sums)

        query_init = jnp.zeros((rows, heads, head_width), jnp.float32)
        grad_init = (
            query_init,
            jnp.zeros((row_len, width), jnp.float32),
            jnp.zeros((row_len, width), jnp.float32),
        )
        folded = by_blocks(
            grad_step,
            grad_init,
            (
                lax.all_gather(key_low, CTX, axis=0, tiled=True),
                lax.all_gather(value_low, CTX, axis=0, tiled=True),
            ),
            rows,
        )
        query_sum, key_sums, value_sums = folded
        key_own, value_own = (
            lax.psum_scatter(
                key_sums.astype(jnp.bfloat16), CTX, scatter_dimension=0, tiled=True
            ).astype(jnp.float32),
            lax.psum_scatter(
                value_sums.astype(jnp.bfloat16), CTX, scatter_dimension=0, tiled=True
            ).astype(jnp.float32),
        )
        back_qkv = jnp.concatenate(
            [query_sum.reshape(rows, width), key_own, value_own], axis=1
        ).astype(jnp.bfloat16)
        grad_qkv = cross(state_low, back_qkv)
        back_qkv_float = back_qkv.astype(jnp.float32)
        grad_value_bias = jnp.sum(back_qkv_float[:, 2 * width : 3 * width], axis=0)
        grad_bias = jnp.concatenate(
            [
                jnp.sum(back_qkv_float[:, 0:width], axis=0),
                jnp.sum(back_branch.astype(jnp.float32), axis=0),
                jnp.sum(back_pre.astype(jnp.float32), axis=0),
                jnp.sum(back_second.astype(jnp.float32), axis=0),
                back_shift_one,
                back_shift_two,
            ]
        )
        grad_gain = jnp.concatenate([back_gain_one, back_gain_two])
        upstream = back_one + back_product(back_qkv, w_qkv)
        shards = (
            lax.psum_scatter(grad_qkv, BOTH, scatter_dimension=0, tiled=True),
            lax.psum_scatter(grad_value_bias, BOTH, scatter_dimension=0, tiled=True),
            lax.psum_scatter(grad_out_proj, BOTH, scatter_dimension=0, tiled=True),
            lax.psum_scatter(grad_first, BOTH, scatter_dimension=0, tiled=True),
            lax.psum_scatter(grad_second, BOTH, scatter_dimension=0, tiled=True),
            lax.psum_scatter(grad_bias, BOTH, scatter_dimension=0, tiled=True),
            lax.psum_scatter(grad_gain, BOTH, scatter_dimension=0, tiled=True),
        )
        per_layer.append(shards)
    ordered = per_layer[::-1]
    stacked = tuple((jnp.stack([item[member] for item in ordered]) for member in range(7)))
    return (
        state.astype(jnp.bfloat16),
        upstream,
        stacked[0],
        stacked[1],
        stacked[2],
        stacked[3],
        stacked[4],
        stacked[5],
        stacked[6],
    )


MESH = pl.DeviceIdType.MESH
F32 = jnp.float32
BF16 = jnp.bfloat16
VMEM = pltpu.VMEM
VMEM_LIMIT = 62 * 2**20
PHASE, COPIES = 32, 208
OWN, XN, YN, DIAG = range(4)
G1, S1, BO, G2, S2, B2 = range(6)


def dot_nn(a, b):
    return lax.dot_general(a, b, (((1,), (0,)), ((), ())), preferred_element_type=F32)


def dot_nt(a, b):
    return lax.dot_general(a, b, (((1,), (1,)), ((), ())), preferred_element_type=F32)


def dot_tn(a, b):
    return lax.dot_general(a, b, (((0,), (0,)), ((), ())), preferred_element_type=F32)


def turned(two_bits):
    return lax.rem(two_bits, 2) * 2 + lax.div(two_bits, 2)


def place():
    d, t = lax.axis_index(DP), lax.axis_index(CTX)
    x, c = lax.div(d, 2), lax.rem(d, 2)
    z, y = lax.div(t, 2), lax.rem(t, 2)
    w = types.SimpleNamespace(d=d, x=x, c=c, z=z, y=y)
    w.part = d * 2 + y
    w.group = (x * 2 + y, (1 - x) * 2 + y, x * 2 + 1 - y, (1 - x) * 2 + 1 - y)
    w.slot = w.group[OWN] * 2 + c
    w.xn, w.yn, w.sib = ((1 - x) * 2 + c, t), (d, z * 2 + 1 - y), (x * 2 + 1 - c, t)
    w.plane = []
    for bits in range(1, 8):
        xx = 1 - x if bits & 4 else x
        cc = 1 - c if bits & 2 else c
        yy = 1 - y if bits & 1 else y
        w.plane.append(((xx * 2 + cc, z * 2 + yy), (xx * 2 + cc) * 2 + yy))
    w.zs = [(d, lax.rem(z + k, 4) * 2 + y) for k in (1, 2, 3)]
    w.far = lax.rem(z + 2, 4)
    w.up, w.down, w.over = (d, (z + 1) * 2 + y), (d, (z - 1) * 2 + y), (d, w.far * 2 + y)
    w.middle = (z == 1) | (z == 2)
    w.edge = (z == 0) | (z == 3)
    w.end = jnp.where(z == 1, 0, 3)
    w.near_end = (d, w.end * 2 + y)
    w.inside = jnp.where(z == 0, 1, 2)
    w.near_middle = (d, w.inside * 2 + y)
    w.opposite = 3 - z
    w.away = d != turned(z)
    w.home = d == turned(z)
    w.swap = (turned(z), turned(d) * 2 + y)
    return w


class Maybe:
    def __init__(self, copy, sends, receives):
        self.copy, self.sends, self.receives = copy, sends, receives

    def start(self):
        pl.when(self.sends)(self.copy.start)

    def wait_send(self):
        pl.when(self.sends)(self.copy.wait_send)

    def wait_recv(self):
        pl.when(self.receives)(self.copy.wait_recv)


class Net:
    def __init__(self, ssem, rsem, lsem):
        self.ssem, self.rsem, self.lsem = ssem, rsem, lsem
        self.sent, self.slow, self.scatters, self.at, self.near = [], [], [], PHASE, 0
        self.phase = 0

    def greet(self, w):
        barrier = pltpu.get_barrier_semaphore()
        devices = [device for device, _ in w.plane] + w.zs
        for device in devices:
            pl.semaphore_signal(barrier, inc=1, device_id=device, device_id_type=MESH)

        @pl.when(w.away)
        def _():
            pl.semaphore_signal(barrier, inc=1, device_id=w.swap, device_id_type=MESH)

        return lambda: pl.semaphore_wait(barrier, len(devices) + jnp.where(w.away, 1, 0))

    def make(self, src, dst, device, slow=True):
        at = self.at if slow else self.phase
        if slow:
            self.at += 1
        else:
            self.phase += 1
        return pltpu.make_async_remote_copy(
            src_ref=src,
            dst_ref=dst,
            send_sem=self.ssem.at[at],
            recv_sem=self.rsem.at[at],
            device_id=device,
            device_id_type=MESH,
        )

    def maybe(self, src, dst, device, sends, receives):
        copy = Maybe(self.make(src, dst, device), sends, receives)
        self.slow.append(copy)
        return copy

    def send(self, src, dst, device, slow=False):
        copy = self.make(src, dst, device, slow)
        copy.start()
        (self.slow if slow else self.sent).append(copy)
        return copy

    def local(self, src, dst):
        copy = pltpu.make_async_copy(src, dst, self.lsem.at[self.near])
        self.near += 1
        return copy

    def swap(self, w, src, dst):
        far = Maybe(self.make(src, dst, w.swap), w.away, w.away)
        near = self.local(src, dst)
        far.start()
        pl.when(w.home)(near.start)

        def wait():
            far.wait_recv()
            far.wait_send()
            pl.when(w.home)(near.wait)

        return wait

    def plane_swap(self, w, at, to):
        copies = [self.send(at(part), to(w.part), device, True) for device, part in w.plane]
        own = self.local(at(w.part), to(w.part))
        own.start()

        def wait():
            own.wait()
            for copy in copies:
                copy.wait_recv()

        return wait

    def z_all(self, w, src, at):
        copies = [self.send(src, at(w.z), device, True) for device in w.zs]
        own = self.local(src, at(w.z))
        own.start()

        def wait():
            own.wait()
            for copy in copies:
                copy.wait_recv()

        return wait

    def z_spread(self, w, src, land):
        copies = [self.send(src, land.at[k], device, True) for k, device in enumerate(w.zs)]

        def wait():
            for copy in copies:
                copy.wait_recv()

        return wait

    def drain(self):
        for copy in self.sent:
            copy.wait_send()
        self.sent, self.phase = [], 0

    def settle(self):
        self.drain()
        for copy in self.slow:
            copy.wait_send()
        self.slow = []
        for scatter in self.scatters:
            scatter.settle()


class ZGather:
    def __init__(self, net, w, src, at):
        self.w, here = w, at(w.z)
        self.over = net.send(src, here, w.over, True)
        self.up = net.maybe(src, here, w.up, w.z < 3, w.z > 0)
        self.down = net.maybe(src, here, w.down, w.z > 0, w.z < 3)
        far = at(w.far)
        self.on = net.maybe(far, far, w.near_end, w.middle, w.edge)
        self.own = net.local(src, here)
        self.up.start()
        self.down.start()
        self.own.start()

    def poll(self):
        pl.when(self.w.middle)(self.over.wait_recv)
        self.on.start()

    def wait(self):
        pl.when(self.w.edge)(self.over.wait_recv)
        self.own.wait()
        for copy in (self.up, self.down, self.on):
            copy.wait_recv()


class ZScatter:
    def __init__(self, net, w, at, land):
        self.w, self.at, self.land = w, at, land
        self.on = net.maybe(at(w.opposite), land.at[3], w.near_middle, w.edge, w.middle)
        self.on.start()
        self.up = net.maybe(at(lax.rem(w.z + 1, 4)), land.at[0], w.up, w.z < 3, w.z > 0)
        self.down = net.maybe(at(lax.rem(w.z + 3, 4)), land.at[1], w.down, w.z > 0, w.z < 3)
        self.end_over = net.maybe(at(w.far), land.at[2], w.over, w.edge, w.middle)
        self.mid_over = net.maybe(land.at[3], land.at[2], w.over, w.middle, w.edge)
        self.sends = (self.on, self.up, self.down, self.end_over, self.mid_over)
        net.slow = [copy for copy in net.slow if copy not in self.sends]
        net.scatters.append(self)
        for copy in (self.end_over, self.up, self.down):
            copy.start()

        @pl.when(w.z == 0)
        def _():
            land[0] = jnp.zeros(land.shape[1:], BF16)

        @pl.when(w.z == 3)
        def _():
            land[1] = jnp.zeros(land.shape[1:], BF16)

    def poll(self):
        @pl.when(self.w.middle)
        def _():
            self.on.copy.wait_recv()
            own = self.at(self.w.far)[...].astype(F32)
            self.land[3] = (self.land[3].astype(F32) + own).astype(BF16)

        self.mid_over.start()

    def settle(self):
        for copy in self.sends:
            copy.wait_send()
        self.sends = ()

    def total(self):
        for copy in (self.up, self.down, self.end_over, self.mid_over):
            copy.wait_recv()
        land = self.land
        return (
            self.at(self.w.z)[...].astype(F32)
            + land[0].astype(F32)
            + land[1].astype(F32)
            + land[2].astype(F32)
        )


def nothing():
    pass


def gather(net, w, buf, on_group, after_start=nothing, after_forward=None):
    def half(group, h):
        return buf.at[pl.ds(pl.multiple_of((group * 2 + w.c) * 128 + h * 64, 64), 64)]

    def put(group, h, device):
        ref = half(group, h)
        return net.send(ref, ref, device)

    own, xn, yn, diag = w.group
    x0 = put(own, 0, w.xn)
    y1 = put(own, 1, w.yn)
    whole = buf.at[rows_of(w.slot, 128)]
    c0 = net.send(whole, whole, w.sib)
    x1 = put(own, 1, w.xn)
    y0 = put(own, 0, w.yn)
    after_start()
    if after_forward is None:
        c0.wait_recv()
        on_group(OWN)
    x0.wait_recv()
    d0 = put(xn, 0, w.yn)
    cx0 = put(xn, 0, w.sib)
    y1.wait_recv()
    d1 = put(yn, 1, w.xn)
    cy1 = put(yn, 1, w.sib)
    if after_forward is not None:
        after_forward()
        c0.wait_recv()
        on_group(OWN)
    x1.wait_recv()
    cx1 = put(xn, 1, w.sib)
    y0.wait_recv()
    cy0 = put(yn, 0, w.sib)
    cx0.wait_recv()
    cx1.wait_recv()
    on_group(XN)
    cy0.wait_recv()
    cy1.wait_recv()
    on_group(YN)
    d0.wait_recv()
    cd0 = put(diag, 0, w.sib)
    d1.wait_recv()
    cd1 = put(diag, 1, w.sib)
    cd0.wait_recv()
    cd1.wait_recv()
    on_group(DIAG)


class Reduce:
    def __init__(self, net, w, r, part):
        self.net, self.w, self.r, self.part = net, w, r, part
        self.cores = [None] * 4

    def produce(self, kind):
        w, r = self.w, self.r
        group = w.group[kind]
        r.core_out[kind] = self.part(group * 2 + 1 - w.c).astype(BF16)
        self.cores[kind] = self.net.send(r.core_out.at[kind], r.core_in.at[kind], w.sib)
        r.keep[kind] = self.part(group * 2 + w.c)

    def both(self, kind, rows):
        return self.r.keep[kind, rows] + self.r.core_in[kind, rows].astype(F32)

    def diag(self):
        w, r = self.w, self.r
        self.cores[DIAG].wait_recv()
        r.across[...] = self.both(DIAG, slice(0, 128)).astype(BF16)
        self.fy = self.net.send(r.across.at[pl.ds(0, 64)], r.via_y, w.yn)
        self.fx = self.net.send(r.across.at[pl.ds(64, 64)], r.via_x, w.xn)

    def first(self):
        w, r = self.w, self.r
        self.cores[XN].wait_recv()
        r.out_x[64:128] = self.both(XN, slice(64, 128)).astype(BF16)
        self.x1 = self.net.send(r.out_x.at[pl.ds(64, 64)], r.in_x.at[pl.ds(64, 64)], w.xn)
        self.cores[YN].wait_recv()
        r.out_y[0:64] = self.both(YN, slice(0, 64)).astype(BF16)
        self.y0 = self.net.send(r.out_y.at[pl.ds(0, 64)], r.in_y.at[pl.ds(0, 64)], w.yn)

    def second(self):
        w, r = self.w, self.r
        self.fy.wait_recv()
        r.out_x[0:64] = (self.both(XN, slice(0, 64)) + r.via_y[...].astype(F32)).astype(BF16)
        self.x0 = self.net.send(r.out_x.at[pl.ds(0, 64)], r.in_x.at[pl.ds(0, 64)], w.xn)
        self.fx.wait_recv()
        r.out_y[64:128] = (self.both(YN, slice(64, 128)) + r.via_x[...].astype(F32)).astype(BF16)
        self.y1 = self.net.send(r.out_y.at[pl.ds(64, 64)], r.in_y.at[pl.ds(64, 64)], w.yn)

    def total(self):
        r = self.r
        self.cores[OWN].wait_recv()
        for copy in (self.x1, self.y0, self.x0, self.y1):
            copy.wait_recv()
        return self.both(OWN, slice(0, 128)) + r.in_x[...].astype(F32) + r.in_y[...].astype(F32)


def rows_of(group, n=256):
    return pl.ds(pl.multiple_of(group * n, n), n)


def norm_parts(resid):
    mean = jnp.mean(resid, axis=-1, keepdims=True)
    centered = resid - mean
    variance = jnp.mean(centered * centered, axis=-1, keepdims=True)
    root = lax.rsqrt(variance + EPS)
    return centered * root, root


def norm_back(grad, hat, root, gain):
    scaled = grad * gain
    return root * (
        scaled
        - jnp.mean(scaled, axis=-1, keepdims=True)
        - hat * jnp.mean(scaled * hat, axis=-1, keepdims=True)
    )


def column_sum(value):
    return jnp.sum(value, axis=0, keepdims=True)


def by_head(value):
    lanes = lax.broadcasted_iota(jnp.int32, value.shape, 1)
    zero = jnp.zeros_like(value)
    return jnp.concatenate([jnp.where(lanes < 64, value, zero), jnp.where(lanes >= 64, value, zero)], axis=0)


def own_lanes(first, second):
    lanes = lax.broadcasted_iota(jnp.int32, first.shape, 1)
    return jnp.where(lanes < 64, first, second)


def attend_forward(net, w, r, s, before, started, ready, gathered, pump):
    width = r.width
    scale = jnp.asarray((width // ATTENTION_HEADS) ** (-0.5), BF16)
    cross = types.SimpleNamespace()

    def on_group(kind):
        rows = rows_of(w.group[kind])
        weights = s.w_qkv[...].reshape(width, 384)
        s.qkv[rows] = (dot_nn(s.all_x[rows], weights) + s.part_bias[0:1, 0:384]).astype(BF16)

    gather(net, w, s.all_x, on_group, started, ready)
    cross.out = net.send(s.out_z.at[pl.ds(2 * (1 - w.y), 2)], s.w_out.at[:, w.y], w.yn)
    cross.own = net.local(s.out_z.at[pl.ds(2 * w.y, 2)], s.w_out.at[:, w.y])
    cross.own.start()
    def attend(kind, begin=0, end=2):
        def block(i, carry):
            rows = pl.ds(pl.multiple_of(w.group[kind] * 256 + i * 128, 128), 128)
            both = by_head(s.qkv[rows, 0:128] * scale)
            mask = r.docs_col[rows, 0:1] == r.docs_row[0:1, :]
            raw_both = dot_nt(both, s.qkv[:, 128:256])
            probs, logs = [], []
            for h in range(2):
                raw = jnp.where(mask, raw_both[h * 128 : (h + 1) * 128], NEGATIVE)
                top = jnp.max(raw, axis=-1, keepdims=True)
                weight = jnp.exp(raw - top)
                mass = jnp.sum(weight, axis=-1, keepdims=True)
                probs.append((weight * (1.0 / mass)).astype(BF16))
                logs.append(top + jnp.log(mass))
            total = dot_nn(jnp.concatenate(probs, axis=0), s.qkv[:, 256:384])
            s.context[rows] = own_lanes(total[0:128], total[128:256]).astype(BF16)
            s.logs[rows] = own_lanes(
                jnp.broadcast_to(logs[0], (128, 128)), jnp.broadcast_to(logs[1], (128, 128))
            )
            return carry

        lax.fori_loop(begin, end, block, 0)

    def part(slot):
        return dot_nn(s.context[rows_of(slot, 128)], s.w_out[...].reshape(128, width))

    reduce = Reduce(net, w, r, part)
    attend(DIAG)
    cross.out.wait_recv()
    cross.own.wait()
    reduce.produce(DIAG)
    attend(XN, 0, 1)
    reduce.diag()
    attend(XN, 1, 2)
    reduce.produce(XN)
    attend(YN)
    reduce.produce(YN)
    reduce.first()
    gathered()
    pump()
    attend(OWN)
    reduce.produce(OWN)
    reduce.second()
    hat, root = norm_parts(before() + reduce.total() + s.vec[BO : BO + 1])
    normed = hat * s.vec[G1 : G1 + 1] + s.vec[S1 : S1 + 1]
    r.normed[...] = normed
    s.all_n[rows_of(w.slot, 128)] = normed.astype(BF16)
    s.hat_one[...] = hat
    s.root_one[...] = jnp.broadcast_to(root, (128, 128))
    net.drain()


def feed_forward(net, w, r, s, ready_in, ready_ffo, pump):
    def part(slot):
        return dot_nn(s.inner[rows_of(slot, 128)], s.w_ffo[...].reshape(r.share, r.width))

    reduce = Reduce(net, w, r, part)

    def on_group(kind):
        weights = s.w_in[...].reshape(r.width, r.share)
        r.pre[...] = dot_nn(s.all_n[rows_of(w.group[kind])], weights) + s.part_bias[1:2, 0 : r.share]

        def block(i, carry):
            here = pl.ds(pl.multiple_of(i * 32, 32), 32)
            there = pl.ds(pl.multiple_of(w.group[kind] * 256 + i * 32, 32), 32)
            pre = r.pre[here]
            cdf = 0.5 * (1.0 + lax.erf(pre * (0.5**0.5)))
            s.inner[there] = (pre * cdf).astype(BF16)
            bell = jnp.exp(pre * pre * (-0.5)) * ((2.0 * math.pi) ** (-0.5))
            s.slope[there] = (cdf + pre * bell).astype(BF16)
            return carry

        lax.fori_loop(0, 8, block, 0)
        if kind == YN:
            ready_ffo()
            reduce.produce(XN)
            reduce.produce(YN)
            reduce.first()

    gather(net, w, s.all_n, on_group, lambda: pump(0), ready_in)
    reduce.produce(DIAG)
    reduce.diag()
    reduce.produce(OWN)
    reduce.second()
    pump(1)
    hat, root = norm_parts(r.normed[...] + reduce.total() + s.vec[B2 : B2 + 1])
    s.hat_two[...] = hat
    s.root_two[...] = jnp.broadcast_to(root, (128, 128))
    net.drain()
    return hat * s.vec[G2 : G2 + 1] + s.vec[S2 : S2 + 1]


def put_row(ref, row, value):
    for k in range(value.shape[1] // 128):
        ref[row + k : row + k + 1, :] = value[:, k * 128 : (k + 1) * 128]


def feed_backward(net, w, r, s, grad, started, free, pump):
    hat = s.hat_two[...]
    back_two = norm_back(grad, hat, s.root_two[:, 0:1], s.vec[G2 : G2 + 1])
    second = back_two.astype(BF16)
    r.normed[...] = back_two
    r.all_second[rows_of(w.slot, 128)] = second

    def part(slot):
        return dot_nt(r.back_pre[rows_of(slot, 128)], s.w_in[...].reshape(r.width, r.share))

    reduce = Reduce(net, w, r, part)

    def after_start():
        put_row(s.sums, 8 * G2, column_sum(grad * hat))
        put_row(s.sums, 8 * S2, column_sum(grad))
        put_row(s.sums, 8 * B2, column_sum(second.astype(F32)))
        started()

    def on_group(kind):
        rows = rows_of(w.group[kind])
        back_inner = dot_nt(r.all_second[rows], s.w_ffo[...].reshape(r.share, r.width))
        r.back_pre[rows] = (back_inner * s.slope[rows].astype(F32)).astype(BF16)
        if kind == YN:
            reduce.produce(XN)
            reduce.produce(YN)
            reduce.first()

    gather(net, w, r.all_second, on_group, after_start)
    reduce.produce(DIAG)
    reduce.diag()
    reduce.produce(OWN)
    free()

    for z in range(4):
        r.g_ffo[z] = dot_tn(s.inner[:, z * 128 : (z + 1) * 128], r.all_second[...]).astype(BF16)
    s.z_ffo = ZScatter(net, w, lambda z: r.g_ffo.at[z], s.land_ffo)
    reduce.second()

    def in_block(i, carry):
        lanes = pl.ds(pl.multiple_of(i * 256, 256), 256)
        piece = dot_tn(s.all_n[:, lanes], r.back_pre[...]).astype(BF16)
        r.g_in[i] = piece.reshape(4, 64, r.share)
        return carry

    lax.fori_loop(0, 4, in_block, 0)
    s.z_in = ZScatter(net, w, lambda z: r.g_in.at[:, z], s.land_in)
    put_row(s.sums, 50, column_sum(r.back_pre[...].astype(F32)))
    pump()
    grad_one = r.normed[...] + reduce.total()
    hat = s.hat_one[...]
    back_one = norm_back(grad_one, hat, s.root_one[:, 0:1], s.vec[G1 : G1 + 1])
    branch = back_one.astype(BF16)
    r.back_one[...] = back_one
    r.all_branch[rows_of(w.slot, 128)] = branch

    def sums():
        put_row(s.sums, 8 * G1, column_sum(grad_one * hat))
        put_row(s.sums, 8 * S1, column_sum(grad_one))
        put_row(s.sums, 8 * BO, column_sum(branch.astype(F32)))

    return sums


def attend_backward(net, w, r, s, started, pump, done):
    width = r.width
    scale = jnp.asarray((width // ATTENTION_HEADS) ** (-0.5), BF16)

    def after_start():
        r.sum_k[...] = jnp.zeros_like(r.sum_k)
        r.sum_v[...] = jnp.zeros_like(r.sum_v)
        started()

    def on_group(kind):
        rows = rows_of(w.group[kind])
        out_w = s.w_out[...].reshape(128, width)
        r.back_context[rows] = dot_nt(r.all_branch[rows], out_w).astype(BF16)

        def block(i, carry):
            here = pl.ds(pl.multiple_of(w.group[kind] * 256 + i * 128, 128), 128)
            query = by_head(s.qkv[here, 0:128] * scale)
            upstream = by_head(r.back_context[here])
            mask = r.docs_col[here, 0:1] == r.docs_row[0:1, :]
            raw_both = dot_nt(query, s.qkv[:, 128:256])
            back_both = dot_nt(upstream, s.qkv[:, 256:384])
            probs_both, scores_both = [], []
            for h in range(2):
                rows_h = slice(h * 128, (h + 1) * 128)
                raw = jnp.where(mask, raw_both[rows_h], NEGATIVE)
                probs = jnp.exp(raw - s.logs[here, h * 64 : h * 64 + 1])
                back = back_both[rows_h]
                delta = jnp.sum(probs * back, axis=-1, keepdims=True)
                scores_both.append((probs * (back - delta)).astype(BF16))
                probs_both.append(probs.astype(BF16))
            scores = jnp.concatenate(scores_both, axis=0)
            total = dot_nn(scores, s.qkv[:, 128:256])
            r.sum_k[...] += dot_tn(scores, query)
            r.sum_v[...] += dot_tn(jnp.concatenate(probs_both, axis=0), upstream)
            total = own_lanes(total[0:128], total[128:256])
            r.back_qkv[here, 0:128] = (total * scale.astype(F32)).astype(BF16)
            return carry

        lax.fori_loop(0, 2, block, 0)

    gather(net, w, r.all_branch, on_group, after_start)
    r.back_qkv[:, 128:256] = r.sum_k[...].astype(BF16)
    r.back_qkv[:, 256:384] = r.sum_v[...].astype(BF16)

    def part(slot):
        return dot_nt(r.back_qkv[rows_of(slot, 128)], s.w_qkv[...].reshape(width, 384))

    reduce = Reduce(net, w, r, part)
    reduce.produce(DIAG)
    reduce.produce(XN)
    reduce.produce(YN)
    reduce.diag()
    reduce.first()
    put_row(s.sums, 48, column_sum(r.back_qkv[:, 0:128].astype(F32)))
    put_row(s.sums, 49, column_sum(r.back_qkv[:, 256:384].astype(F32)))
    pump(0)

    def qkv_block(i, carry):
        lanes = pl.ds(pl.multiple_of(i * 256, 256), 256)
        piece = dot_tn(s.all_x[:, lanes], r.back_qkv[...]).astype(BF16)
        s.g_qkv[i] = piece.reshape(4, 2, 32, 384)
        return carry

    lax.fori_loop(0, 4, qkv_block, 0)
    s.z_qkv = ZScatter(net, w, lambda z: s.g_qkv.at[:, z], s.land_qkv)
    reduce.produce(OWN)
    reduce.second()
    r.g_out[...] = dot_tn(s.context[...], r.all_branch[...]).astype(BF16).reshape(2, 2, 32, width)
    cross = net.send(r.g_out.at[:, 1 - w.y], s.g_out_z.at[pl.ds(2 * w.y, 2)], w.yn)
    kept = net.local(r.g_out.at[:, w.y], s.g_out_z.at[pl.ds(2 * w.y, 2)])
    kept.start()
    pump(1)
    grad = r.back_one[...] + reduce.total()
    done(grad)
    kept.wait()
    cross.wait_recv()
    s.z_out = ZScatter(net, w, lambda z: s.g_out_z.at[z], s.land_out)


FLAT_ROWS = 96


def whole_kernel(r):
    net = Net(r.ssem, r.rsem, r.lsem)
    w = place()
    layers = len(r.layer)
    first, last = r.layer[0], r.layer[-1]
    width, share = r.width, r.share
    unit = share // 4
    r.docs_mine[...] = jnp.broadcast_to(r.docs[...], (8, 128)).astype(F32)

    def pack_qkv(layer):
        for p in range(8):
            for k in range(3):
                lanes = slice(k * width + p * 128, k * width + (p + 1) * 128)
                r.layer[layer].qkv_parts[p // 2, p % 2, :, k * 128 : (k + 1) * 128] = r.qkv_in[layer, :, lanes]

    def pack_inner(layer):
        for p in range(8):
            for z in range(4):
                at = ((p // 2) * 8 + z * 2 + p % 2) * unit
                r.layer[layer].in_parts[p // 2, p % 2, :, z * unit : (z + 1) * unit] = r.inner_in[
                    layer, :, at : at + unit
                ]

    owner = w.d * 8 + w.z * 2 + w.y
    smalls = ((r.biases, r.n_bias, 0, 3), (r.norm_gains, r.n_gain, 3, 1), (r.value_bias, r.n_value, 4, 1))

    def shifted(size, rows):
        j = lax.broadcasted_iota(jnp.int32, (size, rows * 128), 0)
        k = lax.broadcasted_iota(jnp.int32, (size, rows * 128), 1)
        return jnp.where(k == j + lax.rem(owner * size, 128), 1.0, 0.0)

    def pack_vectors():
        r.vec_f[...] = jnp.zeros_like(r.vec_f)
        for ref, size, row, rows in smalls:
            placed = dot_nn(ref[...], shifted(size, rows).astype(BF16))
            for layer in range(layers):
                for k in range(rows):
                    at = 5 * layer + row + k
                    r.vec_f[at : at + 1, :] = placed[layer : layer + 1, k * 128 : (k + 1) * 128]
        r.vec_in[...] = r.vec_f[...].astype(BF16)

    def unpack_vectors():
        for (_, size, _, rows), base, out in zip(
            smalls, (0, 72, 88), (r.bias_grad, r.gain_grad, r.value_grad)
        ):
            for layer in range(layers):
                begin = layer * FLAT_ROWS + base + lax.div(owner * size, 128)
                for k in range(rows):
                    r.lined[layer : layer + 1, k * 128 : (k + 1) * 128] = r.vectors[pl.ds(begin + k, 1), :]
            out[...] = lax.dot_general(
                r.lined[:, 0 : rows * 128],
                shifted(size, rows),
                (((1,), (1,)), ((), ())),
                precision=lax.Precision.HIGHEST,
                preferred_element_type=F32,
            )[0:layers]

    def of_part(ref):
        return lambda p: ref.at[lax.div(p, 2), lax.rem(p, 2)]

    met = net.greet(w)
    pack_vectors()
    pack_qkv(0)
    pack_inner(0)
    met()
    parts = net.plane_swap(w, of_part(first.qkv_parts), of_part(first.qkv_piece))
    hidden = net.swap(w, r.hidden, r.hidden_row)
    docs = net.swap(w, r.docs_mine, r.docs_own)
    vec = net.z_all(w, r.vec_in, lambda z: r.vec_z.at[z])
    parts()
    first.zg_qkv = ZGather(net, w, first.qkv_piece, lambda z: first.w_qkv.at[:, z])
    first.zg_out = ZGather(net, w, r.out_in.at[0], lambda z: first.out_z.at[z])
    first.in_parted = net.plane_swap(w, of_part(first.in_parts), of_part(first.in_piece))
    vec()
    spread = net.plane_swap(w, lambda p: r.vec_z, lambda p: r.vec_all.at[p])
    docs()
    docs = net.plane_swap(w, lambda p: r.docs_own, lambda p: r.docs_all.at[p])
    hidden()
    first.all_x[rows_of(w.slot, 128)] = r.hidden_row[...]

    def unpack():
        spread()
        r.flat[...] = jnp.zeros_like(r.flat)
        for p in range(8):
            for z in range(4):
                owner = (p // 2) * 8 + z * 2 + p % 2
                piece = r.vec_all[p, z].astype(F32)
                for layer in range(layers):
                    base = layer * FLAT_ROWS
                    at = base + r.n_bias * owner // 128
                    r.flat[at : at + 3, :] += piece[5 * layer : 5 * layer + 3]
                    at = base + 72 + r.n_gain * owner // 128
                    r.flat[at : at + 1, :] += piece[5 * layer + 3 : 5 * layer + 4]
                    at = base + 88 + r.n_value * owner // 128
                    r.flat[at : at + 1, :] += piece[5 * layer + 4 : 5 * layer + 5]
        for layer in range(layers):
            s, base = r.layer[layer], layer * FLAT_ROWS
            for row, name in ((G1, 72), (S1, 56), (BO, 8), (G2, 80), (S2, 64), (B2, 48)):
                for k in range(8):
                    s.vec[row : row + 1, k * 128 : (k + 1) * 128] = r.flat[
                        base + name + k : base + name + k + 1, :
                    ]
            s.part_bias[...] = jnp.zeros_like(s.part_bias)
            s.part_bias[0:1, 0:128] = r.flat[pl.ds(base + w.part, 1), :]
            s.part_bias[0:1, 256:384] = r.flat[pl.ds(base + 88 + w.part, 1), :]
            for z in range(4):
                s.part_bias[1:2, z * unit : (z + 1) * unit] = r.flat[
                    pl.ds(base + 16 + 8 * w.d + 2 * z + w.y, 1), :
                ]
        docs()
        for p in range(8):
            slot = (p // 4) * 4 + (p % 2) * 2 + (p // 2) % 2
            numbers = r.docs_all[p]
            r.docs_row[:, slot * 128 : (slot + 1) * 128] = numbers
            r.docs_col[slot * 128 : (slot + 1) * 128, :] = jnp.broadcast_to(numbers[0:1], (128, 128)).T

    def bring_attention(layer):
        s = r.layer[layer]
        s.zg_qkv = ZGather(net, w, s.qkv_piece, lambda z: s.w_qkv.at[:, z])
        s.zg_out = ZGather(net, w, r.out_in.at[layer], lambda z: s.out_z.at[z])

    def bring_in(layer):
        s = r.layer[layer]
        s.zg_qkv.poll()
        s.zg_out.poll()
        s.zg_in = ZGather(net, w, s.in_piece, lambda z: s.w_in.at[:, z])

    def bring_ffo(layer):
        s = r.layer[layer]
        s.zg_in.poll()
        s.zg_ffo = ZGather(net, w, r.ffo_in.at[layer], lambda z: s.w_ffo.at[z])

    swaps = types.SimpleNamespace()
    for layer in range(layers):
        s = r.layer[layer]

        def started(layer=layer):
            if layer == 0:
                unpack()

        def ready(layer=layer, s=s):
            if layer == 0:
                s.in_parted()
                bring_in(0)
            s.zg_qkv.wait()
            s.zg_out.wait()

        def gathered(layer=layer):
            if layer + 1 < layers:
                n = r.layer[layer + 1]
                pack_qkv(layer + 1)
                pack_inner(layer + 1)
                n.qkv_parted = net.plane_swap(w, of_part(n.qkv_parts), of_part(n.qkv_piece))
                n.in_parted = net.plane_swap(w, of_part(n.in_parts), of_part(n.in_piece))

        def before(layer=layer):
            return r.hidden_row[...].astype(F32) if layer == 0 else r.state[...]

        attend_forward(
            net, w, r, s, before, started, ready, gathered, lambda layer=layer: bring_ffo(layer)
        )

        def ready_in(s=s):
            s.zg_in.wait()

        def ready_ffo(s=s):
            s.zg_ffo.wait()

        def pump(at, layer=layer, s=s):
            if at == 0:
                s.zg_ffo.poll()
                if layer + 1 < layers:
                    r.layer[layer + 1].qkv_parted()
                    r.layer[layer + 1].in_parted()
                    bring_attention(layer + 1)
            elif layer + 1 < layers:
                bring_in(layer + 1)
            else:
                swaps.grad = net.swap(w, r.out_grad, r.grad_row)

        state = feed_forward(net, w, r, s, ready_in, ready_ffo, pump)
        r.state[...] = state
        if layer + 1 < layers:
            r.layer[layer + 1].all_x[rows_of(w.slot, 128)] = state.astype(BF16)
        else:
            r.state_low[...] = state.astype(BF16)
    swaps.grad()
    net.settle()
    swaps.out = net.swap(w, r.state_low, r.out)
    grad = r.grad_row[...].astype(F32)

    def vectors_out(s):
        return net.z_spread(w, s.sums, s.sums_z)

    def vectors_plane(s, wait):
        wait()
        s.sums_own[...] = s.sums[...] + s.sums_z[0] + s.sums_z[1] + s.sums_z[2]
        return net.plane_swap(w, lambda p: s.sums_own, lambda p: s.sums_all.at[p])

    def vectors_in(layer, s, wait):
        wait()
        base = layer * FLAT_ROWS
        for row, name in ((G1, 72), (S1, 56), (BO, 8), (G2, 80), (S2, 64), (B2, 48)):
            total = s.sums_all[0, 8 * row : 8 * row + 8]
            for p in range(1, 8):
                total = total + s.sums_all[p, 8 * row : 8 * row + 8]
            r.vectors[base + name : base + name + 8, :] = total
        for p in range(8):
            r.vectors[base + p : base + p + 1, :] = s.sums_all[p, 48:49]
            r.vectors[base + 88 + p : base + 89 + p, :] = s.sums_all[p, 49:50]
            for z in range(4):
                at = base + 16 + 8 * (p // 2) + 2 * z + p % 2
                r.vectors[at : at + 1, :] = s.sums_all[p, 50 + z : 51 + z]

    def send_inner(s):
        s.in_parts[...] = s.z_in.total().astype(BF16).reshape(4, 2, 32, share)
        return net.plane_swap(w, of_part(s.in_parts), of_part(s.in_piece))

    def send_qkv(s):
        s.qkv_parts[...] = s.z_qkv.total().astype(BF16)
        return net.plane_swap(w, of_part(s.qkv_parts), of_part(s.qkv_piece))

    def place_inner(layer, s, wait):
        wait()
        for p in range(8):
            for z in range(4):
                at = ((p // 2) * 8 + z * 2 + p % 2) * unit
                r.in_grad[layer, :, at : at + unit] = s.in_piece[
                    p // 2, p % 2, :, z * unit : (z + 1) * unit
                ].astype(F32)

    def place_qkv(layer, s, wait):
        wait()
        for p in range(8):
            for k in range(3):
                lanes = slice(k * width + p * 128, k * width + (p + 1) * 128)
                r.qkv_grad[layer, :, lanes] = s.qkv_piece[
                    p // 2, p % 2, :, k * 128 : (k + 1) * 128
                ].astype(F32)

    for layer in reversed(range(layers)):
        s = r.layer[layer]
        a = r.layer[layer + 1] if layer + 1 < layers else None
        s.sums[...] = jnp.zeros_like(s.sums)

        def feed_started(layer=layer, a=a):
            if a is not None:
                r.ffo_grad[layer + 1] = a.z_ffo.total()
                a.in_wait = send_inner(a)

        def free(a=a):
            if a is not None:
                a.z_ffo.settle()
                a.z_in.settle()
                a.z_qkv.poll()
                a.z_out.poll()

        def feed_pump(a=a):
            if a is not None:
                a.vec_wait = vectors_plane(a, a.vec_wait)

        sums = feed_backward(net, w, r, s, grad, feed_started, free, feed_pump)
        if a is None:
            swaps.out()
        net.drain()

        def back_started(layer=layer, a=a, sums=sums):
            sums()
            if a is not None:
                place_inner(layer + 1, a, a.in_wait)
                r.out_grad_w[layer + 1] = a.z_out.total()
                a.qkv_wait = send_qkv(a)
                vectors_in(layer + 1, a, a.vec_wait)

        def back_pump(at, s=s):
            if at == 0:
                s.z_ffo.poll()
                s.vec_wait = vectors_out(s)
            else:
                s.z_in.poll()

        def done(grad, layer=layer):
            if layer:
                r.state[...] = grad
            else:
                r.state_low[...] = grad.astype(BF16)
                swaps.back = net.swap(w, r.state_low, r.input_grad)

        attend_backward(net, w, r, s, back_started, back_pump, done)
        if layer:
            grad = r.state[...]
            net.drain()
    r.ffo_grad[0] = first.z_ffo.total()
    first.in_wait = send_inner(first)
    if layers > 1:
        place_qkv(1, r.layer[1], r.layer[1].qkv_wait)
    first.vec_wait = vectors_plane(first, first.vec_wait)
    first.z_qkv.poll()
    first.z_out.poll()
    place_inner(0, first, first.in_wait)
    vectors_in(0, first, first.vec_wait)
    first.qkv_wait = send_qkv(first)
    r.out_grad_w[0] = first.z_out.total()
    swaps.back()
    unpack_vectors()
    place_qkv(0, first, first.qkv_wait)
    net.settle()


def plane_body(
    hidden_in,
    document_index,
    out_grad,
    qkv_weight,
    value_bias,
    attention_output_weight,
    ffn_in_weight,
    ffn_out_weight,
    biases,
    norm_gains,
):
    layers = qkv_weight.shape[0]
    width = hidden_in.shape[1]
    inner = ffn_in_weight.shape[2]
    share = inner // 8
    n_bias, n_gain, n_value = biases.shape[1], norm_gains.shape[1], value_bias.shape[1]

    ins = dict(
        hidden=hidden_in,
        docs=document_index,
        out_grad=out_grad,
        qkv_in=qkv_weight,
        out_in=attention_output_weight,
        inner_in=ffn_in_weight,
        ffo_in=ffn_out_weight,
        biases=biases,
        norm_gains=norm_gains,
        value_bias=value_bias,
    )
    outs = dict(
        out=((128, width), BF16),
        input_grad=((128, width), BF16),
        qkv_grad=(qkv_weight.shape, F32),
        out_grad_w=(attention_output_weight.shape, F32),
        in_grad=(ffn_in_weight.shape, F32),
        ffo_grad=(ffn_out_weight.shape, F32),
        bias_grad=((layers, n_bias), F32),
        gain_grad=((layers, n_gain), F32),
        value_grad=((layers, n_value), F32),
    )
    far = dict(hidden=1, out_grad=1, ffo_in=1, out_in=1, out=1, input_grad=1)
    whole = (1024, width)
    shared = dict(
        hidden_row=((128, width), BF16),
        grad_row=((128, width), BF16),
        docs_mine=((8, 128), F32),
        docs_own=((8, 128), F32),
        docs_all=((8, 8, 128), F32),
        docs_row=((8, 1024), F32),
        docs_col=((1024, 128), F32),
        vec_f=((16, 128), F32),
        vec_in=((16, 128), BF16),
        lined=((8, 384), F32),
        vectors=((layers * FLAT_ROWS, 128), F32),
        vec_z=((4, 16, 128), BF16),
        vec_all=((8, 4, 16, 128), BF16),
        flat=((layers * FLAT_ROWS, 128), F32),
        normed=((128, width), F32),
        state=((128, width), F32),
        state_low=((128, width), BF16),
        back_one=((128, width), F32),
        pre=((256, share), F32),
        all_second=(whole, BF16),
        all_branch=(whole, BF16),
        back_pre=((1024, share), BF16),
        back_context=((1024, 128), BF16),
        back_qkv=((1024, 384), BF16),
        sum_k=((1024, 128), F32),
        sum_v=((1024, 128), F32),
        g_out=((2, 2, 32, width), BF16),
        g_ffo=((4, 128, width), BF16),
        g_in=((4, 4, 64, share), BF16),
        core_out=((4, 128, width), BF16),
        core_in=((4, 128, width), BF16),
        keep=((4, 128, width), F32),
        across=((128, width), BF16),
        via_x=((64, width), BF16),
        via_y=((64, width), BF16),
        out_x=((128, width), BF16),
        out_y=((128, width), BF16),
        in_x=((128, width), BF16),
        in_y=((128, width), BF16),
    )
    each = dict(
        qkv_parts=((4, 2, 32, 384), BF16),
        qkv_piece=((4, 2, 32, 384), BF16),
        in_parts=((4, 2, 32, share), BF16),
        in_piece=((4, 2, 32, share), BF16),
        w_qkv=((4, 4, 2, 32, 384), BF16),
        w_in=((4, 4, 2, 32, share), BF16),
        w_ffo=((4, 128, width), BF16),
        out_z=((4, 32, width), BF16),
        w_out=((2, 2, 32, width), BF16),
        vec=((8, width), F32),
        part_bias=((8, width), F32),
        all_x=(whole, BF16),
        qkv=((1024, 384), BF16),
        context=((1024, 128), BF16),
        logs=((1024, 128), F32),
        all_n=(whole, BF16),
        inner=((1024, share), BF16),
        slope=((1024, share), BF16),
        hat_one=((128, width), F32),
        root_one=((128, 128), F32),
        hat_two=((128, width), F32),
        root_two=((128, 128), F32),
        g_qkv=((4, 4, 2, 32, 384), BF16),
        g_out_z=((4, 32, width), BF16),
        land_ffo=((4, 128, width), BF16),
        land_in=((4, 4, 64, share), BF16),
        land_qkv=((4, 4, 2, 32, 384), BF16),
        land_out=((4, 32, width), BF16),
        sums=((56, 128), F32),
        sums_z=((3, 56, 128), F32),
        sums_own=((56, 128), F32),
        sums_all=((8, 56, 128), F32),
    )

    def kernel(*refs):
        refs = list(refs)

        def take(names):
            return dict(zip(names, [refs.pop(0) for _ in names]))

        r = types.SimpleNamespace(
            width=width, share=share, n_bias=n_bias, n_gain=n_gain, n_value=n_value, **take(ins), **take(outs), **take(shared)
        )
        r.layer = [types.SimpleNamespace(**take(each)) for _ in range(layers)]
        r.ssem, r.rsem, r.lsem = refs
        whole_kernel(r)

    def held(items):
        return [VMEM(shape, dtype) for shape, dtype in items.values()]

    results = pl.pallas_call(
        kernel,
        out_shape=[jax.ShapeDtypeStruct(shape, dtype) for shape, dtype in outs.values()],
        in_specs=[pl.BlockSpec(memory_space=pl.ANY if name in far else VMEM) for name in ins],
        out_specs=[pl.BlockSpec(memory_space=pl.ANY if name in far else VMEM) for name in outs],
        scratch_shapes=[
            *held(shared),
            *(held(each) * layers),
            pltpu.SemaphoreType.DMA((COPIES,)),
            pltpu.SemaphoreType.DMA((COPIES,)),
            pltpu.SemaphoreType.DMA((48,)),
        ],
        compiler_params=pltpu.CompilerParams(
            collective_id=0, has_side_effects=True, vmem_limit_bytes=VMEM_LIMIT
        ),
    )(*ins.values())
    out, input_grad, g_qkv, g_out, g_in, g_ffo, g_bias, g_gain, g_value = results
    return (out, input_grad.astype(F32), g_qkv, g_value, g_out, g_in, g_ffo, g_bias, g_gain)


def fits_plane(mesh):
    return mesh.shape[DP] == 4 and mesh.shape[CTX] == 8


def solution(mesh):
    return jax.shard_map(
        plane_body if fits_plane(mesh) else body,
        mesh=mesh,
        in_specs=(
            P(BOTH, None),
            P(DP, CTX),
            P(BOTH, None),
            P(None, BOTH, None),
            P(None, BOTH),
            P(None, BOTH, None),
            P(None, BOTH, None),
            P(None, BOTH, None),
            P(None, BOTH),
            P(None, BOTH),
        ),
        out_specs=(
            P(BOTH, None),
            P(BOTH, None),
            P(None, BOTH, None),
            P(None, BOTH),
            P(None, BOTH, None),
            P(None, BOTH, None),
            P(None, BOTH, None),
            P(None, BOTH),
            P(None, BOTH),
        ),
        check_vma=False,
    )
```

```python
import math
import types

import jax
import jax.numpy as jnp
from jax import lax
from jax.experimental import pallas as pl
from jax.experimental.pallas import tpu as pltpu
from jax.sharding import PartitionSpec as P

ATTENTION_HEADS = 16


DP, CTX = "dp", "ctx"
BOTH = (DP, CTX)

QUERY_KEY, TO_QUERY, TO_KEY = "qhd,khd->hqk", "hqk,khd->qhd", "hqk,qhd->khd"
EPS = 1e-12
NEGATIVE = -1e30


def norm_rows(resid, gain, shift):
    mean = jnp.mean(resid, axis=-1, keepdims=True)
    centered = resid - mean
    variance = jnp.mean(centered * centered, axis=-1, keepdims=True)
    return centered * lax.rsqrt(variance + EPS) * gain + shift


def exact_gelu(value):
    return jax.nn.gelu(value, approximate=False)


def cross(left, right_operand):
    return lax.dot_general(
        left, right_operand, (((0,), (0,)), ((), ())), preferred_element_type=jnp.float32
    )


def back_product(upstream, weight):
    return lax.dot_general(
        upstream, weight, (((1,), (1,)), ((), ())), preferred_element_type=jnp.float32
    )


def by_blocks(step_fn, carry, pieces, token_block):
    count = pieces[0].shape[0]

    def turn(index, state):
        offset = index * token_block
        parts = tuple((lax.dynamic_slice_in_dim(item, offset, token_block, 0) for item in pieces))
        return step_fn(state, parts, offset)

    return lax.fori_loop(0, count // token_block, turn, carry)


def unpack(fetched, width, inner):
    w_qkv, w_out, w_in, w_ffo, value_vec, bias_all, gains = fetched
    value_vec = value_vec.astype(jnp.float32)
    bias_all = bias_all.astype(jnp.float32)
    gains = gains.astype(jnp.float32)
    query_bias = bias_all[0:width]
    out_bias = bias_all[width : 2 * width]
    inner_bias = bias_all[2 * width : 2 * width + inner]
    ffn_bias = bias_all[2 * width + inner : 3 * width + inner]
    shift_one = bias_all[3 * width + inner : 4 * width + inner]
    shift_two = bias_all[4 * width + inner : 5 * width + inner]
    return (
        w_qkv,
        w_out,
        w_in,
        w_ffo,
        value_vec,
        query_bias,
        out_bias,
        inner_bias,
        ffn_bias,
        shift_one,
        shift_two,
        gains[0:width],
        gains[width : 2 * width],
    )


def masked_scores(query_heads, key_piece, seg_own, segment_row, start, scale):
    count = key_piece.shape[0]
    heads = query_heads.shape[1]
    split_key_heads = key_piece.reshape(count, heads, query_heads.shape[2])
    seg_keys = lax.dynamic_slice_in_dim(segment_row, start, count, 0)
    mask = (seg_own[:, None] == seg_keys[None, :])[None]
    raw = (
        jnp.einsum(QUERY_KEY, query_heads, split_key_heads, preferred_element_type=jnp.float32)
        * scale
    )
    return (jnp.where(mask, raw, NEGATIVE), mask, split_key_heads)


def body(
    hidden_in,
    document_index,
    out_grad,
    qkv_weight,
    value_bias,
    attention_output_weight,
    ffn_in_weight,
    ffn_out_weight,
    biases,
    norm_gains,
):
    layers = qkv_weight.shape[0]
    width = qkv_weight.shape[2] // 3
    inner = ffn_in_weight.shape[2]
    heads = ATTENTION_HEADS
    head_width = width // heads
    scale = head_width ** (-0.5)
    rows = hidden_in.shape[0]
    seg_own = document_index[0]
    segment_row = lax.all_gather(document_index, CTX, axis=1, tiled=True)[0]
    row_len = segment_row.shape[0]
    state = hidden_in.astype(jnp.float32)
    saved = []
    for layer in range(layers):
        fetched = (
            lax.all_gather(qkv_weight[layer], BOTH, axis=0, tiled=True),
            lax.all_gather(attention_output_weight[layer], BOTH, axis=0, tiled=True),
            lax.all_gather(ffn_in_weight[layer], BOTH, axis=0, tiled=True),
            lax.all_gather(ffn_out_weight[layer], BOTH, axis=0, tiled=True),
            lax.all_gather(value_bias[layer], BOTH, axis=0, tiled=True),
            lax.all_gather(biases[layer], BOTH, axis=0, tiled=True),
            lax.all_gather(norm_gains[layer], BOTH, axis=0, tiled=True),
        )
        (
            w_qkv,
            w_out,
            w_in,
            w_ffo,
            value_vec,
            query_bias,
            out_bias,
            inner_bias,
            ffn_bias,
            shift_one,
            shift_two,
            gain_one,
            gain_two,
        ) = unpack(fetched, width, inner)
        state_low = state.astype(jnp.bfloat16)
        qkv_bias = jnp.concatenate([query_bias, jnp.zeros_like(query_bias), value_vec])
        qkv_low = (jnp.dot(state_low, w_qkv, preferred_element_type=jnp.float32) + qkv_bias).astype(
            jnp.bfloat16
        )
        query_heads = qkv_low[:, 0:width].reshape(rows, heads, head_width)
        key_low = qkv_low[:, width : 2 * width]
        value_low = qkv_low[:, 2 * width : 3 * width]

        def stats_step(carry, parts, start):
            top, total = carry
            raw, mask, split_key_heads = masked_scores(
                query_heads, parts[0], seg_own, segment_row, start, scale
            )
            new_top = jnp.maximum(top, jnp.max(raw, axis=-1))
            weights = jnp.where(mask, jnp.exp(raw - new_top[:, :, None]), 0.0)
            return (new_top, total * jnp.exp(top - new_top) + jnp.sum(weights, axis=-1))

        stats_init = (
            jnp.full((heads, rows), NEGATIVE, jnp.float32),
            jnp.zeros((heads, rows), jnp.float32),
        )
        held_pair = None
        top, total = by_blocks(
            stats_step, stats_init, (lax.all_gather(key_low, CTX, axis=0, tiled=True),), rows
        )
        log_total = top + jnp.log(total)

        def value_step(carry, parts, start):
            context_acc, exact_acc = carry
            raw, mask, split_key_heads = masked_scores(
                query_heads, parts[0], seg_own, segment_row, start, scale
            )
            split_value_heads = parts[1].reshape(parts[1].shape[0], heads, head_width)
            probs = jnp.where(mask, jnp.exp(raw - log_total[:, :, None]), 0.0)
            probs_low = probs.astype(jnp.bfloat16)
            residue_low = (probs - probs_low.astype(jnp.float32)).astype(jnp.bfloat16)
            part_low = jnp.einsum(
                TO_QUERY, probs_low, split_value_heads, preferred_element_type=jnp.float32
            )
            part_fix = jnp.einsum(
                TO_QUERY, residue_low, split_value_heads, preferred_element_type=jnp.float32
            )
            return (context_acc + part_low, exact_acc + part_fix)

        value_init = (
            jnp.zeros((rows, heads, head_width), jnp.float32),
            jnp.zeros((rows, heads, head_width), jnp.float32),
        )
        context, correction = by_blocks(
            value_step,
            value_init,
            (
                lax.all_gather(key_low, CTX, axis=0, tiled=True),
                lax.all_gather(value_low, CTX, axis=0, tiled=True),
            ),
            rows,
        )
        context_exact = (context + correction).reshape(rows, width)
        context = context.reshape(rows, width)
        context_low = context.astype(jnp.bfloat16)
        resid_one = (
            state + jnp.dot(context_low, w_out, preferred_element_type=jnp.float32) + out_bias
        )
        normed = norm_rows(resid_one, gain_one, shift_one)
        normed_low = normed.astype(jnp.bfloat16)
        pre = jnp.dot(normed_low, w_in, preferred_element_type=jnp.float32) + inner_bias
        inner_low = exact_gelu(pre).astype(jnp.bfloat16)
        resid_two = (
            normed + jnp.dot(inner_low, w_ffo, preferred_element_type=jnp.float32) + ffn_bias
        )
        saved.append(
            (
                fetched,
                state_low,
                qkv_low,
                log_total,
                context_exact,
                context_low,
                resid_one,
                normed_low,
                pre,
                inner_low,
                resid_two,
                held_pair,
            )
        )
        state = norm_rows(resid_two, gain_two, shift_two)
    upstream = out_grad.astype(jnp.float32)
    per_layer = []
    for layer in reversed(range(layers)):
        (
            fetched,
            state_low,
            qkv_low,
            log_total,
            context_exact,
            context_low,
            resid_one,
            normed_low,
            pre,
            inner_low,
            resid_two,
            held_pair,
        ) = saved[layer]
        weights_now = (
            lax.all_gather(qkv_weight[layer], BOTH, axis=0, tiled=True),
            lax.all_gather(attention_output_weight[layer], BOTH, axis=0, tiled=True),
            lax.all_gather(ffn_in_weight[layer], BOTH, axis=0, tiled=True),
            lax.all_gather(ffn_out_weight[layer], BOTH, axis=0, tiled=True),
            lax.all_gather(value_bias[layer], BOTH, axis=0, tiled=True),
            lax.all_gather(biases[layer], BOTH, axis=0, tiled=True),
            lax.all_gather(norm_gains[layer], BOTH, axis=0, tiled=True),
        )
        (
            w_qkv,
            w_out,
            w_in,
            w_ffo,
            value_vec,
            query_bias,
            out_bias,
            inner_bias,
            ffn_bias,
            shift_one,
            shift_two,
            gain_one,
            gain_two,
        ) = unpack(weights_now, width, inner)
        query_low = qkv_low[:, 0:width]
        query_heads = query_low.reshape(rows, heads, head_width)
        key_low = qkv_low[:, width : 2 * width]
        value_low = qkv_low[:, 2 * width : 3 * width]
        unused_two, pull_two = jax.vjp(norm_rows, resid_two, gain_two, shift_two)
        back_two, back_gain_two, back_shift_two = pull_two(upstream)
        back_second = back_two.astype(jnp.bfloat16)
        grad_second = cross(inner_low, back_second)
        back_inner = back_product(back_second, w_ffo)
        unused_pre, pull_gelu = jax.vjp(exact_gelu, pre)
        back_pre = pull_gelu(back_inner)[0].astype(jnp.bfloat16)
        grad_first = cross(normed_low, back_pre)
        back_normed = back_two + back_product(back_pre, w_in)
        normed_again, pull_one = jax.vjp(norm_rows, resid_one, gain_one, shift_one)
        back_one, back_gain_one, back_shift_one = pull_one(back_normed)
        back_branch = back_one.astype(jnp.bfloat16)
        grad_out_proj = cross(context_low, back_branch)
        back_context = back_product(back_branch, w_out).astype(jnp.bfloat16)
        context_heads_back = back_context.reshape(rows, heads, head_width)
        delta = jnp.sum(
            (back_context.astype(jnp.float32) * context_exact).reshape(rows, heads, head_width),
            axis=-1,
        ).T

        def grad_step(carry, parts, start):
            query_sum, key_sums, value_sums = carry
            count = parts[0].shape[0]
            raw, mask, split_key_heads = masked_scores(
                query_heads, parts[0], seg_own, segment_row, start, scale
            )
            split_value_heads = parts[1].reshape(count, heads, head_width)
            probs = jnp.where(mask, jnp.exp(raw - log_total[:, :, None]), 0.0)
            back_probs = jnp.einsum(
                QUERY_KEY,
                context_heads_back,
                split_value_heads,
                preferred_element_type=jnp.float32,
            )
            back_scores = (probs * (back_probs - delta[:, :, None])).astype(jnp.bfloat16)
            query_part = (
                jnp.einsum(
                    TO_QUERY, back_scores, split_key_heads, preferred_element_type=jnp.float32
                )
                * scale
            )
            key_part = (
                jnp.einsum(
                    TO_KEY, back_scores, query_heads, preferred_element_type=jnp.float32
                ).reshape(count, width)
                * scale
            )
            value_part = jnp.einsum(
                TO_KEY,
                probs.astype(jnp.bfloat16),
                context_heads_back,
                preferred_element_type=jnp.float32,
            ).reshape(count, width)
            key_sums = lax.dynamic_update_slice_in_dim(
                key_sums, lax.dynamic_slice_in_dim(key_sums, start, count, 0) + key_part, start, 0
            )
            value_sums = lax.dynamic_update_slice_in_dim(
                value_sums,
                lax.dynamic_slice_in_dim(value_sums, start, count, 0) + value_part,
                start,
                0,
            )
            return (query_sum + query_part, key_sums, value_sums)

        query_init = jnp.zeros((rows, heads, head_width), jnp.float32)
        grad_init = (
            query_init,
            jnp.zeros((row_len, width), jnp.float32),
            jnp.zeros((row_len, width), jnp.float32),
        )
        folded = by_blocks(
            grad_step,
            grad_init,
            (
                lax.all_gather(key_low, CTX, axis=0, tiled=True),
                lax.all_gather(value_low, CTX, axis=0, tiled=True),
            ),
            rows,
        )
        query_sum, key_sums, value_sums = folded
        key_own, value_own = (
            lax.psum_scatter(
                key_sums.astype(jnp.bfloat16), CTX, scatter_dimension=0, tiled=True
            ).astype(jnp.float32),
            lax.psum_scatter(
                value_sums.astype(jnp.bfloat16), CTX, scatter_dimension=0, tiled=True
            ).astype(jnp.float32),
        )
        back_qkv = jnp.concatenate(
            [query_sum.reshape(rows, width), key_own, value_own], axis=1
        ).astype(jnp.bfloat16)
        grad_qkv = cross(state_low, back_qkv)
        back_qkv_float = back_qkv.astype(jnp.float32)
        grad_value_bias = jnp.sum(back_qkv_float[:, 2 * width : 3 * width], axis=0)
        grad_bias = jnp.concatenate(
            [
                jnp.sum(back_qkv_float[:, 0:width], axis=0),
                jnp.sum(back_branch.astype(jnp.float32), axis=0),
                jnp.sum(back_pre.astype(jnp.float32), axis=0),
                jnp.sum(back_second.astype(jnp.float32), axis=0),
                back_shift_one,
                back_shift_two,
            ]
        )
        grad_gain = jnp.concatenate([back_gain_one, back_gain_two])
        upstream = back_one + back_product(back_qkv, w_qkv)
        shards = (
            lax.psum_scatter(grad_qkv, BOTH, scatter_dimension=0, tiled=True),
            lax.psum_scatter(grad_value_bias, BOTH, scatter_dimension=0, tiled=True),
            lax.psum_scatter(grad_out_proj, BOTH, scatter_dimension=0, tiled=True),
            lax.psum_scatter(grad_first, BOTH, scatter_dimension=0, tiled=True),
            lax.psum_scatter(grad_second, BOTH, scatter_dimension=0, tiled=True),
            lax.psum_scatter(grad_bias, BOTH, scatter_dimension=0, tiled=True),
            lax.psum_scatter(grad_gain, BOTH, scatter_dimension=0, tiled=True),
        )
        per_layer.append(shards)
    ordered = per_layer[::-1]
    stacked = tuple((jnp.stack([item[member] for item in ordered]) for member in range(7)))
    return (
        state.astype(jnp.bfloat16),
        upstream,
        stacked[0],
        stacked[1],
        stacked[2],
        stacked[3],
        stacked[4],
        stacked[5],
        stacked[6],
    )


MESH = pl.DeviceIdType.MESH
F32 = jnp.float32
BF16 = jnp.bfloat16
VMEM = pltpu.VMEM
VMEM_LIMIT = 62 * 2**20
PHASE, COPIES = 32, 208
OWN, XN, YN, DIAG = range(4)
G1, S1, BO, G2, S2, B2 = range(6)


def dot_nn(a, b):
    return lax.dot_general(a, b, (((1,), (0,)), ((), ())), preferred_element_type=F32)


def dot_nt(a, b):
    return lax.dot_general(a, b, (((1,), (1,)), ((), ())), preferred_element_type=F32)


def dot_tn(a, b):
    return lax.dot_general(a, b, (((0,), (0,)), ((), ())), preferred_element_type=F32)


def turned(two_bits):
    return lax.rem(two_bits, 2) * 2 + lax.div(two_bits, 2)


def place():
    d, t = lax.axis_index(DP), lax.axis_index(CTX)
    x, c = lax.div(d, 2), lax.rem(d, 2)
    z, y = lax.div(t, 2), lax.rem(t, 2)
    w = types.SimpleNamespace(d=d, x=x, c=c, z=z, y=y)
    w.part = d * 2 + y
    w.group = (x * 2 + y, (1 - x) * 2 + y, x * 2 + 1 - y, (1 - x) * 2 + 1 - y)
    w.slot = w.group[OWN] * 2 + c
    w.xn, w.yn, w.sib = ((1 - x) * 2 + c, t), (d, z * 2 + 1 - y), (x * 2 + 1 - c, t)
    w.plane = []
    for bits in range(1, 8):
        xx = 1 - x if bits & 4 else x
        cc = 1 - c if bits & 2 else c
        yy = 1 - y if bits & 1 else y
        w.plane.append(((xx * 2 + cc, z * 2 + yy), (xx * 2 + cc) * 2 + yy))
    w.zs = [(d, lax.rem(z + k, 4) * 2 + y) for k in (1, 2, 3)]
    w.far = lax.rem(z + 2, 4)
    w.up, w.down, w.over = (d, (z + 1) * 2 + y), (d, (z - 1) * 2 + y), (d, w.far * 2 + y)
    w.middle = (z == 1) | (z == 2)
    w.edge = (z == 0) | (z == 3)
    w.end = jnp.where(z == 1, 0, 3)
    w.near_end = (d, w.end * 2 + y)
    w.inside = jnp.where(z == 0, 1, 2)
    w.near_middle = (d, w.inside * 2 + y)
    w.opposite = 3 - z
    w.away = d != turned(z)
    w.home = d == turned(z)
    w.swap = (turned(z), turned(d) * 2 + y)
    return w


class Maybe:
    def __init__(self, copy, sends, receives):
        self.copy, self.sends, self.receives = copy, sends, receives

    def start(self):
        pl.when(self.sends)(self.copy.start)

    def wait_send(self):
        pl.when(self.sends)(self.copy.wait_send)

    def wait_recv(self):
        pl.when(self.receives)(self.copy.wait_recv)


class Net:
    def __init__(self, ssem, rsem, lsem):
        self.ssem, self.rsem, self.lsem = ssem, rsem, lsem
        self.sent, self.slow, self.scatters, self.at, self.near = [], [], [], PHASE, 0
        self.phase = 0

    def greet(self, w):
        barrier = pltpu.get_barrier_semaphore()
        devices = [device for device, _ in w.plane] + w.zs
        for device in devices:
            pl.semaphore_signal(barrier, inc=1, device_id=device, device_id_type=MESH)

        @pl.when(w.away)
        def _():
            pl.semaphore_signal(barrier, inc=1, device_id=w.swap, device_id_type=MESH)

        return lambda: pl.semaphore_wait(barrier, len(devices) + jnp.where(w.away, 1, 0))

    def make(self, src, dst, device, slow=True):
        at = self.at if slow else self.phase
        if slow:
            self.at += 1
        else:
            self.phase += 1
        return pltpu.make_async_remote_copy(
            src_ref=src,
            dst_ref=dst,
            send_sem=self.ssem.at[at],
            recv_sem=self.rsem.at[at],
            device_id=device,
            device_id_type=MESH,
        )

    def maybe(self, src, dst, device, sends, receives):
        copy = Maybe(self.make(src, dst, device), sends, receives)
        self.slow.append(copy)
        return copy

    def send(self, src, dst, device, slow=False):
        copy = self.make(src, dst, device, slow)
        copy.start()
        (self.slow if slow else self.sent).append(copy)
        return copy

    def local(self, src, dst):
        copy = pltpu.make_async_copy(src, dst, self.lsem.at[self.near])
        self.near += 1
        return copy

    def swap(self, w, src, dst):
        far = Maybe(self.make(src, dst, w.swap), w.away, w.away)
        near = self.local(src, dst)
        far.start()
        pl.when(w.home)(near.start)

        def wait():
            far.wait_recv()
            far.wait_send()
            pl.when(w.home)(near.wait)

        return wait

    def plane_swap(self, w, at, to):
        copies = [self.send(at(part), to(w.part), device, True) for device, part in w.plane]
        own = self.local(at(w.part), to(w.part))
        own.start()

        def wait():
            own.wait()
            for copy in copies:
                copy.wait_recv()

        return wait

    def z_all(self, w, src, at):
        copies = [self.send(src, at(w.z), device, True) for device in w.zs]
        own = self.local(src, at(w.z))
        own.start()

        def wait():
            own.wait()
            for copy in copies:
                copy.wait_recv()

        return wait

    def z_spread(self, w, src, land):
        copies = [self.send(src, land.at[k], device, True) for k, device in enumerate(w.zs)]

        def wait():
            for copy in copies:
                copy.wait_recv()

        return wait

    def drain(self):
        for copy in self.sent:
            copy.wait_send()
        self.sent, self.phase = [], 0

    def settle(self):
        self.drain()
        for copy in self.slow:
            copy.wait_send()
        self.slow = []
        for scatter in self.scatters:
            scatter.settle()


class ZGather:
    def __init__(self, net, w, src, at):
        self.w, here = w, at(w.z)
        self.over = net.send(src, here, w.over, True)
        self.up = net.maybe(src, here, w.up, w.z < 3, w.z > 0)
        self.down = net.maybe(src, here, w.down, w.z > 0, w.z < 3)
        far = at(w.far)
        self.on = net.maybe(far, far, w.near_end, w.middle, w.edge)
        self.own = net.local(src, here)
        self.up.start()
        self.down.start()
        self.own.start()

    def poll(self):
        pl.when(self.w.middle)(self.over.wait_recv)
        self.on.start()

    def wait(self):
        pl.when(self.w.edge)(self.over.wait_recv)
        self.own.wait()
        for copy in (self.up, self.down, self.on):
            copy.wait_recv()


class ZScatter:
    def __init__(self, net, w, at, land):
        self.w, self.at, self.land = w, at, land
        self.on = net.maybe(at(w.opposite), land.at[3], w.near_middle, w.edge, w.middle)
        self.on.start()
        self.up = net.maybe(at(lax.rem(w.z + 1, 4)), land.at[0], w.up, w.z < 3, w.z > 0)
        self.down = net.maybe(at(lax.rem(w.z + 3, 4)), land.at[1], w.down, w.z > 0, w.z < 3)
        self.end_over = net.maybe(at(w.far), land.at[2], w.over, w.edge, w.middle)
        self.mid_over = net.maybe(land.at[3], land.at[2], w.over, w.middle, w.edge)
        self.sends = (self.on, self.up, self.down, self.end_over, self.mid_over)
        net.slow = [copy for copy in net.slow if copy not in self.sends]
        net.scatters.append(self)
        for copy in (self.end_over, self.up, self.down):
            copy.start()

        @pl.when(w.z == 0)
        def _():
            land[0] = jnp.zeros(land.shape[1:], BF16)

        @pl.when(w.z == 3)
        def _():
            land[1] = jnp.zeros(land.shape[1:], BF16)

    def poll(self):
        @pl.when(self.w.middle)
        def _():
            self.on.copy.wait_recv()
            own = self.at(self.w.far)[...].astype(F32)
            self.land[3] = (self.land[3].astype(F32) + own).astype(BF16)

        self.mid_over.start()

    def settle(self):
        for copy in self.sends:
            copy.wait_send()
        self.sends = ()

    def total(self):
        for copy in (self.up, self.down, self.end_over, self.mid_over):
            copy.wait_recv()
        land = self.land
        return (
            self.at(self.w.z)[...].astype(F32)
            + land[0].astype(F32)
            + land[1].astype(F32)
            + land[2].astype(F32)
        )


def nothing():
    pass


def gather(net, w, buf, on_group, after_start=nothing, after_forward=None):
    def half(group, h):
        return buf.at[pl.ds(pl.multiple_of((group * 2 + w.c) * 128 + h * 64, 64), 64)]

    def put(group, h, device):
        ref = half(group, h)
        return net.send(ref, ref, device)

    own, xn, yn, diag = w.group
    x0 = put(own, 0, w.xn)
    y1 = put(own, 1, w.yn)
    whole = buf.at[rows_of(w.slot, 128)]
    c0 = net.send(whole, whole, w.sib)
    x1 = put(own, 1, w.xn)
    y0 = put(own, 0, w.yn)
    after_start()
    if after_forward is None:
        c0.wait_recv()
        on_group(OWN)
    x0.wait_recv()
    d0 = put(xn, 0, w.yn)
    cx0 = put(xn, 0, w.sib)
    y1.wait_recv()
    d1 = put(yn, 1, w.xn)
    cy1 = put(yn, 1, w.sib)
    x1.wait_recv()
    cx1 = put(xn, 1, w.sib)
    y0.wait_recv()
    cy0 = put(yn, 0, w.sib)
    if after_forward is not None:
        after_forward()
        c0.wait_recv()
        on_group(OWN)
    cx0.wait_recv()
    cx1.wait_recv()
    on_group(XN)
    cy0.wait_recv()
    cy1.wait_recv()
    on_group(YN)
    d0.wait_recv()
    cd0 = put(diag, 0, w.sib)
    d1.wait_recv()
    cd1 = put(diag, 1, w.sib)
    cd0.wait_recv()
    cd1.wait_recv()
    on_group(DIAG)


class Reduce:
    def __init__(self, net, w, r, part):
        self.net, self.w, self.r, self.part = net, w, r, part
        self.cores = [None] * 4

    def produce(self, kind):
        w, r = self.w, self.r
        group = w.group[kind]
        r.core_out[kind] = self.part(group * 2 + 1 - w.c).astype(BF16)
        self.cores[kind] = self.net.send(r.core_out.at[kind], r.core_in.at[kind], w.sib)
        r.keep[kind] = self.part(group * 2 + w.c)

    def both(self, kind, rows):
        return self.r.keep[kind, rows] + self.r.core_in[kind, rows].astype(F32)

    def diag(self):
        w, r = self.w, self.r
        self.cores[DIAG].wait_recv()
        r.across[...] = self.both(DIAG, slice(0, 128)).astype(BF16)
        self.fy = self.net.send(r.across.at[pl.ds(0, 64)], r.via_y, w.yn)
        self.fx = self.net.send(r.across.at[pl.ds(64, 64)], r.via_x, w.xn)

    def first(self):
        w, r = self.w, self.r
        self.cores[XN].wait_recv()
        r.out_x[64:128] = self.both(XN, slice(64, 128)).astype(BF16)
        self.x1 = self.net.send(r.out_x.at[pl.ds(64, 64)], r.in_x.at[pl.ds(64, 64)], w.xn)
        self.cores[YN].wait_recv()
        r.out_y[0:64] = self.both(YN, slice(0, 64)).astype(BF16)
        self.y0 = self.net.send(r.out_y.at[pl.ds(0, 64)], r.in_y.at[pl.ds(0, 64)], w.yn)

    def second(self):
        w, r = self.w, self.r
        self.fy.wait_recv()
        r.out_x[0:64] = (self.both(XN, slice(0, 64)) + r.via_y[...].astype(F32)).astype(BF16)
        self.x0 = self.net.send(r.out_x.at[pl.ds(0, 64)], r.in_x.at[pl.ds(0, 64)], w.xn)
        self.fx.wait_recv()
        r.out_y[64:128] = (self.both(YN, slice(64, 128)) + r.via_x[...].astype(F32)).astype(BF16)
        self.y1 = self.net.send(r.out_y.at[pl.ds(64, 64)], r.in_y.at[pl.ds(64, 64)], w.yn)

    def total(self):
        r = self.r
        self.cores[OWN].wait_recv()
        for copy in (self.x1, self.y0, self.x0, self.y1):
            copy.wait_recv()
        return self.both(OWN, slice(0, 128)) + r.in_x[...].astype(F32) + r.in_y[...].astype(F32)


def rows_of(group, n=256):
    return pl.ds(pl.multiple_of(group * n, n), n)


def norm_parts(resid):
    mean = jnp.mean(resid, axis=-1, keepdims=True)
    centered = resid - mean
    variance = jnp.mean(centered * centered, axis=-1, keepdims=True)
    root = lax.rsqrt(variance + EPS)
    return centered * root, root


def norm_back(grad, hat, root, gain):
    scaled = grad * gain
    return root * (
        scaled
        - jnp.mean(scaled, axis=-1, keepdims=True)
        - hat * jnp.mean(scaled * hat, axis=-1, keepdims=True)
    )


def column_sum(value):
    return jnp.sum(value, axis=0, keepdims=True)


def by_head(value):
    lanes = lax.broadcasted_iota(jnp.int32, value.shape, 1)
    zero = jnp.zeros_like(value)
    return jnp.concatenate([jnp.where(lanes < 64, value, zero), jnp.where(lanes >= 64, value, zero)], axis=0)


def own_lanes(first, second):
    lanes = lax.broadcasted_iota(jnp.int32, first.shape, 1)
    return jnp.where(lanes < 64, first, second)


def attend_forward(net, w, r, s, before, started, handed, ready, gathered, pump):
    width = r.width
    scale = jnp.asarray((width // ATTENTION_HEADS) ** (-0.5), BF16)
    cross = types.SimpleNamespace()

    gather(net, w, s.all_x, lambda kind: None, started, handed)
    ready()

    def project(i, carry):
        rows = rows_of(i)
        weights = s.w_qkv[...].reshape(width, 384)
        s.qkv[rows] = (dot_nn(s.all_x[rows], weights) + s.part_bias[0:1, 0:384]).astype(BF16)
        return carry

    lax.fori_loop(0, 4, project, 0)
    cross.out = net.send(s.out_z.at[pl.ds(2 * (1 - w.y), 2)], s.w_out.at[:, w.y], w.yn)
    cross.own = net.local(s.out_z.at[pl.ds(2 * w.y, 2)], s.w_out.at[:, w.y])
    cross.own.start()
    def attend(kind, begin=0, end=2):
        def block(i, carry):
            rows = pl.ds(pl.multiple_of(w.group[kind] * 256 + i * 128, 128), 128)
            both = by_head(s.qkv[rows, 0:128] * scale)
            mask = r.docs_col[rows, 0:1] == r.docs_row[0:1, :]
            raw_both = dot_nt(both, s.qkv[:, 128:256])
            probs, logs = [], []
            for h in range(2):
                raw = jnp.where(mask, raw_both[h * 128 : (h + 1) * 128], NEGATIVE)
                top = jnp.max(raw, axis=-1, keepdims=True)
                weight = jnp.exp(raw - top)
                mass = jnp.sum(weight, axis=-1, keepdims=True)
                probs.append((weight * (1.0 / mass)).astype(BF16))
                logs.append(top + jnp.log(mass))
            total = dot_nn(jnp.concatenate(probs, axis=0), s.qkv[:, 256:384])
            s.context[rows] = own_lanes(total[0:128], total[128:256]).astype(BF16)
            s.logs[rows] = own_lanes(
                jnp.broadcast_to(logs[0], (128, 128)), jnp.broadcast_to(logs[1], (128, 128))
            )
            return carry

        lax.fori_loop(begin, end, block, 0)

    def part(slot):
        return dot_nn(s.context[rows_of(slot, 128)], s.w_out[...].reshape(128, width))

    reduce = Reduce(net, w, r, part)
    attend(DIAG)
    cross.out.wait_recv()
    cross.own.wait()
    reduce.produce(DIAG)
    attend(XN, 0, 1)
    reduce.diag()
    attend(XN, 1, 2)
    reduce.produce(XN)
    attend(YN)
    reduce.produce(YN)
    reduce.first()
    gathered()
    pump()
    attend(OWN)
    reduce.produce(OWN)
    reduce.second()
    hat, root = norm_parts(before() + reduce.total() + s.vec[BO : BO + 1])
    normed = hat * s.vec[G1 : G1 + 1] + s.vec[S1 : S1 + 1]
    r.normed[...] = normed
    s.all_n[rows_of(w.slot, 128)] = normed.astype(BF16)
    s.hat_one[...] = hat
    s.root_one[...] = jnp.broadcast_to(root, (128, 128))
    net.drain()


def feed_forward(net, w, r, s, ready_in, ready_ffo, pump):
    def part(slot):
        return dot_nn(s.inner[rows_of(slot, 128)], s.w_ffo[...].reshape(r.share, r.width))

    reduce = Reduce(net, w, r, part)

    def on_group(kind):
        weights = s.w_in[...].reshape(r.width, r.share)
        r.pre[...] = dot_nn(s.all_n[rows_of(w.group[kind])], weights) + s.part_bias[1:2, 0 : r.share]

        def block(i, carry):
            here = pl.ds(pl.multiple_of(i * 32, 32), 32)
            there = pl.ds(pl.multiple_of(w.group[kind] * 256 + i * 32, 32), 32)
            pre = r.pre[here]
            cdf = 0.5 * (1.0 + lax.erf(pre * (0.5**0.5)))
            s.inner[there] = (pre * cdf).astype(BF16)
            bell = jnp.exp(pre * pre * (-0.5)) * ((2.0 * math.pi) ** (-0.5))
            s.slope[there] = (cdf + pre * bell).astype(BF16)
            return carry

        lax.fori_loop(0, 8, block, 0)
        if kind == YN:
            ready_ffo()
            reduce.produce(XN)
            reduce.produce(YN)
            reduce.first()

    gather(net, w, s.all_n, on_group, lambda: pump(0), ready_in)
    reduce.produce(DIAG)
    reduce.diag()
    reduce.produce(OWN)
    reduce.second()
    pump(1)
    hat, root = norm_parts(r.normed[...] + reduce.total() + s.vec[B2 : B2 + 1])
    s.hat_two[...] = hat
    s.root_two[...] = jnp.broadcast_to(root, (128, 128))
    net.drain()
    return hat * s.vec[G2 : G2 + 1] + s.vec[S2 : S2 + 1]


def put_row(ref, row, value):
    for k in range(value.shape[1] // 128):
        ref[row + k : row + k + 1, :] = value[:, k * 128 : (k + 1) * 128]


def feed_backward(net, w, r, s, grad, started, free, pump):
    hat = s.hat_two[...]
    back_two = norm_back(grad, hat, s.root_two[:, 0:1], s.vec[G2 : G2 + 1])
    second = back_two.astype(BF16)
    r.normed[...] = back_two
    r.all_second[rows_of(w.slot, 128)] = second

    def part(slot):
        return dot_nt(r.back_pre[rows_of(slot, 128)], s.w_in[...].reshape(r.width, r.share))

    reduce = Reduce(net, w, r, part)

    def after_start():
        put_row(s.sums, 8 * G2, column_sum(grad * hat))
        put_row(s.sums, 8 * S2, column_sum(grad))
        put_row(s.sums, 8 * B2, column_sum(second.astype(F32)))
        started()

    def on_group(kind):
        rows = rows_of(w.group[kind])
        back_inner = dot_nt(r.all_second[rows], s.w_ffo[...].reshape(r.share, r.width))
        r.back_pre[rows] = (back_inner * s.slope[rows].astype(F32)).astype(BF16)
        if kind == YN:
            reduce.produce(XN)
            reduce.produce(YN)
            reduce.first()

    gather(net, w, r.all_second, on_group, after_start)
    reduce.produce(DIAG)
    reduce.diag()
    reduce.produce(OWN)
    free()

    for z in range(4):
        r.g_ffo[z] = dot_tn(s.inner[:, z * 128 : (z + 1) * 128], r.all_second[...]).astype(BF16)
    s.z_ffo = ZScatter(net, w, lambda z: r.g_ffo.at[z], s.land_ffo)
    reduce.second()

    def in_block(i, carry):
        lanes = pl.ds(pl.multiple_of(i * 256, 256), 256)
        piece = dot_tn(s.all_n[:, lanes], r.back_pre[...]).astype(BF16)
        r.g_in[i] = piece.reshape(4, 64, r.share)
        return carry

    lax.fori_loop(0, 4, in_block, 0)
    s.z_in = ZScatter(net, w, lambda z: r.g_in.at[:, z], s.land_in)
    put_row(s.sums, 50, column_sum(r.back_pre[...].astype(F32)))
    pump()
    grad_one = r.normed[...] + reduce.total()
    hat = s.hat_one[...]
    back_one = norm_back(grad_one, hat, s.root_one[:, 0:1], s.vec[G1 : G1 + 1])
    branch = back_one.astype(BF16)
    r.back_one[...] = back_one
    r.all_branch[rows_of(w.slot, 128)] = branch

    def sums():
        put_row(s.sums, 8 * G1, column_sum(grad_one * hat))
        put_row(s.sums, 8 * S1, column_sum(grad_one))
        put_row(s.sums, 8 * BO, column_sum(branch.astype(F32)))

    return sums


def attend_backward(net, w, r, s, started, pump, done):
    width = r.width
    scale = jnp.asarray((width // ATTENTION_HEADS) ** (-0.5), BF16)

    def after_start():
        r.sum_k[...] = jnp.zeros_like(r.sum_k)
        r.sum_v[...] = jnp.zeros_like(r.sum_v)
        started()

    def on_group(kind):
        rows = rows_of(w.group[kind])
        out_w = s.w_out[...].reshape(128, width)
        r.back_context[rows] = dot_nt(r.all_branch[rows], out_w).astype(BF16)

        def block(i, carry):
            here = pl.ds(pl.multiple_of(w.group[kind] * 256 + i * 128, 128), 128)
            query = by_head(s.qkv[here, 0:128] * scale)
            upstream = by_head(r.back_context[here])
            mask = r.docs_col[here, 0:1] == r.docs_row[0:1, :]
            raw_both = dot_nt(query, s.qkv[:, 128:256])
            back_both = dot_nt(upstream, s.qkv[:, 256:384])
            probs_both, scores_both = [], []
            for h in range(2):
                rows_h = slice(h * 128, (h + 1) * 128)
                raw = jnp.where(mask, raw_both[rows_h], NEGATIVE)
                probs = jnp.exp(raw - s.logs[here, h * 64 : h * 64 + 1])
                back = back_both[rows_h]
                delta = jnp.sum(probs * back, axis=-1, keepdims=True)
                scores_both.append((probs * (back - delta)).astype(BF16))
                probs_both.append(probs.astype(BF16))
            scores = jnp.concatenate(scores_both, axis=0)
            total = dot_nn(scores, s.qkv[:, 128:256])
            r.sum_k[...] += dot_tn(scores, query)
            r.sum_v[...] += dot_tn(jnp.concatenate(probs_both, axis=0), upstream)
            total = own_lanes(total[0:128], total[128:256])
            r.back_qkv[here, 0:128] = (total * scale.astype(F32)).astype(BF16)
            return carry

        lax.fori_loop(0, 2, block, 0)

    gather(net, w, r.all_branch, on_group, after_start)
    r.back_qkv[:, 128:256] = r.sum_k[...].astype(BF16)
    r.back_qkv[:, 256:384] = r.sum_v[...].astype(BF16)

    def part(slot):
        return dot_nt(r.back_qkv[rows_of(slot, 128)], s.w_qkv[...].reshape(width, 384))

    reduce = Reduce(net, w, r, part)
    reduce.produce(DIAG)
    reduce.produce(XN)
    reduce.produce(YN)
    reduce.diag()
    reduce.first()
    put_row(s.sums, 48, column_sum(r.back_qkv[:, 0:128].astype(F32)))
    put_row(s.sums, 49, column_sum(r.back_qkv[:, 256:384].astype(F32)))
    pump(0)

    def qkv_block(i, carry):
        lanes = pl.ds(pl.multiple_of(i * 256, 256), 256)
        piece = dot_tn(s.all_x[:, lanes], r.back_qkv[...]).astype(BF16)
        s.g_qkv[i] = piece.reshape(4, 2, 32, 384)
        return carry

    lax.fori_loop(0, 4, qkv_block, 0)
    s.z_qkv = ZScatter(net, w, lambda z: s.g_qkv.at[:, z], s.land_qkv)
    reduce.produce(OWN)
    reduce.second()
    r.g_out[...] = dot_tn(s.context[...], r.all_branch[...]).astype(BF16).reshape(2, 2, 32, width)
    cross = net.send(r.g_out.at[:, 1 - w.y], s.g_out_z.at[pl.ds(2 * w.y, 2)], w.yn)
    kept = net.local(r.g_out.at[:, w.y], s.g_out_z.at[pl.ds(2 * w.y, 2)])
    kept.start()
    pump(1)
    grad = r.back_one[...] + reduce.total()
    done(grad)
    kept.wait()
    cross.wait_recv()
    s.z_out = ZScatter(net, w, lambda z: s.g_out_z.at[z], s.land_out)


FLAT_ROWS = 96


def whole_kernel(r):
    net = Net(r.ssem, r.rsem, r.lsem)
    w = place()
    layers = len(r.layer)
    first, last = r.layer[0], r.layer[-1]
    width, share = r.width, r.share
    unit = share // 4
    r.docs_mine[...] = jnp.broadcast_to(r.docs[...], (8, 128)).astype(F32)

    def pack_qkv(layer):
        for p in range(8):
            for k in range(3):
                lanes = slice(k * width + p * 128, k * width + (p + 1) * 128)
                r.layer[layer].qkv_parts[p // 2, p % 2, :, k * 128 : (k + 1) * 128] = r.qkv_in[layer, :, lanes]

    def pack_inner(layer):
        for p in range(8):
            for z in range(4):
                at = ((p // 2) * 8 + z * 2 + p % 2) * unit
                r.layer[layer].in_parts[p // 2, p % 2, :, z * unit : (z + 1) * unit] = r.inner_in[
                    layer, :, at : at + unit
                ]

    owner = w.d * 8 + w.z * 2 + w.y
    smalls = ((r.biases, r.n_bias, 0, 3), (r.norm_gains, r.n_gain, 3, 1), (r.value_bias, r.n_value, 4, 1))

    def shifted(size, rows):
        j = lax.broadcasted_iota(jnp.int32, (size, rows * 128), 0)
        k = lax.broadcasted_iota(jnp.int32, (size, rows * 128), 1)
        return jnp.where(k == j + lax.rem(owner * size, 128), 1.0, 0.0)

    def pack_vectors():
        r.vec_f[...] = jnp.zeros_like(r.vec_f)
        for ref, size, row, rows in smalls:
            placed = dot_nn(ref[...], shifted(size, rows).astype(BF16))
            for layer in range(layers):
                for k in range(rows):
                    at = 5 * layer + row + k
                    r.vec_f[at : at + 1, :] = placed[layer : layer + 1, k * 128 : (k + 1) * 128]
        r.vec_in[...] = r.vec_f[...].astype(BF16)

    def unpack_vectors():
        for (_, size, _, rows), base, out in zip(
            smalls, (0, 72, 88), (r.bias_grad, r.gain_grad, r.value_grad)
        ):
            for layer in range(layers):
                begin = layer * FLAT_ROWS + base + lax.div(owner * size, 128)
                for k in range(rows):
                    r.lined[layer : layer + 1, k * 128 : (k + 1) * 128] = r.vectors[pl.ds(begin + k, 1), :]
            out[...] = lax.dot_general(
                r.lined[:, 0 : rows * 128],
                shifted(size, rows),
                (((1,), (1,)), ((), ())),
                precision=lax.Precision.HIGHEST,
                preferred_element_type=F32,
            )[0:layers]

    def of_part(ref):
        return lambda p: ref.at[lax.div(p, 2), lax.rem(p, 2)]

    met = net.greet(w)
    pack_vectors()
    pack_qkv(0)
    pack_inner(0)
    met()
    parts = net.plane_swap(w, of_part(first.qkv_parts), of_part(first.qkv_piece))
    hidden = net.swap(w, r.hidden, r.hidden_row)
    docs = net.swap(w, r.docs_mine, r.docs_own)
    vec = net.z_all(w, r.vec_in, lambda z: r.vec_z.at[z])
    parts()
    first.zg_qkv = ZGather(net, w, first.qkv_piece, lambda z: first.w_qkv.at[:, z])
    first.zg_out = ZGather(net, w, r.out_in.at[0], lambda z: first.out_z.at[z])
    first.in_parted = net.plane_swap(w, of_part(first.in_parts), of_part(first.in_piece))
    vec()
    spread = net.plane_swap(w, lambda p: r.vec_z, lambda p: r.vec_all.at[p])
    docs()
    docs = net.plane_swap(w, lambda p: r.docs_own, lambda p: r.docs_all.at[p])
    hidden()
    first.all_x[rows_of(w.slot, 128)] = r.hidden_row[...]

    def unpack():
        spread()
        r.flat[...] = jnp.zeros_like(r.flat)
        for p in range(8):
            for z in range(4):
                owner = (p // 2) * 8 + z * 2 + p % 2
                piece = r.vec_all[p, z].astype(F32)
                for layer in range(layers):
                    base = layer * FLAT_ROWS
                    at = base + r.n_bias * owner // 128
                    r.flat[at : at + 3, :] += piece[5 * layer : 5 * layer + 3]
                    at = base + 72 + r.n_gain * owner // 128
                    r.flat[at : at + 1, :] += piece[5 * layer + 3 : 5 * layer + 4]
                    at = base + 88 + r.n_value * owner // 128
                    r.flat[at : at + 1, :] += piece[5 * layer + 4 : 5 * layer + 5]
        for layer in range(layers):
            s, base = r.layer[layer], layer * FLAT_ROWS
            for row, name in ((G1, 72), (S1, 56), (BO, 8), (G2, 80), (S2, 64), (B2, 48)):
                for k in range(8):
                    s.vec[row : row + 1, k * 128 : (k + 1) * 128] = r.flat[
                        base + name + k : base + name + k + 1, :
                    ]
            s.part_bias[...] = jnp.zeros_like(s.part_bias)
            s.part_bias[0:1, 0:128] = r.flat[pl.ds(base + w.part, 1), :]
            s.part_bias[0:1, 256:384] = r.flat[pl.ds(base + 88 + w.part, 1), :]
            for z in range(4):
                s.part_bias[1:2, z * unit : (z + 1) * unit] = r.flat[
                    pl.ds(base + 16 + 8 * w.d + 2 * z + w.y, 1), :
                ]
        docs()
        for p in range(8):
            slot = (p // 4) * 4 + (p % 2) * 2 + (p // 2) % 2
            numbers = r.docs_all[p]
            r.docs_row[:, slot * 128 : (slot + 1) * 128] = numbers
            r.docs_col[slot * 128 : (slot + 1) * 128, :] = jnp.broadcast_to(numbers[0:1], (128, 128)).T

    def bring_attention(layer):
        s = r.layer[layer]
        s.zg_qkv = ZGather(net, w, s.qkv_piece, lambda z: s.w_qkv.at[:, z])
        s.zg_out = ZGather(net, w, r.out_in.at[layer], lambda z: s.out_z.at[z])

    def bring_in(layer):
        s = r.layer[layer]
        s.zg_qkv.poll()
        s.zg_out.poll()
        s.zg_in = ZGather(net, w, s.in_piece, lambda z: s.w_in.at[:, z])

    def bring_ffo(layer):
        s = r.layer[layer]
        s.zg_in.poll()
        s.zg_ffo = ZGather(net, w, r.ffo_in.at[layer], lambda z: s.w_ffo.at[z])

    swaps = types.SimpleNamespace()
    for layer in range(layers):
        s = r.layer[layer]

        def started(layer=layer):
            if layer == 0:
                unpack()

        def handed(layer=layer, s=s):
            if layer == 0:
                s.in_parted()
                bring_in(0)

        def ready(s=s):
            s.zg_qkv.wait()
            s.zg_out.wait()

        def gathered(layer=layer):
            if layer + 1 < layers:
                n = r.layer[layer + 1]
                pack_qkv(layer + 1)
                pack_inner(layer + 1)
                n.qkv_parted = net.plane_swap(w, of_part(n.qkv_parts), of_part(n.qkv_piece))
                n.in_parted = net.plane_swap(w, of_part(n.in_parts), of_part(n.in_piece))

        def before(layer=layer):
            return r.hidden_row[...].astype(F32) if layer == 0 else r.state[...]

        attend_forward(
            net, w, r, s, before, started, handed, ready, gathered, lambda layer=layer: bring_ffo(layer)
        )

        def ready_in(s=s):
            s.zg_in.wait()

        def ready_ffo(s=s):
            s.zg_ffo.wait()

        def pump(at, layer=layer, s=s):
            if at == 0:
                s.zg_ffo.poll()
                if layer + 1 < layers:
                    r.layer[layer + 1].qkv_parted()
                    r.layer[layer + 1].in_parted()
                    bring_attention(layer + 1)
            elif layer + 1 < layers:
                bring_in(layer + 1)
            else:
                swaps.grad = net.swap(w, r.out_grad, r.grad_row)

        state = feed_forward(net, w, r, s, ready_in, ready_ffo, pump)
        r.state[...] = state
        if layer + 1 < layers:
            r.layer[layer + 1].all_x[rows_of(w.slot, 128)] = state.astype(BF16)
        else:
            r.state_low[...] = state.astype(BF16)
    swaps.grad()
    net.settle()
    swaps.out = net.swap(w, r.state_low, r.out)
    grad = r.grad_row[...].astype(F32)

    def vectors_out(s):
        return net.z_spread(w, s.sums, s.sums_z)

    def vectors_plane(s, wait):
        wait()
        s.sums_own[...] = s.sums[...] + s.sums_z[0] + s.sums_z[1] + s.sums_z[2]
        return net.plane_swap(w, lambda p: s.sums_own, lambda p: s.sums_all.at[p])

    def vectors_in(layer, s, wait):
        wait()
        base = layer * FLAT_ROWS
        for row, name in ((G1, 72), (S1, 56), (BO, 8), (G2, 80), (S2, 64), (B2, 48)):
            total = s.sums_all[0, 8 * row : 8 * row + 8]
            for p in range(1, 8):
                total = total + s.sums_all[p, 8 * row : 8 * row + 8]
            r.vectors[base + name : base + name + 8, :] = total
        for p in range(8):
            r.vectors[base + p : base + p + 1, :] = s.sums_all[p, 48:49]
            r.vectors[base + 88 + p : base + 89 + p, :] = s.sums_all[p, 49:50]
            for z in range(4):
                at = base + 16 + 8 * (p // 2) + 2 * z + p % 2
                r.vectors[at : at + 1, :] = s.sums_all[p, 50 + z : 51 + z]

    def send_inner(s):
        s.in_parts[...] = s.z_in.total().astype(BF16).reshape(4, 2, 32, share)
        return net.plane_swap(w, of_part(s.in_parts), of_part(s.in_piece))

    def send_qkv(s):
        s.qkv_parts[...] = s.z_qkv.total().astype(BF16)
        return net.plane_swap(w, of_part(s.qkv_parts), of_part(s.qkv_piece))

    def place_inner(layer, s, wait):
        wait()
        for p in range(8):
            for z in range(4):
                at = ((p // 2) * 8 + z * 2 + p % 2) * unit
                r.in_grad[layer, :, at : at + unit] = s.in_piece[
                    p // 2, p % 2, :, z * unit : (z + 1) * unit
                ].astype(F32)

    def place_qkv(layer, s, wait):
        wait()
        for p in range(8):
            for k in range(3):
                lanes = slice(k * width + p * 128, k * width + (p + 1) * 128)
                r.qkv_grad[layer, :, lanes] = s.qkv_piece[
                    p // 2, p % 2, :, k * 128 : (k + 1) * 128
                ].astype(F32)

    for layer in reversed(range(layers)):
        s = r.layer[layer]
        a = r.layer[layer + 1] if layer + 1 < layers else None
        s.sums[...] = jnp.zeros_like(s.sums)

        def feed_started(layer=layer, a=a):
            if a is not None:
                r.ffo_grad[layer + 1] = a.z_ffo.total()
                a.in_wait = send_inner(a)

        def free(a=a):
            if a is not None:
                a.z_ffo.settle()
                a.z_in.settle()
                a.z_qkv.poll()
                a.z_out.poll()

        def feed_pump(a=a):
            if a is not None:
                a.vec_wait = vectors_plane(a, a.vec_wait)

        sums = feed_backward(net, w, r, s, grad, feed_started, free, feed_pump)
        if a is None:
            swaps.out()
        net.drain()

        def back_started(layer=layer, a=a, sums=sums):
            sums()
            if a is not None:
                place_inner(layer + 1, a, a.in_wait)
                r.out_grad_w[layer + 1] = a.z_out.total()
                a.qkv_wait = send_qkv(a)
                vectors_in(layer + 1, a, a.vec_wait)

        def back_pump(at, s=s):
            if at == 0:
                s.z_ffo.poll()
                s.vec_wait = vectors_out(s)
            else:
                s.z_in.poll()

        def done(grad, layer=layer):
            if layer:
                r.state[...] = grad
            else:
                r.state_low[...] = grad.astype(BF16)
                swaps.back = net.swap(w, r.state_low, r.input_grad)

        attend_backward(net, w, r, s, back_started, back_pump, done)
        if layer:
            grad = r.state[...]
            net.drain()
    r.ffo_grad[0] = first.z_ffo.total()
    first.in_wait = send_inner(first)
    if layers > 1:
        place_qkv(1, r.layer[1], r.layer[1].qkv_wait)
    first.vec_wait = vectors_plane(first, first.vec_wait)
    first.z_qkv.poll()
    first.z_out.poll()
    place_inner(0, first, first.in_wait)
    vectors_in(0, first, first.vec_wait)
    first.qkv_wait = send_qkv(first)
    r.out_grad_w[0] = first.z_out.total()
    swaps.back()
    unpack_vectors()
    place_qkv(0, first, first.qkv_wait)
    net.settle()


def plane_body(
    hidden_in,
    document_index,
    out_grad,
    qkv_weight,
    value_bias,
    attention_output_weight,
    ffn_in_weight,
    ffn_out_weight,
    biases,
    norm_gains,
):
    layers = qkv_weight.shape[0]
    width = hidden_in.shape[1]
    inner = ffn_in_weight.shape[2]
    share = inner // 8
    n_bias, n_gain, n_value = biases.shape[1], norm_gains.shape[1], value_bias.shape[1]

    ins = dict(
        hidden=hidden_in,
        docs=document_index,
        out_grad=out_grad,
        qkv_in=qkv_weight,
        out_in=attention_output_weight,
        inner_in=ffn_in_weight,
        ffo_in=ffn_out_weight,
        biases=biases,
        norm_gains=norm_gains,
        value_bias=value_bias,
    )
    outs = dict(
        out=((128, width), BF16),
        input_grad=((128, width), BF16),
        qkv_grad=(qkv_weight.shape, F32),
        out_grad_w=(attention_output_weight.shape, F32),
        in_grad=(ffn_in_weight.shape, F32),
        ffo_grad=(ffn_out_weight.shape, F32),
        bias_grad=((layers, n_bias), F32),
        gain_grad=((layers, n_gain), F32),
        value_grad=((layers, n_value), F32),
    )
    far = dict(hidden=1, out_grad=1, ffo_in=1, out_in=1, out=1, input_grad=1)
    whole = (1024, width)
    shared = dict(
        hidden_row=((128, width), BF16),
        grad_row=((128, width), BF16),
        docs_mine=((8, 128), F32),
        docs_own=((8, 128), F32),
        docs_all=((8, 8, 128), F32),
        docs_row=((8, 1024), F32),
        docs_col=((1024, 128), F32),
        vec_f=((16, 128), F32),
        vec_in=((16, 128), BF16),
        lined=((8, 384), F32),
        vectors=((layers * FLAT_ROWS, 128), F32),
        vec_z=((4, 16, 128), BF16),
        vec_all=((8, 4, 16, 128), BF16),
        flat=((layers * FLAT_ROWS, 128), F32),
        normed=((128, width), F32),
        state=((128, width), F32),
        state_low=((128, width), BF16),
        back_one=((128, width), F32),
        pre=((256, share), F32),
        all_second=(whole, BF16),
        all_branch=(whole, BF16),
        back_pre=((1024, share), BF16),
        back_context=((1024, 128), BF16),
        back_qkv=((1024, 384), BF16),
        sum_k=((1024, 128), F32),
        sum_v=((1024, 128), F32),
        g_out=((2, 2, 32, width), BF16),
        g_ffo=((4, 128, width), BF16),
        g_in=((4, 4, 64, share), BF16),
        core_out=((4, 128, width), BF16),
        core_in=((4, 128, width), BF16),
        keep=((4, 128, width), F32),
        across=((128, width), BF16),
        via_x=((64, width), BF16),
        via_y=((64, width), BF16),
        out_x=((128, width), BF16),
        out_y=((128, width), BF16),
        in_x=((128, width), BF16),
        in_y=((128, width), BF16),
    )
    each = dict(
        qkv_parts=((4, 2, 32, 384), BF16),
        qkv_piece=((4, 2, 32, 384), BF16),
        in_parts=((4, 2, 32, share), BF16),
        in_piece=((4, 2, 32, share), BF16),
        w_qkv=((4, 4, 2, 32, 384), BF16),
        w_in=((4, 4, 2, 32, share), BF16),
        w_ffo=((4, 128, width), BF16),
        out_z=((4, 32, width), BF16),
        w_out=((2, 2, 32, width), BF16),
        vec=((8, width), F32),
        part_bias=((8, width), F32),
        all_x=(whole, BF16),
        qkv=((1024, 384), BF16),
        context=((1024, 128), BF16),
        logs=((1024, 128), F32),
        all_n=(whole, BF16),
        inner=((1024, share), BF16),
        slope=((1024, share), BF16),
        hat_one=((128, width), F32),
        root_one=((128, 128), F32),
        hat_two=((128, width), F32),
        root_two=((128, 128), F32),
        g_qkv=((4, 4, 2, 32, 384), BF16),
        g_out_z=((4, 32, width), BF16),
        land_ffo=((4, 128, width), BF16),
        land_in=((4, 4, 64, share), BF16),
        land_qkv=((4, 4, 2, 32, 384), BF16),
        land_out=((4, 32, width), BF16),
        sums=((56, 128), F32),
        sums_z=((3, 56, 128), F32),
        sums_own=((56, 128), F32),
        sums_all=((8, 56, 128), F32),
    )

    def kernel(*refs):
        refs = list(refs)

        def take(names):
            return dict(zip(names, [refs.pop(0) for _ in names]))

        r = types.SimpleNamespace(
            width=width, share=share, n_bias=n_bias, n_gain=n_gain, n_value=n_value, **take(ins), **take(outs), **take(shared)
        )
        r.layer = [types.SimpleNamespace(**take(each)) for _ in range(layers)]
        r.ssem, r.rsem, r.lsem = refs
        whole_kernel(r)

    def held(items):
        return [VMEM(shape, dtype) for shape, dtype in items.values()]

    results = pl.pallas_call(
        kernel,
        out_shape=[jax.ShapeDtypeStruct(shape, dtype) for shape, dtype in outs.values()],
        in_specs=[pl.BlockSpec(memory_space=pl.ANY if name in far else VMEM) for name in ins],
        out_specs=[pl.BlockSpec(memory_space=pl.ANY if name in far else VMEM) for name in outs],
        scratch_shapes=[
            *held(shared),
            *(held(each) * layers),
            pltpu.SemaphoreType.DMA((COPIES,)),
            pltpu.SemaphoreType.DMA((COPIES,)),
            pltpu.SemaphoreType.DMA((48,)),
        ],
        compiler_params=pltpu.CompilerParams(
            collective_id=0, has_side_effects=True, vmem_limit_bytes=VMEM_LIMIT
        ),
    )(*ins.values())
    out, input_grad, g_qkv, g_out, g_in, g_ffo, g_bias, g_gain, g_value = results
    return in_place((out, input_grad, g_qkv, g_value, g_out, g_in, g_ffo, g_bias, g_gain))


def in_place(results):
    last = len(results)

    def kernel(*refs):
        sems = refs[-1]
        copies = [
            pltpu.make_async_copy(refs[k], refs[last + k], sems.at[k]) for k in range(last) if k != 1
        ]
        for copy in copies:
            copy.start()
        refs[last + 1][...] = refs[1][...].astype(F32)
        for copy in copies:
            copy.wait()

    return pl.pallas_call(
        kernel,
        out_shape=[jax.ShapeDtypeStruct(v.shape, F32 if k == 1 else v.dtype) for k, v in enumerate(results)],
        in_specs=[pl.BlockSpec(memory_space=VMEM)] * last,
        out_specs=[pl.BlockSpec(memory_space=VMEM if k == 1 else pl.ANY) for k in range(last)],
        scratch_shapes=[pltpu.SemaphoreType.DMA((last,))],
    )(*results)


def fits_plane(mesh):
    return mesh.shape[DP] == 4 and mesh.shape[CTX] == 8


def solution(mesh):
    return jax.shard_map(
        plane_body if fits_plane(mesh) else body,
        mesh=mesh,
        in_specs=(
            P(BOTH, None),
            P(DP, CTX),
            P(BOTH, None),
            P(None, BOTH, None),
            P(None, BOTH),
            P(None, BOTH, None),
            P(None, BOTH, None),
            P(None, BOTH, None),
            P(None, BOTH),
            P(None, BOTH),
        ),
        out_specs=(
            P(BOTH, None),
            P(BOTH, None),
            P(None, BOTH, None),
            P(None, BOTH),
            P(None, BOTH, None),
            P(None, BOTH, None),
            P(None, BOTH, None),
            P(None, BOTH),
            P(None, BOTH),
        ),
        check_vma=False,
    )
```

```python
import math
import types

import jax
import jax.numpy as jnp
from jax import lax
from jax.experimental import pallas as pl
from jax.experimental.pallas import tpu as pltpu
from jax.sharding import PartitionSpec as P

ATTENTION_HEADS = 16


DP, CTX = "dp", "ctx"
BOTH = (DP, CTX)

QUERY_KEY, TO_QUERY, TO_KEY = "qhd,khd->hqk", "hqk,khd->qhd", "hqk,qhd->khd"
EPS = 1e-12
NEGATIVE = -1e30


def norm_rows(resid, gain, shift):
    mean = jnp.mean(resid, axis=-1, keepdims=True)
    centered = resid - mean
    variance = jnp.mean(centered * centered, axis=-1, keepdims=True)
    return centered * lax.rsqrt(variance + EPS) * gain + shift


def exact_gelu(value):
    return jax.nn.gelu(value, approximate=False)


def cross(left, right_operand):
    return lax.dot_general(
        left, right_operand, (((0,), (0,)), ((), ())), preferred_element_type=jnp.float32
    )


def back_product(upstream, weight):
    return lax.dot_general(
        upstream, weight, (((1,), (1,)), ((), ())), preferred_element_type=jnp.float32
    )


def by_blocks(step_fn, carry, pieces, token_block):
    count = pieces[0].shape[0]

    def turn(index, state):
        offset = index * token_block
        parts = tuple((lax.dynamic_slice_in_dim(item, offset, token_block, 0) for item in pieces))
        return step_fn(state, parts, offset)

    return lax.fori_loop(0, count // token_block, turn, carry)


def unpack(fetched, width, inner):
    w_qkv, w_out, w_in, w_ffo, value_vec, bias_all, gains = fetched
    value_vec = value_vec.astype(jnp.float32)
    bias_all = bias_all.astype(jnp.float32)
    gains = gains.astype(jnp.float32)
    query_bias = bias_all[0:width]
    out_bias = bias_all[width : 2 * width]
    inner_bias = bias_all[2 * width : 2 * width + inner]
    ffn_bias = bias_all[2 * width + inner : 3 * width + inner]
    shift_one = bias_all[3 * width + inner : 4 * width + inner]
    shift_two = bias_all[4 * width + inner : 5 * width + inner]
    return (
        w_qkv,
        w_out,
        w_in,
        w_ffo,
        value_vec,
        query_bias,
        out_bias,
        inner_bias,
        ffn_bias,
        shift_one,
        shift_two,
        gains[0:width],
        gains[width : 2 * width],
    )


def masked_scores(query_heads, key_piece, seg_own, segment_row, start, scale):
    count = key_piece.shape[0]
    heads = query_heads.shape[1]
    split_key_heads = key_piece.reshape(count, heads, query_heads.shape[2])
    seg_keys = lax.dynamic_slice_in_dim(segment_row, start, count, 0)
    mask = (seg_own[:, None] == seg_keys[None, :])[None]
    raw = (
        jnp.einsum(QUERY_KEY, query_heads, split_key_heads, preferred_element_type=jnp.float32)
        * scale
    )
    return (jnp.where(mask, raw, NEGATIVE), mask, split_key_heads)


def body(
    hidden_in,
    document_index,
    out_grad,
    qkv_weight,
    value_bias,
    attention_output_weight,
    ffn_in_weight,
    ffn_out_weight,
    biases,
    norm_gains,
):
    layers = qkv_weight.shape[0]
    width = qkv_weight.shape[2] // 3
    inner = ffn_in_weight.shape[2]
    heads = ATTENTION_HEADS
    head_width = width // heads
    scale = head_width ** (-0.5)
    rows = hidden_in.shape[0]
    seg_own = document_index[0]
    segment_row = lax.all_gather(document_index, CTX, axis=1, tiled=True)[0]
    row_len = segment_row.shape[0]
    state = hidden_in.astype(jnp.float32)
    saved = []
    for layer in range(layers):
        fetched = (
            lax.all_gather(qkv_weight[layer], BOTH, axis=0, tiled=True),
            lax.all_gather(attention_output_weight[layer], BOTH, axis=0, tiled=True),
            lax.all_gather(ffn_in_weight[layer], BOTH, axis=0, tiled=True),
            lax.all_gather(ffn_out_weight[layer], BOTH, axis=0, tiled=True),
            lax.all_gather(value_bias[layer], BOTH, axis=0, tiled=True),
            lax.all_gather(biases[layer], BOTH, axis=0, tiled=True),
            lax.all_gather(norm_gains[layer], BOTH, axis=0, tiled=True),
        )
        (
            w_qkv,
            w_out,
            w_in,
            w_ffo,
            value_vec,
            query_bias,
            out_bias,
            inner_bias,
            ffn_bias,
            shift_one,
            shift_two,
            gain_one,
            gain_two,
        ) = unpack(fetched, width, inner)
        state_low = state.astype(jnp.bfloat16)
        qkv_bias = jnp.concatenate([query_bias, jnp.zeros_like(query_bias), value_vec])
        qkv_low = (jnp.dot(state_low, w_qkv, preferred_element_type=jnp.float32) + qkv_bias).astype(
            jnp.bfloat16
        )
        query_heads = qkv_low[:, 0:width].reshape(rows, heads, head_width)
        key_low = qkv_low[:, width : 2 * width]
        value_low = qkv_low[:, 2 * width : 3 * width]

        def stats_step(carry, parts, start):
            top, total = carry
            raw, mask, split_key_heads = masked_scores(
                query_heads, parts[0], seg_own, segment_row, start, scale
            )
            new_top = jnp.maximum(top, jnp.max(raw, axis=-1))
            weights = jnp.where(mask, jnp.exp(raw - new_top[:, :, None]), 0.0)
            return (new_top, total * jnp.exp(top - new_top) + jnp.sum(weights, axis=-1))

        stats_init = (
            jnp.full((heads, rows), NEGATIVE, jnp.float32),
            jnp.zeros((heads, rows), jnp.float32),
        )
        held_pair = None
        top, total = by_blocks(
            stats_step, stats_init, (lax.all_gather(key_low, CTX, axis=0, tiled=True),), rows
        )
        log_total = top + jnp.log(total)

        def value_step(carry, parts, start):
            context_acc, exact_acc = carry
            raw, mask, split_key_heads = masked_scores(
                query_heads, parts[0], seg_own, segment_row, start, scale
            )
            split_value_heads = parts[1].reshape(parts[1].shape[0], heads, head_width)
            probs = jnp.where(mask, jnp.exp(raw - log_total[:, :, None]), 0.0)
            probs_low = probs.astype(jnp.bfloat16)
            residue_low = (probs - probs_low.astype(jnp.float32)).astype(jnp.bfloat16)
            part_low = jnp.einsum(
                TO_QUERY, probs_low, split_value_heads, preferred_element_type=jnp.float32
            )
            part_fix = jnp.einsum(
                TO_QUERY, residue_low, split_value_heads, preferred_element_type=jnp.float32
            )
            return (context_acc + part_low, exact_acc + part_fix)

        value_init = (
            jnp.zeros((rows, heads, head_width), jnp.float32),
            jnp.zeros((rows, heads, head_width), jnp.float32),
        )
        context, correction = by_blocks(
            value_step,
            value_init,
            (
                lax.all_gather(key_low, CTX, axis=0, tiled=True),
                lax.all_gather(value_low, CTX, axis=0, tiled=True),
            ),
            rows,
        )
        context_exact = (context + correction).reshape(rows, width)
        context = context.reshape(rows, width)
        context_low = context.astype(jnp.bfloat16)
        resid_one = (
            state + jnp.dot(context_low, w_out, preferred_element_type=jnp.float32) + out_bias
        )
        normed = norm_rows(resid_one, gain_one, shift_one)
        normed_low = normed.astype(jnp.bfloat16)
        pre = jnp.dot(normed_low, w_in, preferred_element_type=jnp.float32) + inner_bias
        inner_low = exact_gelu(pre).astype(jnp.bfloat16)
        resid_two = (
            normed + jnp.dot(inner_low, w_ffo, preferred_element_type=jnp.float32) + ffn_bias
        )
        saved.append(
            (
                fetched,
                state_low,
                qkv_low,
                log_total,
                context_exact,
                context_low,
                resid_one,
                normed_low,
                pre,
                inner_low,
                resid_two,
                held_pair,
            )
        )
        state = norm_rows(resid_two, gain_two, shift_two)
    upstream = out_grad.astype(jnp.float32)
    per_layer = []
    for layer in reversed(range(layers)):
        (
            fetched,
            state_low,
            qkv_low,
            log_total,
            context_exact,
            context_low,
            resid_one,
            normed_low,
            pre,
            inner_low,
            resid_two,
            held_pair,
        ) = saved[layer]
        weights_now = (
            lax.all_gather(qkv_weight[layer], BOTH, axis=0, tiled=True),
            lax.all_gather(attention_output_weight[layer], BOTH, axis=0, tiled=True),
            lax.all_gather(ffn_in_weight[layer], BOTH, axis=0, tiled=True),
            lax.all_gather(ffn_out_weight[layer], BOTH, axis=0, tiled=True),
            lax.all_gather(value_bias[layer], BOTH, axis=0, tiled=True),
            lax.all_gather(biases[layer], BOTH, axis=0, tiled=True),
            lax.all_gather(norm_gains[layer], BOTH, axis=0, tiled=True),
        )
        (
            w_qkv,
            w_out,
            w_in,
            w_ffo,
            value_vec,
            query_bias,
            out_bias,
            inner_bias,
            ffn_bias,
            shift_one,
            shift_two,
            gain_one,
            gain_two,
        ) = unpack(weights_now, width, inner)
        query_low = qkv_low[:, 0:width]
        query_heads = query_low.reshape(rows, heads, head_width)
        key_low = qkv_low[:, width : 2 * width]
        value_low = qkv_low[:, 2 * width : 3 * width]
        unused_two, pull_two = jax.vjp(norm_rows, resid_two, gain_two, shift_two)
        back_two, back_gain_two, back_shift_two = pull_two(upstream)
        back_second = back_two.astype(jnp.bfloat16)
        grad_second = cross(inner_low, back_second)
        back_inner = back_product(back_second, w_ffo)
        unused_pre, pull_gelu = jax.vjp(exact_gelu, pre)
        back_pre = pull_gelu(back_inner)[0].astype(jnp.bfloat16)
        grad_first = cross(normed_low, back_pre)
        back_normed = back_two + back_product(back_pre, w_in)
        normed_again, pull_one = jax.vjp(norm_rows, resid_one, gain_one, shift_one)
        back_one, back_gain_one, back_shift_one = pull_one(back_normed)
        back_branch = back_one.astype(jnp.bfloat16)
        grad_out_proj = cross(context_low, back_branch)
        back_context = back_product(back_branch, w_out).astype(jnp.bfloat16)
        context_heads_back = back_context.reshape(rows, heads, head_width)
        delta = jnp.sum(
            (back_context.astype(jnp.float32) * context_exact).reshape(rows, heads, head_width),
            axis=-1,
        ).T

        def grad_step(carry, parts, start):
            query_sum, key_sums, value_sums = carry
            count = parts[0].shape[0]
            raw, mask, split_key_heads = masked_scores(
                query_heads, parts[0], seg_own, segment_row, start, scale
            )
            split_value_heads = parts[1].reshape(count, heads, head_width)
            probs = jnp.where(mask, jnp.exp(raw - log_total[:, :, None]), 0.0)
            back_probs = jnp.einsum(
                QUERY_KEY,
                context_heads_back,
                split_value_heads,
                preferred_element_type=jnp.float32,
            )
            back_scores = (probs * (back_probs - delta[:, :, None])).astype(jnp.bfloat16)
            query_part = (
                jnp.einsum(
                    TO_QUERY, back_scores, split_key_heads, preferred_element_type=jnp.float32
                )
                * scale
            )
            key_part = (
                jnp.einsum(
                    TO_KEY, back_scores, query_heads, preferred_element_type=jnp.float32
                ).reshape(count, width)
                * scale
            )
            value_part = jnp.einsum(
                TO_KEY,
                probs.astype(jnp.bfloat16),
                context_heads_back,
                preferred_element_type=jnp.float32,
            ).reshape(count, width)
            key_sums = lax.dynamic_update_slice_in_dim(
                key_sums, lax.dynamic_slice_in_dim(key_sums, start, count, 0) + key_part, start, 0
            )
            value_sums = lax.dynamic_update_slice_in_dim(
                value_sums,
                lax.dynamic_slice_in_dim(value_sums, start, count, 0) + value_part,
                start,
                0,
            )
            return (query_sum + query_part, key_sums, value_sums)

        query_init = jnp.zeros((rows, heads, head_width), jnp.float32)
        grad_init = (
            query_init,
            jnp.zeros((row_len, width), jnp.float32),
            jnp.zeros((row_len, width), jnp.float32),
        )
        folded = by_blocks(
            grad_step,
            grad_init,
            (
                lax.all_gather(key_low, CTX, axis=0, tiled=True),
                lax.all_gather(value_low, CTX, axis=0, tiled=True),
            ),
            rows,
        )
        query_sum, key_sums, value_sums = folded
        key_own, value_own = (
            lax.psum_scatter(
                key_sums.astype(jnp.bfloat16), CTX, scatter_dimension=0, tiled=True
            ).astype(jnp.float32),
            lax.psum_scatter(
                value_sums.astype(jnp.bfloat16), CTX, scatter_dimension=0, tiled=True
            ).astype(jnp.float32),
        )
        back_qkv = jnp.concatenate(
            [query_sum.reshape(rows, width), key_own, value_own], axis=1
        ).astype(jnp.bfloat16)
        grad_qkv = cross(state_low, back_qkv)
        back_qkv_float = back_qkv.astype(jnp.float32)
        grad_value_bias = jnp.sum(back_qkv_float[:, 2 * width : 3 * width], axis=0)
        grad_bias = jnp.concatenate(
            [
                jnp.sum(back_qkv_float[:, 0:width], axis=0),
                jnp.sum(back_branch.astype(jnp.float32), axis=0),
                jnp.sum(back_pre.astype(jnp.float32), axis=0),
                jnp.sum(back_second.astype(jnp.float32), axis=0),
                back_shift_one,
                back_shift_two,
            ]
        )
        grad_gain = jnp.concatenate([back_gain_one, back_gain_two])
        upstream = back_one + back_product(back_qkv, w_qkv)
        shards = (
            lax.psum_scatter(grad_qkv, BOTH, scatter_dimension=0, tiled=True),
            lax.psum_scatter(grad_value_bias, BOTH, scatter_dimension=0, tiled=True),
            lax.psum_scatter(grad_out_proj, BOTH, scatter_dimension=0, tiled=True),
            lax.psum_scatter(grad_first, BOTH, scatter_dimension=0, tiled=True),
            lax.psum_scatter(grad_second, BOTH, scatter_dimension=0, tiled=True),
            lax.psum_scatter(grad_bias, BOTH, scatter_dimension=0, tiled=True),
            lax.psum_scatter(grad_gain, BOTH, scatter_dimension=0, tiled=True),
        )
        per_layer.append(shards)
    ordered = per_layer[::-1]
    stacked = tuple((jnp.stack([item[member] for item in ordered]) for member in range(7)))
    return (
        state.astype(jnp.bfloat16),
        upstream,
        stacked[0],
        stacked[1],
        stacked[2],
        stacked[3],
        stacked[4],
        stacked[5],
        stacked[6],
    )


MESH = pl.DeviceIdType.MESH
F32 = jnp.float32
BF16 = jnp.bfloat16
VMEM = pltpu.VMEM
VMEM_LIMIT = 62 * 2**20
PHASE, COPIES = 32, 208
OWN, XN, YN, DIAG = range(4)
G1, S1, BO, G2, S2, B2 = range(6)


def dot_nn(a, b):
    return lax.dot_general(a, b, (((1,), (0,)), ((), ())), preferred_element_type=F32)


def dot_nt(a, b):
    return lax.dot_general(a, b, (((1,), (1,)), ((), ())), preferred_element_type=F32)


def dot_tn(a, b):
    return lax.dot_general(a, b, (((0,), (0,)), ((), ())), preferred_element_type=F32)


def turned(two_bits):
    return lax.rem(two_bits, 2) * 2 + lax.div(two_bits, 2)


def place():
    d, t = lax.axis_index(DP), lax.axis_index(CTX)
    x, c = lax.div(d, 2), lax.rem(d, 2)
    z, y = lax.div(t, 2), lax.rem(t, 2)
    w = types.SimpleNamespace(d=d, x=x, c=c, z=z, y=y)
    w.part = d * 2 + y
    w.group = (x * 2 + y, (1 - x) * 2 + y, x * 2 + 1 - y, (1 - x) * 2 + 1 - y)
    w.slot = w.group[OWN] * 2 + c
    w.xn, w.yn, w.sib = ((1 - x) * 2 + c, t), (d, z * 2 + 1 - y), (x * 2 + 1 - c, t)
    w.plane = []
    for bits in range(1, 8):
        xx = 1 - x if bits & 4 else x
        cc = 1 - c if bits & 2 else c
        yy = 1 - y if bits & 1 else y
        w.plane.append(((xx * 2 + cc, z * 2 + yy), (xx * 2 + cc) * 2 + yy))
    w.zs = [(d, lax.rem(z + k, 4) * 2 + y) for k in (1, 2, 3)]
    w.far = lax.rem(z + 2, 4)
    w.up, w.down, w.over = (d, (z + 1) * 2 + y), (d, (z - 1) * 2 + y), (d, w.far * 2 + y)
    w.middle = (z == 1) | (z == 2)
    w.edge = (z == 0) | (z == 3)
    w.end = jnp.where(z == 1, 0, 3)
    w.near_end = (d, w.end * 2 + y)
    w.inside = jnp.where(z == 0, 1, 2)
    w.near_middle = (d, w.inside * 2 + y)
    w.opposite = 3 - z
    w.away = d != turned(z)
    w.home = d == turned(z)
    w.swap = (turned(z), turned(d) * 2 + y)
    return w


class Maybe:
    def __init__(self, copy, sends, receives):
        self.copy, self.sends, self.receives = copy, sends, receives

    def start(self):
        pl.when(self.sends)(self.copy.start)

    def wait_send(self):
        pl.when(self.sends)(self.copy.wait_send)

    def wait_recv(self):
        pl.when(self.receives)(self.copy.wait_recv)


class Net:
    def __init__(self, ssem, rsem, lsem):
        self.ssem, self.rsem, self.lsem = ssem, rsem, lsem
        self.sent, self.slow, self.scatters, self.at, self.near = [], [], [], PHASE, 0
        self.phase = 0

    def greet(self, w):
        barrier = pltpu.get_barrier_semaphore()
        devices = [device for device, _ in w.plane] + w.zs
        for device in devices:
            pl.semaphore_signal(barrier, inc=1, device_id=device, device_id_type=MESH)

        @pl.when(w.away)
        def _():
            pl.semaphore_signal(barrier, inc=1, device_id=w.swap, device_id_type=MESH)

        return lambda: pl.semaphore_wait(barrier, len(devices) + jnp.where(w.away, 1, 0))

    def make(self, src, dst, device, slow=True):
        at = self.at if slow else self.phase
        if slow:
            self.at += 1
        else:
            self.phase += 1
        return pltpu.make_async_remote_copy(
            src_ref=src,
            dst_ref=dst,
            send_sem=self.ssem.at[at],
            recv_sem=self.rsem.at[at],
            device_id=device,
            device_id_type=MESH,
        )

    def maybe(self, src, dst, device, sends, receives):
        copy = Maybe(self.make(src, dst, device), sends, receives)
        self.slow.append(copy)
        return copy

    def send(self, src, dst, device, slow=False):
        copy = self.make(src, dst, device, slow)
        copy.start()
        (self.slow if slow else self.sent).append(copy)
        return copy

    def local(self, src, dst):
        copy = pltpu.make_async_copy(src, dst, self.lsem.at[self.near])
        self.near += 1
        return copy

    def swap(self, w, src, dst):
        far = Maybe(self.make(src, dst, w.swap), w.away, w.away)
        near = self.local(src, dst)
        far.start()
        pl.when(w.home)(near.start)

        def wait():
            far.wait_recv()
            far.wait_send()
            pl.when(w.home)(near.wait)

        return wait

    def plane_swap(self, w, at, to):
        copies = [self.send(at(part), to(w.part), device, True) for device, part in w.plane]
        own = self.local(at(w.part), to(w.part))
        own.start()

        def wait():
            own.wait()
            for copy in copies:
                copy.wait_recv()

        return wait

    def z_all(self, w, src, at):
        copies = [self.send(src, at(w.z), device, True) for device in w.zs]
        own = self.local(src, at(w.z))
        own.start()

        def wait():
            own.wait()
            for copy in copies:
                copy.wait_recv()

        return wait

    def z_spread(self, w, src, land):
        copies = [self.send(src, land.at[k], device, True) for k, device in enumerate(w.zs)]

        def wait():
            for copy in copies:
                copy.wait_recv()

        return wait

    def drain(self):
        for copy in self.sent:
            copy.wait_send()
        self.sent, self.phase = [], 0

    def settle(self):
        self.drain()
        for copy in self.slow:
            copy.wait_send()
        self.slow = []
        for scatter in self.scatters:
            scatter.settle()


class ZGather:
    def __init__(self, net, w, src, at):
        self.w, here = w, at(w.z)
        self.over = net.send(src, here, w.over, True)
        self.up = net.maybe(src, here, w.up, w.z < 3, w.z > 0)
        self.down = net.maybe(src, here, w.down, w.z > 0, w.z < 3)
        far = at(w.far)
        self.on = net.maybe(far, far, w.near_end, w.middle, w.edge)
        self.own = net.local(src, here)
        self.up.start()
        self.down.start()
        self.own.start()

    def poll(self):
        pl.when(self.w.middle)(self.over.wait_recv)
        self.on.start()

    def wait(self):
        pl.when(self.w.edge)(self.over.wait_recv)
        self.own.wait()
        for copy in (self.up, self.down, self.on):
            copy.wait_recv()


class ZScatter:
    def __init__(self, net, w, at, land):
        self.w, self.at, self.land = w, at, land
        self.on = net.maybe(at(w.opposite), land.at[3], w.near_middle, w.edge, w.middle)
        self.on.start()
        self.up = net.maybe(at(lax.rem(w.z + 1, 4)), land.at[0], w.up, w.z < 3, w.z > 0)
        self.down = net.maybe(at(lax.rem(w.z + 3, 4)), land.at[1], w.down, w.z > 0, w.z < 3)
        self.end_over = net.maybe(at(w.far), land.at[2], w.over, w.edge, w.middle)
        self.mid_over = net.maybe(land.at[3], land.at[2], w.over, w.middle, w.edge)
        self.sends = (self.on, self.up, self.down, self.end_over, self.mid_over)
        net.slow = [copy for copy in net.slow if copy not in self.sends]
        net.scatters.append(self)
        for copy in (self.end_over, self.up, self.down):
            copy.start()

        @pl.when(w.z == 0)
        def _():
            land[0] = jnp.zeros(land.shape[1:], BF16)

        @pl.when(w.z == 3)
        def _():
            land[1] = jnp.zeros(land.shape[1:], BF16)

    def poll(self):
        @pl.when(self.w.middle)
        def _():
            self.on.copy.wait_recv()
            own = self.at(self.w.far)[...].astype(F32)
            self.land[3] = (self.land[3].astype(F32) + own).astype(BF16)

        self.mid_over.start()

    def settle(self):
        for copy in self.sends:
            copy.wait_send()
        self.sends = ()

    def total(self):
        for copy in (self.up, self.down, self.end_over, self.mid_over):
            copy.wait_recv()
        land = self.land
        return (
            self.at(self.w.z)[...].astype(F32)
            + land[0].astype(F32)
            + land[1].astype(F32)
            + land[2].astype(F32)
        )


def nothing():
    pass


def gather(net, w, buf, on_group, after_start=nothing, after_forward=None):
    def half(group, h):
        return buf.at[pl.ds(pl.multiple_of((group * 2 + w.c) * 128 + h * 64, 64), 64)]

    def put(group, h, device):
        ref = half(group, h)
        return net.send(ref, ref, device)

    own, xn, yn, diag = w.group
    x0 = put(own, 0, w.xn)
    y1 = put(own, 1, w.yn)
    whole = buf.at[rows_of(w.slot, 128)]
    c0 = net.send(whole, whole, w.sib)
    x1 = put(own, 1, w.xn)
    y0 = put(own, 0, w.yn)
    after_start()
    if after_forward is None:
        c0.wait_recv()
        on_group(OWN)
    x0.wait_recv()
    d0 = put(xn, 0, w.yn)
    cx0 = put(xn, 0, w.sib)
    y1.wait_recv()
    d1 = put(yn, 1, w.xn)
    cy1 = put(yn, 1, w.sib)
    x1.wait_recv()
    cx1 = put(xn, 1, w.sib)
    y0.wait_recv()
    cy0 = put(yn, 0, w.sib)
    if after_forward is not None:
        after_forward()
        c0.wait_recv()
        on_group(OWN)
    cx0.wait_recv()
    cx1.wait_recv()
    on_group(XN)
    cy0.wait_recv()
    cy1.wait_recv()
    on_group(YN)
    d0.wait_recv()
    cd0 = put(diag, 0, w.sib)
    d1.wait_recv()
    cd1 = put(diag, 1, w.sib)
    cd0.wait_recv()
    cd1.wait_recv()
    on_group(DIAG)


class Reduce:
    def __init__(self, net, w, r, part):
        self.net, self.w, self.r, self.part = net, w, r, part
        self.cores = [None] * 4

    def produce(self, kind):
        w, r = self.w, self.r
        group = w.group[kind]
        r.core_out[kind] = self.part(group * 2 + 1 - w.c).astype(BF16)
        self.cores[kind] = self.net.send(r.core_out.at[kind], r.core_in.at[kind], w.sib)
        r.keep[kind] = self.part(group * 2 + w.c)

    def both(self, kind, rows):
        return self.r.keep[kind, rows] + self.r.core_in[kind, rows].astype(F32)

    def diag(self):
        w, r = self.w, self.r
        self.cores[DIAG].wait_recv()
        r.across[...] = self.both(DIAG, slice(0, 128)).astype(BF16)
        self.fy = self.net.send(r.across.at[pl.ds(0, 64)], r.via_y, w.yn)
        self.fx = self.net.send(r.across.at[pl.ds(64, 64)], r.via_x, w.xn)

    def first(self):
        w, r = self.w, self.r
        self.cores[XN].wait_recv()
        r.out_x[64:128] = self.both(XN, slice(64, 128)).astype(BF16)
        self.x1 = self.net.send(r.out_x.at[pl.ds(64, 64)], r.in_x.at[pl.ds(64, 64)], w.xn)
        self.cores[YN].wait_recv()
        r.out_y[0:64] = self.both(YN, slice(0, 64)).astype(BF16)
        self.y0 = self.net.send(r.out_y.at[pl.ds(0, 64)], r.in_y.at[pl.ds(0, 64)], w.yn)

    def second(self):
        w, r = self.w, self.r
        self.fy.wait_recv()
        r.out_x[0:64] = (self.both(XN, slice(0, 64)) + r.via_y[...].astype(F32)).astype(BF16)
        self.x0 = self.net.send(r.out_x.at[pl.ds(0, 64)], r.in_x.at[pl.ds(0, 64)], w.xn)
        self.fx.wait_recv()
        r.out_y[64:128] = (self.both(YN, slice(64, 128)) + r.via_x[...].astype(F32)).astype(BF16)
        self.y1 = self.net.send(r.out_y.at[pl.ds(64, 64)], r.in_y.at[pl.ds(64, 64)], w.yn)

    def total(self):
        r = self.r
        self.cores[OWN].wait_recv()
        for copy in (self.x1, self.y0, self.x0, self.y1):
            copy.wait_recv()
        return self.both(OWN, slice(0, 128)) + r.in_x[...].astype(F32) + r.in_y[...].astype(F32)


def rows_of(group, n=256):
    return pl.ds(pl.multiple_of(group * n, n), n)


def norm_parts(resid):
    mean = jnp.mean(resid, axis=-1, keepdims=True)
    centered = resid - mean
    variance = jnp.mean(centered * centered, axis=-1, keepdims=True)
    root = lax.rsqrt(variance + EPS)
    return centered * root, root


def norm_back(grad, hat, root, gain):
    scaled = grad * gain
    return root * (
        scaled
        - jnp.mean(scaled, axis=-1, keepdims=True)
        - hat * jnp.mean(scaled * hat, axis=-1, keepdims=True)
    )


def column_sum(value):
    return jnp.sum(value, axis=0, keepdims=True)


def by_head(value):
    lanes = lax.broadcasted_iota(jnp.int32, value.shape, 1)
    zero = jnp.zeros_like(value)
    return jnp.concatenate([jnp.where(lanes < 64, value, zero), jnp.where(lanes >= 64, value, zero)], axis=0)


def own_lanes(first, second):
    lanes = lax.broadcasted_iota(jnp.int32, first.shape, 1)
    return jnp.where(lanes < 64, first, second)


def attend_forward(net, w, r, s, before, started, handed, ready, gathered, pump):
    width = r.width
    scale = jnp.asarray((width // ATTENTION_HEADS) ** (-0.5), BF16)
    cross = types.SimpleNamespace()

    gather(net, w, s.all_x, lambda kind: None, started, handed)
    ready()

    def project(i, carry):
        rows = rows_of(i)
        weights = s.w_qkv[...].reshape(width, 384)
        s.qkv[rows] = (dot_nn(s.all_x[rows], weights) + s.part_bias[0:1, 0:384]).astype(BF16)
        return carry

    lax.fori_loop(0, 4, project, 0)
    cross.out = net.send(s.out_z.at[pl.ds(2 * (1 - w.y), 2)], s.w_out.at[:, w.y], w.yn)
    cross.own = net.local(s.out_z.at[pl.ds(2 * w.y, 2)], s.w_out.at[:, w.y])
    cross.own.start()
    def attend(kind, begin=0, end=2):
        def block(i, carry):
            rows = pl.ds(pl.multiple_of(w.group[kind] * 256 + i * 128, 128), 128)
            both = by_head(s.qkv[rows, 0:128] * scale)
            mask = r.docs_col[rows, 0:1] == r.docs_row[0:1, :]
            raw_both = dot_nt(both, s.qkv[:, 128:256])
            probs, logs = [], []
            for h in range(2):
                raw = jnp.where(mask, raw_both[h * 128 : (h + 1) * 128], NEGATIVE)
                top = jnp.max(raw, axis=-1, keepdims=True)
                weight = jnp.exp(raw - top)
                mass = jnp.sum(weight, axis=-1, keepdims=True)
                probs.append((weight * (1.0 / mass)).astype(BF16))
                logs.append(top + jnp.log(mass))
            total = dot_nn(jnp.concatenate(probs, axis=0), s.qkv[:, 256:384])
            s.context[rows] = own_lanes(total[0:128], total[128:256]).astype(BF16)
            s.logs[rows] = own_lanes(
                jnp.broadcast_to(logs[0], (128, 128)), jnp.broadcast_to(logs[1], (128, 128))
            )
            return carry

        lax.fori_loop(begin, end, block, 0)

    def part(slot):
        return dot_nn(s.context[rows_of(slot, 128)], s.w_out[...].reshape(128, width))

    reduce = Reduce(net, w, r, part)
    attend(DIAG)
    cross.out.wait_recv()
    cross.own.wait()
    reduce.produce(DIAG)
    attend(XN, 0, 1)
    reduce.diag()
    attend(XN, 1, 2)
    reduce.produce(XN)
    attend(YN)
    reduce.produce(YN)
    reduce.first()
    gathered()
    pump()
    attend(OWN)
    reduce.produce(OWN)
    reduce.second()
    hat, root = norm_parts(before() + reduce.total() + s.vec[BO : BO + 1])
    normed = hat * s.vec[G1 : G1 + 1] + s.vec[S1 : S1 + 1]
    r.normed[...] = normed
    s.all_n[rows_of(w.slot, 128)] = normed.astype(BF16)
    s.hat_one[...] = hat
    s.root_one[...] = jnp.broadcast_to(root, (128, 128))
    net.drain()


def feed_forward(net, w, r, s, ready_in, ready_ffo, pump):
    def part(slot):
        return dot_nn(s.inner[rows_of(slot, 128)], s.w_ffo[...].reshape(r.share, r.width))

    reduce = Reduce(net, w, r, part)

    def on_group(kind):
        weights = s.w_in[...].reshape(r.width, r.share)
        r.pre[...] = dot_nn(s.all_n[rows_of(w.group[kind])], weights) + s.part_bias[1:2, 0 : r.share]

        def block(i, carry):
            here = pl.ds(pl.multiple_of(i * 32, 32), 32)
            there = pl.ds(pl.multiple_of(w.group[kind] * 256 + i * 32, 32), 32)
            pre = r.pre[here]
            cdf = 0.5 * (1.0 + lax.erf(pre * (0.5**0.5)))
            s.inner[there] = (pre * cdf).astype(BF16)
            bell = jnp.exp(pre * pre * (-0.5)) * ((2.0 * math.pi) ** (-0.5))
            s.slope[there] = (cdf + pre * bell).astype(BF16)
            return carry

        lax.fori_loop(0, 8, block, 0)
        if kind == YN:
            ready_ffo()
            reduce.produce(XN)
            reduce.produce(YN)
            reduce.first()

    gather(net, w, s.all_n, on_group, lambda: pump(0), ready_in)
    reduce.produce(DIAG)
    reduce.diag()
    reduce.produce(OWN)
    reduce.second()
    pump(1)
    hat, root = norm_parts(r.normed[...] + reduce.total() + s.vec[B2 : B2 + 1])
    s.hat_two[...] = hat
    s.root_two[...] = jnp.broadcast_to(root, (128, 128))
    net.drain()
    return hat * s.vec[G2 : G2 + 1] + s.vec[S2 : S2 + 1]


def put_row(ref, row, value):
    for k in range(value.shape[1] // 128):
        ref[row + k : row + k + 1, :] = value[:, k * 128 : (k + 1) * 128]


def feed_backward(net, w, r, s, grad, started, free, pump):
    hat = s.hat_two[...]
    back_two = norm_back(grad, hat, s.root_two[:, 0:1], s.vec[G2 : G2 + 1])
    second = back_two.astype(BF16)
    r.normed[...] = back_two
    r.all_second[rows_of(w.slot, 128)] = second

    def part(slot):
        return dot_nt(r.back_pre[rows_of(slot, 128)], s.w_in[...].reshape(r.width, r.share))

    reduce = Reduce(net, w, r, part)

    def after_start():
        put_row(s.sums, 8 * G2, column_sum(grad * hat))
        put_row(s.sums, 8 * S2, column_sum(grad))
        put_row(s.sums, 8 * B2, column_sum(second.astype(F32)))
        started()

    def on_group(kind):
        rows = rows_of(w.group[kind])
        back_inner = dot_nt(r.all_second[rows], s.w_ffo[...].reshape(r.share, r.width))
        r.back_pre[rows] = (back_inner * s.slope[rows].astype(F32)).astype(BF16)
        if kind == YN:
            reduce.produce(XN)
            reduce.produce(YN)
            reduce.first()

    gather(net, w, r.all_second, on_group, after_start)
    reduce.produce(DIAG)
    reduce.diag()
    reduce.produce(OWN)
    free()

    for z in range(4):
        r.g_ffo[z] = dot_tn(s.inner[:, z * 128 : (z + 1) * 128], r.all_second[...]).astype(BF16)
    s.z_ffo = ZScatter(net, w, lambda z: r.g_ffo.at[z], s.land_ffo)
    reduce.second()

    def in_block(i, carry):
        lanes = pl.ds(pl.multiple_of(i * 256, 256), 256)
        piece = dot_tn(s.all_n[:, lanes], r.back_pre[...]).astype(BF16)
        r.g_in[i] = piece.reshape(4, 64, r.share)
        return carry

    lax.fori_loop(0, 4, in_block, 0)
    s.z_in = ZScatter(net, w, lambda z: r.g_in.at[:, z], s.land_in)
    put_row(s.sums, 50, column_sum(r.back_pre[...].astype(F32)))
    pump()
    grad_one = r.normed[...] + reduce.total()
    hat = s.hat_one[...]
    back_one = norm_back(grad_one, hat, s.root_one[:, 0:1], s.vec[G1 : G1 + 1])
    branch = back_one.astype(BF16)
    r.back_one[...] = back_one
    r.all_branch[rows_of(w.slot, 128)] = branch

    def sums():
        put_row(s.sums, 8 * G1, column_sum(grad_one * hat))
        put_row(s.sums, 8 * S1, column_sum(grad_one))
        put_row(s.sums, 8 * BO, column_sum(branch.astype(F32)))

    return sums


def attend_backward(net, w, r, s, started, pump, done):
    width = r.width
    scale = jnp.asarray((width // ATTENTION_HEADS) ** (-0.5), BF16)

    def after_start():
        r.sum_k[...] = jnp.zeros_like(r.sum_k)
        r.sum_v[...] = jnp.zeros_like(r.sum_v)
        started()

    def on_group(kind):
        rows = rows_of(w.group[kind])
        out_w = s.w_out[...].reshape(128, width)
        r.back_context[rows] = dot_nt(r.all_branch[rows], out_w).astype(BF16)

        def block(i, carry):
            here = pl.ds(pl.multiple_of(w.group[kind] * 256 + i * 128, 128), 128)
            query = by_head(s.qkv[here, 0:128] * scale)
            upstream = by_head(r.back_context[here])
            mask = r.docs_col[here, 0:1] == r.docs_row[0:1, :]
            raw_both = dot_nt(query, s.qkv[:, 128:256])
            back_both = dot_nt(upstream, s.qkv[:, 256:384])
            probs_both, scores_both = [], []
            for h in range(2):
                rows_h = slice(h * 128, (h + 1) * 128)
                raw = jnp.where(mask, raw_both[rows_h], NEGATIVE)
                probs = jnp.exp(raw - s.logs[here, h * 64 : h * 64 + 1])
                back = back_both[rows_h]
                delta = jnp.sum(probs * back, axis=-1, keepdims=True)
                scores_both.append((probs * (back - delta)).astype(BF16))
                probs_both.append(probs.astype(BF16))
            scores = jnp.concatenate(scores_both, axis=0)
            total = dot_nn(scores, s.qkv[:, 128:256])
            r.sum_k[...] += dot_tn(scores, query)
            r.sum_v[...] += dot_tn(jnp.concatenate(probs_both, axis=0), upstream)
            total = own_lanes(total[0:128], total[128:256])
            r.back_qkv[here, 0:128] = (total * scale.astype(F32)).astype(BF16)
            return carry

        lax.fori_loop(0, 2, block, 0)

    gather(net, w, r.all_branch, on_group, after_start)
    r.back_qkv[:, 128:256] = r.sum_k[...].astype(BF16)
    r.back_qkv[:, 256:384] = r.sum_v[...].astype(BF16)

    def part(slot):
        return dot_nt(r.back_qkv[rows_of(slot, 128)], s.w_qkv[...].reshape(width, 384))

    reduce = Reduce(net, w, r, part)
    reduce.produce(DIAG)
    reduce.produce(XN)
    reduce.produce(YN)
    reduce.diag()
    reduce.first()
    put_row(s.sums, 48, column_sum(r.back_qkv[:, 0:128].astype(F32)))
    put_row(s.sums, 49, column_sum(r.back_qkv[:, 256:384].astype(F32)))
    pump(0)

    def qkv_block(i, carry):
        lanes = pl.ds(pl.multiple_of(i * 256, 256), 256)
        piece = dot_tn(s.all_x[:, lanes], r.back_qkv[...]).astype(BF16)
        s.g_qkv[i] = piece.reshape(4, 2, 32, 384)
        return carry

    lax.fori_loop(0, 4, qkv_block, 0)
    s.z_qkv = ZScatter(net, w, lambda z: s.g_qkv.at[:, z], s.land_qkv)
    reduce.produce(OWN)
    reduce.second()
    r.g_out[...] = dot_tn(s.context[...], r.all_branch[...]).astype(BF16).reshape(2, 2, 32, width)
    cross = net.send(r.g_out.at[:, 1 - w.y], s.g_out_z.at[pl.ds(2 * w.y, 2)], w.yn)
    kept = net.local(r.g_out.at[:, w.y], s.g_out_z.at[pl.ds(2 * w.y, 2)])
    kept.start()
    pump(1)
    grad = r.back_one[...] + reduce.total()
    done(grad)
    kept.wait()
    cross.wait_recv()
    s.z_out = ZScatter(net, w, lambda z: s.g_out_z.at[z], s.land_out)


FLAT_ROWS = 96


def whole_kernel(r):
    net = Net(r.ssem, r.rsem, r.lsem)
    w = place()
    layers = len(r.layer)
    first, last = r.layer[0], r.layer[-1]
    width, share = r.width, r.share
    unit = share // 4
    r.docs_mine[...] = jnp.broadcast_to(r.docs[...], (8, 128)).astype(F32)

    def pack_qkv(layer):
        for p in range(8):
            for k in range(3):
                lanes = slice(k * width + p * 128, k * width + (p + 1) * 128)
                r.layer[layer].qkv_parts[p // 2, p % 2, :, k * 128 : (k + 1) * 128] = r.qkv_in[layer, :, lanes]

    def pack_inner(layer):
        for p in range(8):
            for z in range(4):
                at = ((p // 2) * 8 + z * 2 + p % 2) * unit
                r.layer[layer].in_parts[p // 2, p % 2, :, z * unit : (z + 1) * unit] = r.inner_in[
                    layer, :, at : at + unit
                ]

    owner = w.d * 8 + w.z * 2 + w.y
    smalls = ((r.biases, r.n_bias, 0, 3), (r.norm_gains, r.n_gain, 3, 1), (r.value_bias, r.n_value, 4, 1))

    def shifted(size, rows):
        j = lax.broadcasted_iota(jnp.int32, (size, rows * 128), 0)
        k = lax.broadcasted_iota(jnp.int32, (size, rows * 128), 1)
        return jnp.where(k == j + lax.rem(owner * size, 128), 1.0, 0.0)

    def pack_vectors():
        r.vec_f[...] = jnp.zeros_like(r.vec_f)
        for ref, size, row, rows in smalls:
            placed = dot_nn(ref[...], shifted(size, rows).astype(BF16))
            for layer in range(layers):
                for k in range(rows):
                    at = 5 * layer + row + k
                    r.vec_f[at : at + 1, :] = placed[layer : layer + 1, k * 128 : (k + 1) * 128]
        r.vec_in[...] = r.vec_f[...].astype(BF16)

    def unpack_vectors():
        for (_, size, _, rows), base, out in zip(
            smalls, (0, 72, 88), (r.bias_grad, r.gain_grad, r.value_grad)
        ):
            for layer in range(layers):
                begin = layer * FLAT_ROWS + base + lax.div(owner * size, 128)
                for k in range(rows):
                    r.lined[layer : layer + 1, k * 128 : (k + 1) * 128] = r.vectors[pl.ds(begin + k, 1), :]
            out[...] = lax.dot_general(
                r.lined[:, 0 : rows * 128],
                shifted(size, rows),
                (((1,), (1,)), ((), ())),
                precision=lax.Precision.HIGHEST,
                preferred_element_type=F32,
            )[0:layers]

    def of_part(ref):
        return lambda p: ref.at[lax.div(p, 2), lax.rem(p, 2)]

    met = net.greet(w)
    pack_vectors()
    pack_qkv(0)
    pack_inner(0)
    met()
    parts = net.plane_swap(w, of_part(first.qkv_parts), of_part(first.qkv_piece))
    hidden = net.swap(w, r.hidden, r.hidden_row)
    docs = net.swap(w, r.docs_mine, r.docs_own)
    vec = net.z_all(w, r.vec_in, lambda z: r.vec_z.at[z])
    parts()
    first.zg_qkv = ZGather(net, w, first.qkv_piece, lambda z: first.w_qkv.at[:, z])
    first.zg_out = ZGather(net, w, r.out_in.at[0], lambda z: first.out_z.at[z])
    first.in_parted = net.plane_swap(w, of_part(first.in_parts), of_part(first.in_piece))
    vec()
    spread = net.plane_swap(w, lambda p: r.vec_z, lambda p: r.vec_all.at[p])
    docs()
    docs = net.plane_swap(w, lambda p: r.docs_own, lambda p: r.docs_all.at[p])
    hidden()
    first.all_x[rows_of(w.slot, 128)] = r.hidden_row[...]

    def unpack():
        spread()
        r.flat[...] = jnp.zeros_like(r.flat)
        for p in range(8):
            for z in range(4):
                owner = (p // 2) * 8 + z * 2 + p % 2
                piece = r.vec_all[p, z].astype(F32)
                for layer in range(layers):
                    base = layer * FLAT_ROWS
                    at = base + r.n_bias * owner // 128
                    r.flat[at : at + 3, :] += piece[5 * layer : 5 * layer + 3]
                    at = base + 72 + r.n_gain * owner // 128
                    r.flat[at : at + 1, :] += piece[5 * layer + 3 : 5 * layer + 4]
                    at = base + 88 + r.n_value * owner // 128
                    r.flat[at : at + 1, :] += piece[5 * layer + 4 : 5 * layer + 5]
        for layer in range(layers):
            s, base = r.layer[layer], layer * FLAT_ROWS
            for row, name in ((G1, 72), (S1, 56), (BO, 8), (G2, 80), (S2, 64), (B2, 48)):
                for k in range(8):
                    s.vec[row : row + 1, k * 128 : (k + 1) * 128] = r.flat[
                        base + name + k : base + name + k + 1, :
                    ]
            s.part_bias[...] = jnp.zeros_like(s.part_bias)
            s.part_bias[0:1, 0:128] = r.flat[pl.ds(base + w.part, 1), :]
            s.part_bias[0:1, 256:384] = r.flat[pl.ds(base + 88 + w.part, 1), :]
            for z in range(4):
                s.part_bias[1:2, z * unit : (z + 1) * unit] = r.flat[
                    pl.ds(base + 16 + 8 * w.d + 2 * z + w.y, 1), :
                ]
        docs()
        for p in range(8):
            slot = (p // 4) * 4 + (p % 2) * 2 + (p // 2) % 2
            numbers = r.docs_all[p]
            r.docs_row[:, slot * 128 : (slot + 1) * 128] = numbers
            r.docs_col[slot * 128 : (slot + 1) * 128, :] = jnp.broadcast_to(numbers[0:1], (128, 128)).T

    def bring_attention(layer):
        s = r.layer[layer]
        s.zg_qkv = ZGather(net, w, s.qkv_piece, lambda z: s.w_qkv.at[:, z])
        s.zg_out = ZGather(net, w, r.out_in.at[layer], lambda z: s.out_z.at[z])

    def bring_in(layer):
        s = r.layer[layer]
        s.zg_qkv.poll()
        s.zg_out.poll()
        s.zg_in = ZGather(net, w, s.in_piece, lambda z: s.w_in.at[:, z])
        s.zg_ffo = ZGather(net, w, r.ffo_in.at[layer], lambda z: s.w_ffo.at[z])

    def bring_ffo(layer):
        s = r.layer[layer]
        s.zg_in.poll()

    swaps = types.SimpleNamespace()
    for layer in range(layers):
        s = r.layer[layer]

        def started(layer=layer):
            if layer == 0:
                unpack()

        def handed(layer=layer, s=s):
            if layer == 0:
                s.in_parted()
                bring_in(0)

        def ready(s=s):
            s.zg_qkv.wait()
            s.zg_out.wait()

        def gathered(layer=layer):
            if layer + 1 < layers:
                n = r.layer[layer + 1]
                pack_qkv(layer + 1)
                pack_inner(layer + 1)
                n.qkv_parted = net.plane_swap(w, of_part(n.qkv_parts), of_part(n.qkv_piece))
                n.in_parted = net.plane_swap(w, of_part(n.in_parts), of_part(n.in_piece))

        def before(layer=layer):
            return r.hidden_row[...].astype(F32) if layer == 0 else r.state[...]

        attend_forward(
            net, w, r, s, before, started, handed, ready, gathered, lambda layer=layer: bring_ffo(layer)
        )

        def ready_in(s=s):
            s.zg_in.wait()

        def ready_ffo(s=s):
            s.zg_ffo.wait()

        def pump(at, layer=layer, s=s):
            if at == 0:
                s.zg_ffo.poll()
                if layer + 1 < layers:
                    r.layer[layer + 1].qkv_parted()
                    r.layer[layer + 1].in_parted()
                    bring_attention(layer + 1)
            elif layer + 1 < layers:
                bring_in(layer + 1)
            else:
                swaps.grad = net.swap(w, r.out_grad, r.grad_row)

        state = feed_forward(net, w, r, s, ready_in, ready_ffo, pump)
        r.state[...] = state
        if layer + 1 < layers:
            r.layer[layer + 1].all_x[rows_of(w.slot, 128)] = state.astype(BF16)
        else:
            r.state_low[...] = state.astype(BF16)
    swaps.grad()
    net.settle()
    swaps.out = net.swap(w, r.state_low, r.out)
    grad = r.grad_row[...].astype(F32)

    def vectors_out(s):
        return net.z_spread(w, s.sums, s.sums_z)

    def vectors_plane(s, wait):
        wait()
        s.sums_own[...] = s.sums[...] + s.sums_z[0] + s.sums_z[1] + s.sums_z[2]
        return net.plane_swap(w, lambda p: s.sums_own, lambda p: s.sums_all.at[p])

    def vectors_in(layer, s, wait):
        wait()
        base = layer * FLAT_ROWS
        for row, name in ((G1, 72), (S1, 56), (BO, 8), (G2, 80), (S2, 64), (B2, 48)):
            total = s.sums_all[0, 8 * row : 8 * row + 8]
            for p in range(1, 8):
                total = total + s.sums_all[p, 8 * row : 8 * row + 8]
            r.vectors[base + name : base + name + 8, :] = total
        for p in range(8):
            r.vectors[base + p : base + p + 1, :] = s.sums_all[p, 48:49]
            r.vectors[base + 88 + p : base + 89 + p, :] = s.sums_all[p, 49:50]
            for z in range(4):
                at = base + 16 + 8 * (p // 2) + 2 * z + p % 2
                r.vectors[at : at + 1, :] = s.sums_all[p, 50 + z : 51 + z]

    def send_inner(s):
        s.in_parts[...] = s.z_in.total().astype(BF16).reshape(4, 2, 32, share)
        return net.plane_swap(w, of_part(s.in_parts), of_part(s.in_piece))

    def send_qkv(s):
        s.qkv_parts[...] = s.z_qkv.total().astype(BF16)
        return net.plane_swap(w, of_part(s.qkv_parts), of_part(s.qkv_piece))

    def place_inner(layer, s, wait):
        wait()
        for p in range(8):
            for z in range(4):
                at = ((p // 2) * 8 + z * 2 + p % 2) * unit
                r.in_grad[layer, :, at : at + unit] = s.in_piece[
                    p // 2, p % 2, :, z * unit : (z + 1) * unit
                ].astype(F32)

    def place_qkv(layer, s, wait):
        wait()
        for p in range(8):
            for k in range(3):
                lanes = slice(k * width + p * 128, k * width + (p + 1) * 128)
                r.qkv_grad[layer, :, lanes] = s.qkv_piece[
                    p // 2, p % 2, :, k * 128 : (k + 1) * 128
                ].astype(F32)

    for layer in reversed(range(layers)):
        s = r.layer[layer]
        a = r.layer[layer + 1] if layer + 1 < layers else None
        s.sums[...] = jnp.zeros_like(s.sums)

        def feed_started(layer=layer, a=a):
            if a is not None:
                r.ffo_grad[layer + 1] = a.z_ffo.total()
                a.in_wait = send_inner(a)

        def free(a=a):
            if a is not None:
                a.z_ffo.settle()
                a.z_in.settle()
                a.z_qkv.poll()
                a.z_out.poll()

        def feed_pump(a=a):
            if a is not None:
                a.vec_wait = vectors_plane(a, a.vec_wait)

        sums = feed_backward(net, w, r, s, grad, feed_started, free, feed_pump)
        if a is None:
            swaps.out()
        net.drain()

        def back_started(layer=layer, a=a, sums=sums):
            sums()
            if a is not None:
                place_inner(layer + 1, a, a.in_wait)
                r.out_grad_w[layer + 1] = a.z_out.total()
                a.qkv_wait = send_qkv(a)
                vectors_in(layer + 1, a, a.vec_wait)

        def back_pump(at, s=s):
            if at == 0:
                s.z_ffo.poll()
                s.vec_wait = vectors_out(s)
            else:
                s.z_in.poll()

        def done(grad, layer=layer):
            if layer:
                r.state[...] = grad
            else:
                r.state_low[...] = grad.astype(BF16)
                swaps.back = net.swap(w, r.state_low, r.input_grad)

        attend_backward(net, w, r, s, back_started, back_pump, done)
        if layer:
            grad = r.state[...]
            net.drain()
    r.ffo_grad[0] = first.z_ffo.total()
    first.in_wait = send_inner(first)
    if layers > 1:
        place_qkv(1, r.layer[1], r.layer[1].qkv_wait)
    first.vec_wait = vectors_plane(first, first.vec_wait)
    first.z_qkv.poll()
    first.z_out.poll()
    place_inner(0, first, first.in_wait)
    vectors_in(0, first, first.vec_wait)
    first.qkv_wait = send_qkv(first)
    r.out_grad_w[0] = first.z_out.total()
    swaps.back()
    unpack_vectors()
    place_qkv(0, first, first.qkv_wait)
    net.settle()


def plane_body(
    hidden_in,
    document_index,
    out_grad,
    qkv_weight,
    value_bias,
    attention_output_weight,
    ffn_in_weight,
    ffn_out_weight,
    biases,
    norm_gains,
):
    layers = qkv_weight.shape[0]
    width = hidden_in.shape[1]
    inner = ffn_in_weight.shape[2]
    share = inner // 8
    n_bias, n_gain, n_value = biases.shape[1], norm_gains.shape[1], value_bias.shape[1]

    ins = dict(
        hidden=hidden_in,
        docs=document_index,
        out_grad=out_grad,
        qkv_in=qkv_weight,
        out_in=attention_output_weight,
        inner_in=ffn_in_weight,
        ffo_in=ffn_out_weight,
        biases=biases,
        norm_gains=norm_gains,
        value_bias=value_bias,
    )
    outs = dict(
        out=((128, width), BF16),
        input_grad=((128, width), BF16),
        qkv_grad=(qkv_weight.shape, F32),
        out_grad_w=(attention_output_weight.shape, F32),
        in_grad=(ffn_in_weight.shape, F32),
        ffo_grad=(ffn_out_weight.shape, F32),
        bias_grad=((layers, n_bias), F32),
        gain_grad=((layers, n_gain), F32),
        value_grad=((layers, n_value), F32),
    )
    far = dict(hidden=1, out_grad=1, ffo_in=1, out_in=1, out=1, input_grad=1)
    whole = (1024, width)
    shared = dict(
        hidden_row=((128, width), BF16),
        grad_row=((128, width), BF16),
        docs_mine=((8, 128), F32),
        docs_own=((8, 128), F32),
        docs_all=((8, 8, 128), F32),
        docs_row=((8, 1024), F32),
        docs_col=((1024, 128), F32),
        vec_f=((16, 128), F32),
        vec_in=((16, 128), BF16),
        lined=((8, 384), F32),
        vectors=((layers * FLAT_ROWS, 128), F32),
        vec_z=((4, 16, 128), BF16),
        vec_all=((8, 4, 16, 128), BF16),
        flat=((layers * FLAT_ROWS, 128), F32),
        normed=((128, width), F32),
        state=((128, width), F32),
        state_low=((128, width), BF16),
        back_one=((128, width), F32),
        pre=((256, share), F32),
        all_second=(whole, BF16),
        all_branch=(whole, BF16),
        back_pre=((1024, share), BF16),
        back_context=((1024, 128), BF16),
        back_qkv=((1024, 384), BF16),
        sum_k=((1024, 128), F32),
        sum_v=((1024, 128), F32),
        g_out=((2, 2, 32, width), BF16),
        g_ffo=((4, 128, width), BF16),
        g_in=((4, 4, 64, share), BF16),
        core_out=((4, 128, width), BF16),
        core_in=((4, 128, width), BF16),
        keep=((4, 128, width), F32),
        across=((128, width), BF16),
        via_x=((64, width), BF16),
        via_y=((64, width), BF16),
        out_x=((128, width), BF16),
        out_y=((128, width), BF16),
        in_x=((128, width), BF16),
        in_y=((128, width), BF16),
    )
    each = dict(
        qkv_parts=((4, 2, 32, 384), BF16),
        qkv_piece=((4, 2, 32, 384), BF16),
        in_parts=((4, 2, 32, share), BF16),
        in_piece=((4, 2, 32, share), BF16),
        w_qkv=((4, 4, 2, 32, 384), BF16),
        w_in=((4, 4, 2, 32, share), BF16),
        w_ffo=((4, 128, width), BF16),
        out_z=((4, 32, width), BF16),
        w_out=((2, 2, 32, width), BF16),
        vec=((8, width), F32),
        part_bias=((8, width), F32),
        all_x=(whole, BF16),
        qkv=((1024, 384), BF16),
        context=((1024, 128), BF16),
        logs=((1024, 128), F32),
        all_n=(whole, BF16),
        inner=((1024, share), BF16),
        slope=((1024, share), BF16),
        hat_one=((128, width), F32),
        root_one=((128, 128), F32),
        hat_two=((128, width), F32),
        root_two=((128, 128), F32),
        g_qkv=((4, 4, 2, 32, 384), BF16),
        g_out_z=((4, 32, width), BF16),
        land_ffo=((4, 128, width), BF16),
        land_in=((4, 4, 64, share), BF16),
        land_qkv=((4, 4, 2, 32, 384), BF16),
        land_out=((4, 32, width), BF16),
        sums=((56, 128), F32),
        sums_z=((3, 56, 128), F32),
        sums_own=((56, 128), F32),
        sums_all=((8, 56, 128), F32),
    )

    def kernel(*refs):
        refs = list(refs)

        def take(names):
            return dict(zip(names, [refs.pop(0) for _ in names]))

        r = types.SimpleNamespace(
            width=width, share=share, n_bias=n_bias, n_gain=n_gain, n_value=n_value, **take(ins), **take(outs), **take(shared)
        )
        r.layer = [types.SimpleNamespace(**take(each)) for _ in range(layers)]
        r.ssem, r.rsem, r.lsem = refs
        whole_kernel(r)

    def held(items):
        return [VMEM(shape, dtype) for shape, dtype in items.values()]

    results = pl.pallas_call(
        kernel,
        out_shape=[jax.ShapeDtypeStruct(shape, dtype) for shape, dtype in outs.values()],
        in_specs=[pl.BlockSpec(memory_space=pl.ANY if name in far else VMEM) for name in ins],
        out_specs=[pl.BlockSpec(memory_space=pl.ANY if name in far else VMEM) for name in outs],
        scratch_shapes=[
            *held(shared),
            *(held(each) * layers),
            pltpu.SemaphoreType.DMA((COPIES,)),
            pltpu.SemaphoreType.DMA((COPIES,)),
            pltpu.SemaphoreType.DMA((48,)),
        ],
        compiler_params=pltpu.CompilerParams(
            collective_id=0, has_side_effects=True, vmem_limit_bytes=VMEM_LIMIT
        ),
    )(*ins.values())
    out, input_grad, g_qkv, g_out, g_in, g_ffo, g_bias, g_gain, g_value = results
    return in_place((out, input_grad, g_qkv, g_value, g_out, g_in, g_ffo, g_bias, g_gain))


def in_place(results):
    last = len(results)

    def kernel(*refs):
        sems = refs[-1]
        copies = [
            pltpu.make_async_copy(refs[k], refs[last + k], sems.at[k]) for k in range(last) if k != 1
        ]
        for copy in copies:
            copy.start()
        refs[last + 1][...] = refs[1][...].astype(F32)
        for copy in copies:
            copy.wait()

    return pl.pallas_call(
        kernel,
        out_shape=[jax.ShapeDtypeStruct(v.shape, F32 if k == 1 else v.dtype) for k, v in enumerate(results)],
        in_specs=[pl.BlockSpec(memory_space=VMEM)] * last,
        out_specs=[pl.BlockSpec(memory_space=VMEM if k == 1 else pl.ANY) for k in range(last)],
        scratch_shapes=[pltpu.SemaphoreType.DMA((last,))],
    )(*results)


def fits_plane(mesh):
    return mesh.shape[DP] == 4 and mesh.shape[CTX] == 8


def solution(mesh):
    return jax.shard_map(
        plane_body if fits_plane(mesh) else body,
        mesh=mesh,
        in_specs=(
            P(BOTH, None),
            P(DP, CTX),
            P(BOTH, None),
            P(None, BOTH, None),
            P(None, BOTH),
            P(None, BOTH, None),
            P(None, BOTH, None),
            P(None, BOTH, None),
            P(None, BOTH),
            P(None, BOTH),
        ),
        out_specs=(
            P(BOTH, None),
            P(BOTH, None),
            P(None, BOTH, None),
            P(None, BOTH),
            P(None, BOTH, None),
            P(None, BOTH, None),
            P(None, BOTH, None),
            P(None, BOTH),
            P(None, BOTH),
        ),
        check_vma=False,
    )
```

```python
import math
import types

import jax
import jax.numpy as jnp
from jax import lax
from jax.experimental import pallas as pl
from jax.experimental.pallas import tpu as pltpu
from jax.sharding import PartitionSpec as P

ATTENTION_HEADS = 16


DP, CTX = "dp", "ctx"
BOTH = (DP, CTX)

QUERY_KEY, TO_QUERY, TO_KEY = "qhd,khd->hqk", "hqk,khd->qhd", "hqk,qhd->khd"
EPS = 1e-12
NEGATIVE = -1e30


def norm_rows(resid, gain, shift):
    mean = jnp.mean(resid, axis=-1, keepdims=True)
    centered = resid - mean
    variance = jnp.mean(centered * centered, axis=-1, keepdims=True)
    return centered * lax.rsqrt(variance + EPS) * gain + shift


def exact_gelu(value):
    return jax.nn.gelu(value, approximate=False)


def cross(left, right_operand):
    return lax.dot_general(
        left, right_operand, (((0,), (0,)), ((), ())), preferred_element_type=jnp.float32
    )


def back_product(upstream, weight):
    return lax.dot_general(
        upstream, weight, (((1,), (1,)), ((), ())), preferred_element_type=jnp.float32
    )


def by_blocks(step_fn, carry, pieces, token_block):
    count = pieces[0].shape[0]

    def turn(index, state):
        offset = index * token_block
        parts = tuple((lax.dynamic_slice_in_dim(item, offset, token_block, 0) for item in pieces))
        return step_fn(state, parts, offset)

    return lax.fori_loop(0, count // token_block, turn, carry)


def unpack(fetched, width, inner):
    w_qkv, w_out, w_in, w_ffo, value_vec, bias_all, gains = fetched
    value_vec = value_vec.astype(jnp.float32)
    bias_all = bias_all.astype(jnp.float32)
    gains = gains.astype(jnp.float32)
    query_bias = bias_all[0:width]
    out_bias = bias_all[width : 2 * width]
    inner_bias = bias_all[2 * width : 2 * width + inner]
    ffn_bias = bias_all[2 * width + inner : 3 * width + inner]
    shift_one = bias_all[3 * width + inner : 4 * width + inner]
    shift_two = bias_all[4 * width + inner : 5 * width + inner]
    return (
        w_qkv,
        w_out,
        w_in,
        w_ffo,
        value_vec,
        query_bias,
        out_bias,
        inner_bias,
        ffn_bias,
        shift_one,
        shift_two,
        gains[0:width],
        gains[width : 2 * width],
    )


def masked_scores(query_heads, key_piece, seg_own, segment_row, start, scale):
    count = key_piece.shape[0]
    heads = query_heads.shape[1]
    split_key_heads = key_piece.reshape(count, heads, query_heads.shape[2])
    seg_keys = lax.dynamic_slice_in_dim(segment_row, start, count, 0)
    mask = (seg_own[:, None] == seg_keys[None, :])[None]
    raw = (
        jnp.einsum(QUERY_KEY, query_heads, split_key_heads, preferred_element_type=jnp.float32)
        * scale
    )
    return (jnp.where(mask, raw, NEGATIVE), mask, split_key_heads)


def body(
    hidden_in,
    document_index,
    out_grad,
    qkv_weight,
    value_bias,
    attention_output_weight,
    ffn_in_weight,
    ffn_out_weight,
    biases,
    norm_gains,
):
    layers = qkv_weight.shape[0]
    width = qkv_weight.shape[2] // 3
    inner = ffn_in_weight.shape[2]
    heads = ATTENTION_HEADS
    head_width = width // heads
    scale = head_width ** (-0.5)
    rows = hidden_in.shape[0]
    seg_own = document_index[0]
    segment_row = lax.all_gather(document_index, CTX, axis=1, tiled=True)[0]
    row_len = segment_row.shape[0]
    state = hidden_in.astype(jnp.float32)
    saved = []
    for layer in range(layers):
        fetched = (
            lax.all_gather(qkv_weight[layer], BOTH, axis=0, tiled=True),
            lax.all_gather(attention_output_weight[layer], BOTH, axis=0, tiled=True),
            lax.all_gather(ffn_in_weight[layer], BOTH, axis=0, tiled=True),
            lax.all_gather(ffn_out_weight[layer], BOTH, axis=0, tiled=True),
            lax.all_gather(value_bias[layer], BOTH, axis=0, tiled=True),
            lax.all_gather(biases[layer], BOTH, axis=0, tiled=True),
            lax.all_gather(norm_gains[layer], BOTH, axis=0, tiled=True),
        )
        (
            w_qkv,
            w_out,
            w_in,
            w_ffo,
            value_vec,
            query_bias,
            out_bias,
            inner_bias,
            ffn_bias,
            shift_one,
            shift_two,
            gain_one,
            gain_two,
        ) = unpack(fetched, width, inner)
        state_low = state.astype(jnp.bfloat16)
        qkv_bias = jnp.concatenate([query_bias, jnp.zeros_like(query_bias), value_vec])
        qkv_low = (jnp.dot(state_low, w_qkv, preferred_element_type=jnp.float32) + qkv_bias).astype(
            jnp.bfloat16
        )
        query_heads = qkv_low[:, 0:width].reshape(rows, heads, head_width)
        key_low = qkv_low[:, width : 2 * width]
        value_low = qkv_low[:, 2 * width : 3 * width]

        def stats_step(carry, parts, start):
            top, total = carry
            raw, mask, split_key_heads = masked_scores(
                query_heads, parts[0], seg_own, segment_row, start, scale
            )
            new_top = jnp.maximum(top, jnp.max(raw, axis=-1))
            weights = jnp.where(mask, jnp.exp(raw - new_top[:, :, None]), 0.0)
            return (new_top, total * jnp.exp(top - new_top) + jnp.sum(weights, axis=-1))

        stats_init = (
            jnp.full((heads, rows), NEGATIVE, jnp.float32),
            jnp.zeros((heads, rows), jnp.float32),
        )
        held_pair = None
        top, total = by_blocks(
            stats_step, stats_init, (lax.all_gather(key_low, CTX, axis=0, tiled=True),), rows
        )
        log_total = top + jnp.log(total)

        def value_step(carry, parts, start):
            context_acc, exact_acc = carry
            raw, mask, split_key_heads = masked_scores(
                query_heads, parts[0], seg_own, segment_row, start, scale
            )
            split_value_heads = parts[1].reshape(parts[1].shape[0], heads, head_width)
            probs = jnp.where(mask, jnp.exp(raw - log_total[:, :, None]), 0.0)
            probs_low = probs.astype(jnp.bfloat16)
            residue_low = (probs - probs_low.astype(jnp.float32)).astype(jnp.bfloat16)
            part_low = jnp.einsum(
                TO_QUERY, probs_low, split_value_heads, preferred_element_type=jnp.float32
            )
            part_fix = jnp.einsum(
                TO_QUERY, residue_low, split_value_heads, preferred_element_type=jnp.float32
            )
            return (context_acc + part_low, exact_acc + part_fix)

        value_init = (
            jnp.zeros((rows, heads, head_width), jnp.float32),
            jnp.zeros((rows, heads, head_width), jnp.float32),
        )
        context, correction = by_blocks(
            value_step,
            value_init,
            (
                lax.all_gather(key_low, CTX, axis=0, tiled=True),
                lax.all_gather(value_low, CTX, axis=0, tiled=True),
            ),
            rows,
        )
        context_exact = (context + correction).reshape(rows, width)
        context = context.reshape(rows, width)
        context_low = context.astype(jnp.bfloat16)
        resid_one = (
            state + jnp.dot(context_low, w_out, preferred_element_type=jnp.float32) + out_bias
        )
        normed = norm_rows(resid_one, gain_one, shift_one)
        normed_low = normed.astype(jnp.bfloat16)
        pre = jnp.dot(normed_low, w_in, preferred_element_type=jnp.float32) + inner_bias
        inner_low = exact_gelu(pre).astype(jnp.bfloat16)
        resid_two = (
            normed + jnp.dot(inner_low, w_ffo, preferred_element_type=jnp.float32) + ffn_bias
        )
        saved.append(
            (
                fetched,
                state_low,
                qkv_low,
                log_total,
                context_exact,
                context_low,
                resid_one,
                normed_low,
                pre,
                inner_low,
                resid_two,
                held_pair,
            )
        )
        state = norm_rows(resid_two, gain_two, shift_two)
    upstream = out_grad.astype(jnp.float32)
    per_layer = []
    for layer in reversed(range(layers)):
        (
            fetched,
            state_low,
            qkv_low,
            log_total,
            context_exact,
            context_low,
            resid_one,
            normed_low,
            pre,
            inner_low,
            resid_two,
            held_pair,
        ) = saved[layer]
        weights_now = (
            lax.all_gather(qkv_weight[layer], BOTH, axis=0, tiled=True),
            lax.all_gather(attention_output_weight[layer], BOTH, axis=0, tiled=True),
            lax.all_gather(ffn_in_weight[layer], BOTH, axis=0, tiled=True),
            lax.all_gather(ffn_out_weight[layer], BOTH, axis=0, tiled=True),
            lax.all_gather(value_bias[layer], BOTH, axis=0, tiled=True),
            lax.all_gather(biases[layer], BOTH, axis=0, tiled=True),
            lax.all_gather(norm_gains[layer], BOTH, axis=0, tiled=True),
        )
        (
            w_qkv,
            w_out,
            w_in,
            w_ffo,
            value_vec,
            query_bias,
            out_bias,
            inner_bias,
            ffn_bias,
            shift_one,
            shift_two,
            gain_one,
            gain_two,
        ) = unpack(weights_now, width, inner)
        query_low = qkv_low[:, 0:width]
        query_heads = query_low.reshape(rows, heads, head_width)
        key_low = qkv_low[:, width : 2 * width]
        value_low = qkv_low[:, 2 * width : 3 * width]
        unused_two, pull_two = jax.vjp(norm_rows, resid_two, gain_two, shift_two)
        back_two, back_gain_two, back_shift_two = pull_two(upstream)
        back_second = back_two.astype(jnp.bfloat16)
        grad_second = cross(inner_low, back_second)
        back_inner = back_product(back_second, w_ffo)
        unused_pre, pull_gelu = jax.vjp(exact_gelu, pre)
        back_pre = pull_gelu(back_inner)[0].astype(jnp.bfloat16)
        grad_first = cross(normed_low, back_pre)
        back_normed = back_two + back_product(back_pre, w_in)
        normed_again, pull_one = jax.vjp(norm_rows, resid_one, gain_one, shift_one)
        back_one, back_gain_one, back_shift_one = pull_one(back_normed)
        back_branch = back_one.astype(jnp.bfloat16)
        grad_out_proj = cross(context_low, back_branch)
        back_context = back_product(back_branch, w_out).astype(jnp.bfloat16)
        context_heads_back = back_context.reshape(rows, heads, head_width)
        delta = jnp.sum(
            (back_context.astype(jnp.float32) * context_exact).reshape(rows, heads, head_width),
            axis=-1,
        ).T

        def grad_step(carry, parts, start):
            query_sum, key_sums, value_sums = carry
            count = parts[0].shape[0]
            raw, mask, split_key_heads = masked_scores(
                query_heads, parts[0], seg_own, segment_row, start, scale
            )
            split_value_heads = parts[1].reshape(count, heads, head_width)
            probs = jnp.where(mask, jnp.exp(raw - log_total[:, :, None]), 0.0)
            back_probs = jnp.einsum(
                QUERY_KEY,
                context_heads_back,
                split_value_heads,
                preferred_element_type=jnp.float32,
            )
            back_scores = (probs * (back_probs - delta[:, :, None])).astype(jnp.bfloat16)
            query_part = (
                jnp.einsum(
                    TO_QUERY, back_scores, split_key_heads, preferred_element_type=jnp.float32
                )
                * scale
            )
            key_part = (
                jnp.einsum(
                    TO_KEY, back_scores, query_heads, preferred_element_type=jnp.float32
                ).reshape(count, width)
                * scale
            )
            value_part = jnp.einsum(
                TO_KEY,
                probs.astype(jnp.bfloat16),
                context_heads_back,
                preferred_element_type=jnp.float32,
            ).reshape(count, width)
            key_sums = lax.dynamic_update_slice_in_dim(
                key_sums, lax.dynamic_slice_in_dim(key_sums, start, count, 0) + key_part, start, 0
            )
            value_sums = lax.dynamic_update_slice_in_dim(
                value_sums,
                lax.dynamic_slice_in_dim(value_sums, start, count, 0) + value_part,
                start,
                0,
            )
            return (query_sum + query_part, key_sums, value_sums)

        query_init = jnp.zeros((rows, heads, head_width), jnp.float32)
        grad_init = (
            query_init,
            jnp.zeros((row_len, width), jnp.float32),
            jnp.zeros((row_len, width), jnp.float32),
        )
        folded = by_blocks(
            grad_step,
            grad_init,
            (
                lax.all_gather(key_low, CTX, axis=0, tiled=True),
                lax.all_gather(value_low, CTX, axis=0, tiled=True),
            ),
            rows,
        )
        query_sum, key_sums, value_sums = folded
        key_own, value_own = (
            lax.psum_scatter(
                key_sums.astype(jnp.bfloat16), CTX, scatter_dimension=0, tiled=True
            ).astype(jnp.float32),
            lax.psum_scatter(
                value_sums.astype(jnp.bfloat16), CTX, scatter_dimension=0, tiled=True
            ).astype(jnp.float32),
        )
        back_qkv = jnp.concatenate(
            [query_sum.reshape(rows, width), key_own, value_own], axis=1
        ).astype(jnp.bfloat16)
        grad_qkv = cross(state_low, back_qkv)
        back_qkv_float = back_qkv.astype(jnp.float32)
        grad_value_bias = jnp.sum(back_qkv_float[:, 2 * width : 3 * width], axis=0)
        grad_bias = jnp.concatenate(
            [
                jnp.sum(back_qkv_float[:, 0:width], axis=0),
                jnp.sum(back_branch.astype(jnp.float32), axis=0),
                jnp.sum(back_pre.astype(jnp.float32), axis=0),
                jnp.sum(back_second.astype(jnp.float32), axis=0),
                back_shift_one,
                back_shift_two,
            ]
        )
        grad_gain = jnp.concatenate([back_gain_one, back_gain_two])
        upstream = back_one + back_product(back_qkv, w_qkv)
        shards = (
            lax.psum_scatter(grad_qkv, BOTH, scatter_dimension=0, tiled=True),
            lax.psum_scatter(grad_value_bias, BOTH, scatter_dimension=0, tiled=True),
            lax.psum_scatter(grad_out_proj, BOTH, scatter_dimension=0, tiled=True),
            lax.psum_scatter(grad_first, BOTH, scatter_dimension=0, tiled=True),
            lax.psum_scatter(grad_second, BOTH, scatter_dimension=0, tiled=True),
            lax.psum_scatter(grad_bias, BOTH, scatter_dimension=0, tiled=True),
            lax.psum_scatter(grad_gain, BOTH, scatter_dimension=0, tiled=True),
        )
        per_layer.append(shards)
    ordered = per_layer[::-1]
    stacked = tuple((jnp.stack([item[member] for item in ordered]) for member in range(7)))
    return (
        state.astype(jnp.bfloat16),
        upstream,
        stacked[0],
        stacked[1],
        stacked[2],
        stacked[3],
        stacked[4],
        stacked[5],
        stacked[6],
    )


MESH = pl.DeviceIdType.MESH
F32 = jnp.float32
BF16 = jnp.bfloat16
VMEM = pltpu.VMEM
VMEM_LIMIT = 62 * 2**20
PHASE, COPIES = 32, 208
OWN, XN, YN, DIAG = range(4)
G1, S1, BO, G2, S2, B2 = range(6)


def dot_nn(a, b):
    return lax.dot_general(a, b, (((1,), (0,)), ((), ())), preferred_element_type=F32)


def dot_nt(a, b):
    return lax.dot_general(a, b, (((1,), (1,)), ((), ())), preferred_element_type=F32)


def dot_tn(a, b):
    return lax.dot_general(a, b, (((0,), (0,)), ((), ())), preferred_element_type=F32)


def turned(two_bits):
    return lax.rem(two_bits, 2) * 2 + lax.div(two_bits, 2)


def place():
    d, t = lax.axis_index(DP), lax.axis_index(CTX)
    x, c = lax.div(d, 2), lax.rem(d, 2)
    z, y = lax.div(t, 2), lax.rem(t, 2)
    w = types.SimpleNamespace(d=d, x=x, c=c, z=z, y=y)
    w.part = d * 2 + y
    w.group = (x * 2 + y, (1 - x) * 2 + y, x * 2 + 1 - y, (1 - x) * 2 + 1 - y)
    w.slot = w.group[OWN] * 2 + c
    w.xn, w.yn, w.sib = ((1 - x) * 2 + c, t), (d, z * 2 + 1 - y), (x * 2 + 1 - c, t)
    w.plane = []
    for bits in range(1, 8):
        xx = 1 - x if bits & 4 else x
        cc = 1 - c if bits & 2 else c
        yy = 1 - y if bits & 1 else y
        w.plane.append(((xx * 2 + cc, z * 2 + yy), (xx * 2 + cc) * 2 + yy))
    w.zs = [(d, lax.rem(z + k, 4) * 2 + y) for k in (1, 2, 3)]
    w.far = lax.rem(z + 2, 4)
    w.up, w.down, w.over = (d, (z + 1) * 2 + y), (d, (z - 1) * 2 + y), (d, w.far * 2 + y)
    w.middle = (z == 1) | (z == 2)
    w.edge = (z == 0) | (z == 3)
    w.end = jnp.where(z == 1, 0, 3)
    w.near_end = (d, w.end * 2 + y)
    w.inside = jnp.where(z == 0, 1, 2)
    w.near_middle = (d, w.inside * 2 + y)
    w.opposite = 3 - z
    w.away = d != turned(z)
    w.home = d == turned(z)
    w.swap = (turned(z), turned(d) * 2 + y)
    return w


class Maybe:
    def __init__(self, copy, sends, receives):
        self.copy, self.sends, self.receives = copy, sends, receives

    def start(self):
        pl.when(self.sends)(self.copy.start)

    def wait_send(self):
        pl.when(self.sends)(self.copy.wait_send)

    def wait_recv(self):
        pl.when(self.receives)(self.copy.wait_recv)


class Net:
    def __init__(self, ssem, rsem, lsem):
        self.ssem, self.rsem, self.lsem = ssem, rsem, lsem
        self.sent, self.slow, self.scatters, self.at, self.near = [], [], [], PHASE, 0
        self.phase = 0

    def greet(self, w):
        barrier = pltpu.get_barrier_semaphore()
        devices = [device for device, _ in w.plane] + w.zs
        for device in devices:
            pl.semaphore_signal(barrier, inc=1, device_id=device, device_id_type=MESH)

        @pl.when(w.away)
        def _():
            pl.semaphore_signal(barrier, inc=1, device_id=w.swap, device_id_type=MESH)

        return lambda: pl.semaphore_wait(barrier, len(devices) + jnp.where(w.away, 1, 0))

    def make(self, src, dst, device, slow=True):
        at = self.at if slow else self.phase
        if slow:
            self.at += 1
        else:
            self.phase += 1
        return pltpu.make_async_remote_copy(
            src_ref=src,
            dst_ref=dst,
            send_sem=self.ssem.at[at],
            recv_sem=self.rsem.at[at],
            device_id=device,
            device_id_type=MESH,
        )

    def maybe(self, src, dst, device, sends, receives):
        copy = Maybe(self.make(src, dst, device), sends, receives)
        self.slow.append(copy)
        return copy

    def send(self, src, dst, device, slow=False):
        copy = self.make(src, dst, device, slow)
        copy.start()
        (self.slow if slow else self.sent).append(copy)
        return copy

    def local(self, src, dst):
        copy = pltpu.make_async_copy(src, dst, self.lsem.at[self.near])
        self.near += 1
        return copy

    def swap(self, w, src, dst):
        far = Maybe(self.make(src, dst, w.swap), w.away, w.away)
        near = self.local(src, dst)
        far.start()
        pl.when(w.home)(near.start)

        def wait():
            far.wait_recv()
            far.wait_send()
            pl.when(w.home)(near.wait)

        return wait

    def plane_swap(self, w, at, to):
        copies = [self.send(at(part), to(w.part), device, True) for device, part in w.plane]
        own = self.local(at(w.part), to(w.part))
        own.start()

        def wait():
            own.wait()
            for copy in copies:
                copy.wait_recv()

        return wait

    def z_all(self, w, src, at):
        copies = [self.send(src, at(w.z), device, True) for device in w.zs]
        own = self.local(src, at(w.z))
        own.start()

        def wait():
            own.wait()
            for copy in copies:
                copy.wait_recv()

        return wait

    def z_spread(self, w, src, land):
        copies = [self.send(src, land.at[k], device, True) for k, device in enumerate(w.zs)]

        def wait():
            for copy in copies:
                copy.wait_recv()

        return wait

    def drain(self):
        for copy in self.sent:
            copy.wait_send()
        self.sent, self.phase = [], 0

    def settle(self):
        self.drain()
        for copy in self.slow:
            copy.wait_send()
        self.slow = []
        for scatter in self.scatters:
            scatter.settle()


class ZGather:
    def __init__(self, net, w, src, at):
        self.w, here = w, at(w.z)
        self.over = net.send(src, here, w.over, True)
        self.up = net.maybe(src, here, w.up, w.z < 3, w.z > 0)
        self.down = net.maybe(src, here, w.down, w.z > 0, w.z < 3)
        far = at(w.far)
        self.on = net.maybe(far, far, w.near_end, w.middle, w.edge)
        self.own = net.local(src, here)
        self.up.start()
        self.down.start()
        self.own.start()

    def poll(self):
        pl.when(self.w.middle)(self.over.wait_recv)
        self.on.start()

    def wait(self):
        pl.when(self.w.edge)(self.over.wait_recv)
        self.own.wait()
        for copy in (self.up, self.down, self.on):
            copy.wait_recv()


class ZScatter:
    def __init__(self, net, w, at, land):
        self.w, self.at, self.land = w, at, land
        self.on = net.maybe(at(w.opposite), land.at[3], w.near_middle, w.edge, w.middle)
        self.on.start()
        self.up = net.maybe(at(lax.rem(w.z + 1, 4)), land.at[0], w.up, w.z < 3, w.z > 0)
        self.down = net.maybe(at(lax.rem(w.z + 3, 4)), land.at[1], w.down, w.z > 0, w.z < 3)
        self.end_over = net.maybe(at(w.far), land.at[2], w.over, w.edge, w.middle)
        self.mid_over = net.maybe(land.at[3], land.at[2], w.over, w.middle, w.edge)
        self.sends = (self.on, self.up, self.down, self.end_over, self.mid_over)
        net.slow = [copy for copy in net.slow if copy not in self.sends]
        net.scatters.append(self)
        for copy in (self.end_over, self.up, self.down):
            copy.start()

        @pl.when(w.z == 0)
        def _():
            land[0] = jnp.zeros(land.shape[1:], BF16)

        @pl.when(w.z == 3)
        def _():
            land[1] = jnp.zeros(land.shape[1:], BF16)

    def poll(self):
        @pl.when(self.w.middle)
        def _():
            self.on.copy.wait_recv()
            own = self.at(self.w.far)[...].astype(F32)
            self.land[3] = (self.land[3].astype(F32) + own).astype(BF16)

        self.mid_over.start()

    def settle(self):
        for copy in self.sends:
            copy.wait_send()
        self.sends = ()

    def total(self):
        for copy in (self.up, self.down, self.end_over, self.mid_over):
            copy.wait_recv()
        land = self.land
        return (
            self.at(self.w.z)[...].astype(F32)
            + land[0].astype(F32)
            + land[1].astype(F32)
            + land[2].astype(F32)
        )


def nothing():
    pass


def gather(net, w, buf, on_group, after_start=nothing, after_forward=None):
    def half(group, h):
        return buf.at[pl.ds(pl.multiple_of((group * 2 + w.c) * 128 + h * 64, 64), 64)]

    def put(group, h, device):
        ref = half(group, h)
        return net.send(ref, ref, device)

    own, xn, yn, diag = w.group
    x0 = put(own, 0, w.xn)
    y1 = put(own, 1, w.yn)
    whole = buf.at[rows_of(w.slot, 128)]
    c0 = net.send(whole, whole, w.sib)
    x1 = put(own, 1, w.xn)
    y0 = put(own, 0, w.yn)
    after_start()
    if after_forward is None:
        c0.wait_recv()
        on_group(OWN)
    x0.wait_recv()
    d0 = put(xn, 0, w.yn)
    cx0 = put(xn, 0, w.sib)
    y1.wait_recv()
    d1 = put(yn, 1, w.xn)
    cy1 = put(yn, 1, w.sib)
    x1.wait_recv()
    cx1 = put(xn, 1, w.sib)
    y0.wait_recv()
    cy0 = put(yn, 0, w.sib)
    if after_forward is not None:
        after_forward()
        c0.wait_recv()
        on_group(OWN)
    cx0.wait_recv()
    cx1.wait_recv()
    on_group(XN)
    cy0.wait_recv()
    cy1.wait_recv()
    on_group(YN)
    d0.wait_recv()
    cd0 = put(diag, 0, w.sib)
    d1.wait_recv()
    cd1 = put(diag, 1, w.sib)
    cd0.wait_recv()
    cd1.wait_recv()
    on_group(DIAG)


class Reduce:
    def __init__(self, net, w, r, part):
        self.net, self.w, self.r, self.part = net, w, r, part
        self.cores = [None] * 4

    def produce(self, kind):
        w, r = self.w, self.r
        group = w.group[kind]
        r.core_out[kind] = self.part(group * 2 + 1 - w.c).astype(BF16)
        self.cores[kind] = self.net.send(r.core_out.at[kind], r.core_in.at[kind], w.sib)
        r.keep[kind] = self.part(group * 2 + w.c)

    def both(self, kind, rows):
        return self.r.keep[kind, rows] + self.r.core_in[kind, rows].astype(F32)

    def diag(self):
        w, r = self.w, self.r
        self.cores[DIAG].wait_recv()
        r.across[...] = self.both(DIAG, slice(0, 128)).astype(BF16)
        self.fy = self.net.send(r.across.at[pl.ds(0, 64)], r.via_y, w.yn)
        self.fx = self.net.send(r.across.at[pl.ds(64, 64)], r.via_x, w.xn)

    def first(self):
        w, r = self.w, self.r
        self.cores[XN].wait_recv()
        r.out_x[64:128] = self.both(XN, slice(64, 128)).astype(BF16)
        self.x1 = self.net.send(r.out_x.at[pl.ds(64, 64)], r.in_x.at[pl.ds(64, 64)], w.xn)
        self.cores[YN].wait_recv()
        r.out_y[0:64] = self.both(YN, slice(0, 64)).astype(BF16)
        self.y0 = self.net.send(r.out_y.at[pl.ds(0, 64)], r.in_y.at[pl.ds(0, 64)], w.yn)

    def second(self):
        w, r = self.w, self.r
        self.fy.wait_recv()
        r.out_x[0:64] = (self.both(XN, slice(0, 64)) + r.via_y[...].astype(F32)).astype(BF16)
        self.x0 = self.net.send(r.out_x.at[pl.ds(0, 64)], r.in_x.at[pl.ds(0, 64)], w.xn)
        self.fx.wait_recv()
        r.out_y[64:128] = (self.both(YN, slice(64, 128)) + r.via_x[...].astype(F32)).astype(BF16)
        self.y1 = self.net.send(r.out_y.at[pl.ds(64, 64)], r.in_y.at[pl.ds(64, 64)], w.yn)

    def total(self):
        r = self.r
        self.cores[OWN].wait_recv()
        for copy in (self.x1, self.y0, self.x0, self.y1):
            copy.wait_recv()
        return self.both(OWN, slice(0, 128)) + r.in_x[...].astype(F32) + r.in_y[...].astype(F32)


def rows_of(group, n=256):
    return pl.ds(pl.multiple_of(group * n, n), n)


def norm_parts(resid):
    mean = jnp.mean(resid, axis=-1, keepdims=True)
    centered = resid - mean
    variance = jnp.mean(centered * centered, axis=-1, keepdims=True)
    root = lax.rsqrt(variance + EPS)
    return centered * root, root


def norm_back(grad, hat, root, gain):
    scaled = grad * gain
    return root * (
        scaled
        - jnp.mean(scaled, axis=-1, keepdims=True)
        - hat * jnp.mean(scaled * hat, axis=-1, keepdims=True)
    )


def column_sum(value):
    return jnp.sum(value, axis=0, keepdims=True)


def by_head(value):
    lanes = lax.broadcasted_iota(jnp.int32, value.shape, 1)
    zero = jnp.zeros_like(value)
    return jnp.concatenate([jnp.where(lanes < 64, value, zero), jnp.where(lanes >= 64, value, zero)], axis=0)


def own_lanes(first, second):
    lanes = lax.broadcasted_iota(jnp.int32, first.shape, 1)
    return jnp.where(lanes < 64, first, second)


def attend_forward(net, w, r, s, before, started, handed, ready, gathered, pump):
    width = r.width
    scale = jnp.asarray((width // ATTENTION_HEADS) ** (-0.5), BF16)
    cross = types.SimpleNamespace()

    gather(net, w, s.all_x, lambda kind: None, started, handed)
    ready()

    def project(i, carry):
        rows = rows_of(i)
        weights = s.w_qkv[...].reshape(width, 384)
        s.qkv[rows] = (dot_nn(s.all_x[rows], weights) + s.part_bias[0:1, 0:384]).astype(BF16)
        return carry

    lax.fori_loop(0, 4, project, 0)
    cross.out = net.send(s.out_z.at[pl.ds(2 * (1 - w.y), 2)], s.w_out.at[:, w.y], w.yn)
    cross.own = net.local(s.out_z.at[pl.ds(2 * w.y, 2)], s.w_out.at[:, w.y])
    cross.own.start()
    def attend(kind, begin=0, end=2):
        def block(i, carry):
            rows = pl.ds(pl.multiple_of(w.group[kind] * 256 + i * 128, 128), 128)
            both = by_head(s.qkv[rows, 0:128] * scale)
            mask = r.docs_col[rows, 0:1] == r.docs_row[0:1, :]
            raw_both = dot_nt(both, s.qkv[:, 128:256])
            probs, logs = [], []
            for h in range(2):
                raw = jnp.where(mask, raw_both[h * 128 : (h + 1) * 128], NEGATIVE)
                top = jnp.max(raw, axis=-1, keepdims=True)
                weight = jnp.exp(raw - top)
                mass = jnp.sum(weight, axis=-1, keepdims=True)
                probs.append((weight * (1.0 / mass)).astype(BF16))
                logs.append(top + jnp.log(mass))
            total = dot_nn(jnp.concatenate(probs, axis=0), s.qkv[:, 256:384])
            s.context[rows] = own_lanes(total[0:128], total[128:256]).astype(BF16)
            s.logs[rows] = own_lanes(
                jnp.broadcast_to(logs[0], (128, 128)), jnp.broadcast_to(logs[1], (128, 128))
            )
            return carry

        lax.fori_loop(begin, end, block, 0)

    def part(slot):
        return dot_nn(s.context[rows_of(slot, 128)], s.w_out[...].reshape(128, width))

    reduce = Reduce(net, w, r, part)
    attend(DIAG)
    cross.out.wait_recv()
    cross.own.wait()
    reduce.produce(DIAG)
    attend(XN, 0, 1)
    reduce.diag()
    attend(XN, 1, 2)
    reduce.produce(XN)
    attend(YN)
    reduce.produce(YN)
    reduce.first()
    gathered()
    pump()
    attend(OWN)
    reduce.produce(OWN)
    reduce.second()
    hat, root = norm_parts(before() + reduce.total() + s.vec[BO : BO + 1])
    normed = hat * s.vec[G1 : G1 + 1] + s.vec[S1 : S1 + 1]
    r.normed[...] = normed
    s.all_n[rows_of(w.slot, 128)] = normed.astype(BF16)
    s.hat_one[...] = hat
    s.root_one[...] = jnp.broadcast_to(root, (128, 128))
    net.drain()


def feed_forward(net, w, r, s, ready_in, ready_ffo, pump):
    def part(slot):
        return dot_nn(s.inner[rows_of(slot, 128)], s.w_ffo[...].reshape(r.share, r.width))

    reduce = Reduce(net, w, r, part)

    def on_group(kind):
        weights = s.w_in[...].reshape(r.width, r.share)
        r.pre[...] = dot_nn(s.all_n[rows_of(w.group[kind])], weights) + s.part_bias[1:2, 0 : r.share]

        def block(i, carry):
            here = pl.ds(pl.multiple_of(i * 32, 32), 32)
            there = pl.ds(pl.multiple_of(w.group[kind] * 256 + i * 32, 32), 32)
            pre = r.pre[here]
            cdf = 0.5 * (1.0 + lax.erf(pre * (0.5**0.5)))
            s.inner[there] = (pre * cdf).astype(BF16)
            bell = jnp.exp(pre * pre * (-0.5)) * ((2.0 * math.pi) ** (-0.5))
            s.slope[there] = (cdf + pre * bell).astype(BF16)
            return carry

        lax.fori_loop(0, 8, block, 0)
        if kind == YN:
            ready_ffo()
            reduce.produce(XN)
            reduce.produce(YN)
            reduce.first()

    gather(net, w, s.all_n, on_group, lambda: pump(0), ready_in)
    reduce.produce(DIAG)
    reduce.diag()
    reduce.produce(OWN)
    reduce.second()
    pump(1)
    hat, root = norm_parts(r.normed[...] + reduce.total() + s.vec[B2 : B2 + 1])
    s.hat_two[...] = hat
    s.root_two[...] = jnp.broadcast_to(root, (128, 128))
    net.drain()
    return hat * s.vec[G2 : G2 + 1] + s.vec[S2 : S2 + 1]


def put_row(ref, row, value):
    for k in range(value.shape[1] // 128):
        ref[row + k : row + k + 1, :] = value[:, k * 128 : (k + 1) * 128]


def feed_backward(net, w, r, s, grad, started, free, pump):
    hat = s.hat_two[...]
    back_two = norm_back(grad, hat, s.root_two[:, 0:1], s.vec[G2 : G2 + 1])
    second = back_two.astype(BF16)
    r.normed[...] = back_two
    r.all_second[rows_of(w.slot, 128)] = second

    def part(slot):
        return dot_nt(r.back_pre[rows_of(slot, 128)], s.w_in[...].reshape(r.width, r.share))

    reduce = Reduce(net, w, r, part)

    def after_start():
        put_row(s.sums, 8 * G2, column_sum(grad * hat))
        put_row(s.sums, 8 * S2, column_sum(grad))
        put_row(s.sums, 8 * B2, column_sum(second.astype(F32)))
        started()

    def on_group(kind):
        rows = rows_of(w.group[kind])
        back_inner = dot_nt(r.all_second[rows], s.w_ffo[...].reshape(r.share, r.width))
        r.back_pre[rows] = (back_inner * s.slope[rows].astype(F32)).astype(BF16)
        if kind == YN:
            reduce.produce(XN)
            reduce.produce(YN)
            reduce.first()

    gather(net, w, r.all_second, on_group, after_start)
    reduce.produce(DIAG)
    reduce.diag()
    reduce.produce(OWN)
    free()

    for z in range(4):
        r.g_ffo[z] = dot_tn(s.inner[:, z * 128 : (z + 1) * 128], r.all_second[...]).astype(BF16)
    s.z_ffo = ZScatter(net, w, lambda z: r.g_ffo.at[z], s.land_ffo)
    reduce.second()

    def in_block(i, carry):
        lanes = pl.ds(pl.multiple_of(i * 256, 256), 256)
        piece = dot_tn(s.all_n[:, lanes], r.back_pre[...]).astype(BF16)
        r.g_in[i] = piece.reshape(4, 64, r.share)
        return carry

    lax.fori_loop(0, 4, in_block, 0)
    s.z_in = ZScatter(net, w, lambda z: r.g_in.at[:, z], s.land_in)
    put_row(s.sums, 50, column_sum(r.back_pre[...].astype(F32)))
    pump()
    grad_one = r.normed[...] + reduce.total()
    hat = s.hat_one[...]
    back_one = norm_back(grad_one, hat, s.root_one[:, 0:1], s.vec[G1 : G1 + 1])
    branch = back_one.astype(BF16)
    r.back_one[...] = back_one
    r.all_branch[rows_of(w.slot, 128)] = branch

    def sums():
        put_row(s.sums, 8 * G1, column_sum(grad_one * hat))
        put_row(s.sums, 8 * S1, column_sum(grad_one))
        put_row(s.sums, 8 * BO, column_sum(branch.astype(F32)))

    return sums


def attend_backward(net, w, r, s, started, pump, done):
    width = r.width
    scale = jnp.asarray((width // ATTENTION_HEADS) ** (-0.5), BF16)

    def after_start():
        r.sum_k[...] = jnp.zeros_like(r.sum_k)
        r.sum_v[...] = jnp.zeros_like(r.sum_v)
        started()

    def on_group(kind):
        rows = rows_of(w.group[kind])
        out_w = s.w_out[...].reshape(128, width)
        r.back_context[rows] = dot_nt(r.all_branch[rows], out_w).astype(BF16)

        def block(i, carry):
            here = pl.ds(pl.multiple_of(w.group[kind] * 256 + i * 128, 128), 128)
            query = by_head(s.qkv[here, 0:128] * scale)
            upstream = by_head(r.back_context[here])
            mask = r.docs_col[here, 0:1] == r.docs_row[0:1, :]
            raw_both = dot_nt(query, s.qkv[:, 128:256])
            back_both = dot_nt(upstream, s.qkv[:, 256:384])
            probs_both, scores_both = [], []
            for h in range(2):
                rows_h = slice(h * 128, (h + 1) * 128)
                raw = jnp.where(mask, raw_both[rows_h], NEGATIVE)
                probs = jnp.exp(raw - s.logs[here, h * 64 : h * 64 + 1])
                back = back_both[rows_h]
                delta = jnp.sum(probs * back, axis=-1, keepdims=True)
                scores_both.append((probs * (back - delta)).astype(BF16))
                probs_both.append(probs.astype(BF16))
            scores = jnp.concatenate(scores_both, axis=0)
            total = dot_nn(scores, s.qkv[:, 128:256])
            r.sum_k[...] += dot_tn(scores, query)
            r.sum_v[...] += dot_tn(jnp.concatenate(probs_both, axis=0), upstream)
            total = own_lanes(total[0:128], total[128:256])
            r.back_qkv[here, 0:128] = (total * scale.astype(F32)).astype(BF16)
            return carry

        lax.fori_loop(0, 2, block, 0)

    gather(net, w, r.all_branch, on_group, after_start)
    r.back_qkv[:, 128:256] = r.sum_k[...].astype(BF16)
    r.back_qkv[:, 256:384] = r.sum_v[...].astype(BF16)

    def part(slot):
        return dot_nt(r.back_qkv[rows_of(slot, 128)], s.w_qkv[...].reshape(width, 384))

    reduce = Reduce(net, w, r, part)
    reduce.produce(DIAG)
    reduce.produce(XN)
    reduce.produce(YN)
    reduce.diag()
    reduce.first()
    put_row(s.sums, 48, column_sum(r.back_qkv[:, 0:128].astype(F32)))
    put_row(s.sums, 49, column_sum(r.back_qkv[:, 256:384].astype(F32)))
    pump(0)

    def qkv_block(i, carry):
        lanes = pl.ds(pl.multiple_of(i * 256, 256), 256)
        piece = dot_tn(s.all_x[:, lanes], r.back_qkv[...]).astype(BF16)
        s.g_qkv[i] = piece.reshape(4, 2, 32, 384)
        return carry

    lax.fori_loop(0, 4, qkv_block, 0)
    s.z_qkv = ZScatter(net, w, lambda z: s.g_qkv.at[:, z], s.land_qkv)
    reduce.produce(OWN)
    reduce.second()
    r.g_out[...] = dot_tn(s.context[...], r.all_branch[...]).astype(BF16).reshape(2, 2, 32, width)
    cross = net.send(r.g_out.at[:, 1 - w.y], s.g_out_z.at[pl.ds(2 * w.y, 2)], w.yn)
    kept = net.local(r.g_out.at[:, w.y], s.g_out_z.at[pl.ds(2 * w.y, 2)])
    kept.start()
    pump(1)
    grad = r.back_one[...] + reduce.total()
    done(grad)
    kept.wait()
    cross.wait_recv()
    s.z_out = ZScatter(net, w, lambda z: s.g_out_z.at[z], s.land_out)


FLAT_ROWS = 96


def whole_kernel(r):
    net = Net(r.ssem, r.rsem, r.lsem)
    w = place()
    layers = len(r.layer)
    first, last = r.layer[0], r.layer[-1]
    width, share = r.width, r.share
    unit = share // 4
    r.docs_mine[...] = jnp.broadcast_to(r.docs[...], (8, 128)).astype(F32)

    def pack_qkv(layer):
        for p in range(8):
            for k in range(3):
                lanes = slice(k * width + p * 128, k * width + (p + 1) * 128)
                r.layer[layer].qkv_parts[p // 2, p % 2, :, k * 128 : (k + 1) * 128] = r.qkv_in[layer, :, lanes]

    def pack_inner(layer):
        for p in range(8):
            for z in range(4):
                at = ((p // 2) * 8 + z * 2 + p % 2) * unit
                r.layer[layer].in_parts[p // 2, p % 2, :, z * unit : (z + 1) * unit] = r.inner_in[
                    layer, :, at : at + unit
                ]

    owner = w.d * 8 + w.z * 2 + w.y
    smalls = ((r.biases, r.n_bias, 0, 3), (r.norm_gains, r.n_gain, 3, 1), (r.value_bias, r.n_value, 4, 1))

    def shifted(size, rows):
        j = lax.broadcasted_iota(jnp.int32, (size, rows * 128), 0)
        k = lax.broadcasted_iota(jnp.int32, (size, rows * 128), 1)
        return jnp.where(k == j + lax.rem(owner * size, 128), 1.0, 0.0)

    def pack_vectors():
        r.vec_f[...] = jnp.zeros_like(r.vec_f)
        for ref, size, row, rows in smalls:
            placed = dot_nn(ref[...], shifted(size, rows).astype(BF16))
            for layer in range(layers):
                for k in range(rows):
                    at = 5 * layer + row + k
                    r.vec_f[at : at + 1, :] = placed[layer : layer + 1, k * 128 : (k + 1) * 128]
        r.vec_in[...] = r.vec_f[...].astype(BF16)

    def unpack_vectors():
        for (_, size, _, rows), base, out in zip(
            smalls, (0, 72, 88), (r.bias_grad, r.gain_grad, r.value_grad)
        ):
            for layer in range(layers):
                begin = layer * FLAT_ROWS + base + lax.div(owner * size, 128)
                for k in range(rows):
                    r.lined[layer : layer + 1, k * 128 : (k + 1) * 128] = r.vectors[pl.ds(begin + k, 1), :]
            out[...] = lax.dot_general(
                r.lined[:, 0 : rows * 128],
                shifted(size, rows),
                (((1,), (1,)), ((), ())),
                precision=lax.Precision.HIGHEST,
                preferred_element_type=F32,
            )[0:layers]

    def of_part(ref):
        return lambda p: ref.at[lax.div(p, 2), lax.rem(p, 2)]

    met = net.greet(w)
    pack_vectors()
    pack_qkv(0)
    pack_inner(0)
    met()
    parts = net.plane_swap(w, of_part(first.qkv_parts), of_part(first.qkv_piece))
    hidden = net.swap(w, r.hidden, r.hidden_row)
    docs = net.swap(w, r.docs_mine, r.docs_own)
    vec = net.z_all(w, r.vec_in, lambda z: r.vec_z.at[z])
    parts()
    first.zg_qkv = ZGather(net, w, first.qkv_piece, lambda z: first.w_qkv.at[:, z])
    first.zg_out = ZGather(net, w, r.out_in.at[0], lambda z: first.out_z.at[z])
    first.in_parted = net.plane_swap(w, of_part(first.in_parts), of_part(first.in_piece))
    vec()
    spread = net.plane_swap(w, lambda p: r.vec_z, lambda p: r.vec_all.at[p])
    docs()
    docs = net.plane_swap(w, lambda p: r.docs_own, lambda p: r.docs_all.at[p])
    hidden()
    first.all_x[rows_of(w.slot, 128)] = r.hidden_row[...]

    def unpack():
        spread()
        r.flat[...] = jnp.zeros_like(r.flat)
        for p in range(8):
            for z in range(4):
                owner = (p // 2) * 8 + z * 2 + p % 2
                piece = r.vec_all[p, z].astype(F32)
                for layer in range(layers):
                    base = layer * FLAT_ROWS
                    at = base + r.n_bias * owner // 128
                    r.flat[at : at + 3, :] += piece[5 * layer : 5 * layer + 3]
                    at = base + 72 + r.n_gain * owner // 128
                    r.flat[at : at + 1, :] += piece[5 * layer + 3 : 5 * layer + 4]
                    at = base + 88 + r.n_value * owner // 128
                    r.flat[at : at + 1, :] += piece[5 * layer + 4 : 5 * layer + 5]
        for layer in range(layers):
            s, base = r.layer[layer], layer * FLAT_ROWS
            for row, name in ((G1, 72), (S1, 56), (BO, 8), (G2, 80), (S2, 64), (B2, 48)):
                for k in range(8):
                    s.vec[row : row + 1, k * 128 : (k + 1) * 128] = r.flat[
                        base + name + k : base + name + k + 1, :
                    ]
            s.part_bias[...] = jnp.zeros_like(s.part_bias)
            s.part_bias[0:1, 0:128] = r.flat[pl.ds(base + w.part, 1), :]
            s.part_bias[0:1, 256:384] = r.flat[pl.ds(base + 88 + w.part, 1), :]
            for z in range(4):
                s.part_bias[1:2, z * unit : (z + 1) * unit] = r.flat[
                    pl.ds(base + 16 + 8 * w.d + 2 * z + w.y, 1), :
                ]
        docs()
        for p in range(8):
            slot = (p // 4) * 4 + (p % 2) * 2 + (p // 2) % 2
            numbers = r.docs_all[p]
            r.docs_row[:, slot * 128 : (slot + 1) * 128] = numbers
            r.docs_col[slot * 128 : (slot + 1) * 128, :] = jnp.broadcast_to(numbers[0:1], (128, 128)).T

    def bring_attention(layer):
        s = r.layer[layer]
        s.zg_qkv = ZGather(net, w, s.qkv_piece, lambda z: s.w_qkv.at[:, z])
        s.zg_out = ZGather(net, w, r.out_in.at[layer], lambda z: s.out_z.at[z])

    def bring_in(layer):
        s = r.layer[layer]
        s.zg_qkv.poll()
        s.zg_out.poll()
        s.zg_in = ZGather(net, w, s.in_piece, lambda z: s.w_in.at[:, z])
        s.zg_ffo = ZGather(net, w, r.ffo_in.at[layer], lambda z: s.w_ffo.at[z])

    def bring_ffo(layer):
        s = r.layer[layer]
        s.zg_in.poll()

    swaps = types.SimpleNamespace()
    for layer in range(layers):
        s = r.layer[layer]

        def started(layer=layer):
            if layer == 0:
                unpack()

        def handed(layer=layer, s=s):
            if layer == 0:
                s.in_parted()
                bring_in(0)

        def ready(s=s):
            s.zg_qkv.wait()
            s.zg_out.wait()

        def gathered(layer=layer):
            if layer + 1 < layers:
                n = r.layer[layer + 1]
                pack_qkv(layer + 1)
                pack_inner(layer + 1)
                n.qkv_parted = net.plane_swap(w, of_part(n.qkv_parts), of_part(n.qkv_piece))
                n.in_parted = net.plane_swap(w, of_part(n.in_parts), of_part(n.in_piece))

        def before(layer=layer):
            return r.hidden_row[...].astype(F32) if layer == 0 else r.state[...]

        attend_forward(
            net, w, r, s, before, started, handed, ready, gathered, lambda layer=layer: bring_ffo(layer)
        )

        def ready_in(s=s):
            s.zg_in.wait()

        def ready_ffo(s=s):
            s.zg_ffo.wait()

        def pump(at, layer=layer, s=s):
            if at == 0:
                s.zg_ffo.poll()
                if layer + 1 < layers:
                    r.layer[layer + 1].qkv_parted()
                    r.layer[layer + 1].in_parted()
                    bring_attention(layer + 1)
            elif layer + 1 < layers:
                bring_in(layer + 1)
            else:
                swaps.grad = net.swap(w, r.out_grad, r.grad_row)

        state = feed_forward(net, w, r, s, ready_in, ready_ffo, pump)
        r.state[...] = state
        if layer + 1 < layers:
            r.layer[layer + 1].all_x[rows_of(w.slot, 128)] = state.astype(BF16)
        else:
            r.state_low[...] = state.astype(BF16)
    swaps.grad()
    net.settle()
    swaps.out = net.swap(w, r.state_low, r.out)
    grad = r.grad_row[...].astype(F32)

    def vectors_out(s):
        return net.z_spread(w, s.sums, s.sums_z)

    def vectors_plane(s, wait):
        wait()
        s.sums_own[...] = s.sums[...] + s.sums_z[0] + s.sums_z[1] + s.sums_z[2]
        return net.plane_swap(w, lambda p: s.sums_own, lambda p: s.sums_all.at[p])

    def vectors_in(layer, s, wait):
        wait()
        base = layer * FLAT_ROWS
        for row, name in ((G1, 72), (S1, 56), (BO, 8), (G2, 80), (S2, 64), (B2, 48)):
            total = s.sums_all[0, 8 * row : 8 * row + 8]
            for p in range(1, 8):
                total = total + s.sums_all[p, 8 * row : 8 * row + 8]
            r.vectors[base + name : base + name + 8, :] = total
        for p in range(8):
            r.vectors[base + p : base + p + 1, :] = s.sums_all[p, 48:49]
            r.vectors[base + 88 + p : base + 89 + p, :] = s.sums_all[p, 49:50]
            for z in range(4):
                at = base + 16 + 8 * (p // 2) + 2 * z + p % 2
                r.vectors[at : at + 1, :] = s.sums_all[p, 50 + z : 51 + z]

    def send_inner(s):
        s.in_parts[...] = s.z_in.total().astype(BF16).reshape(4, 2, 32, share)
        return net.plane_swap(w, of_part(s.in_parts), of_part(s.in_piece))

    def send_qkv(s):
        s.qkv_parts[...] = s.z_qkv.total().astype(BF16)
        return net.plane_swap(w, of_part(s.qkv_parts), of_part(s.qkv_piece))

    def place_inner(layer, s, wait):
        wait()
        for p in range(8):
            for z in range(4):
                at = ((p // 2) * 8 + z * 2 + p % 2) * unit
                r.in_grad[layer, :, at : at + unit] = s.in_piece[
                    p // 2, p % 2, :, z * unit : (z + 1) * unit
                ].astype(F32)

    def place_qkv(layer, s, wait):
        wait()
        for p in range(8):
            for k in range(3):
                lanes = slice(k * width + p * 128, k * width + (p + 1) * 128)
                r.qkv_grad[layer, :, lanes] = s.qkv_piece[
                    p // 2, p % 2, :, k * 128 : (k + 1) * 128
                ].astype(F32)

    for layer in reversed(range(layers)):
        s = r.layer[layer]
        a = r.layer[layer + 1] if layer + 1 < layers else None
        s.sums[...] = jnp.zeros_like(s.sums)

        def feed_started(layer=layer, a=a):
            if a is not None:
                r.ffo_grad[layer + 1] = a.z_ffo.total()
                a.in_wait = send_inner(a)

        def free(a=a):
            if a is not None:
                a.z_ffo.settle()
                a.z_in.settle()
                a.z_qkv.poll()
                a.z_out.poll()

        def feed_pump(a=a):
            if a is not None:
                a.vec_wait = vectors_plane(a, a.vec_wait)

        sums = feed_backward(net, w, r, s, grad, feed_started, free, feed_pump)
        if a is None:
            swaps.out()
        net.drain()

        def back_started(layer=layer, a=a, sums=sums):
            sums()
            if a is not None:
                place_inner(layer + 1, a, a.in_wait)
                r.out_grad_w[layer + 1] = a.z_out.total()
                a.qkv_wait = send_qkv(a)
                vectors_in(layer + 1, a, a.vec_wait)

        def back_pump(at, s=s):
            if at == 0:
                s.z_ffo.poll()
                s.vec_wait = vectors_out(s)
            else:
                s.z_in.poll()

        def done(grad, layer=layer):
            if layer:
                r.state[...] = grad
            else:
                first.z_qkv.poll()
                r.state_low[...] = grad.astype(BF16)
                swaps.back = net.swap(w, r.state_low, r.input_grad)

        attend_backward(net, w, r, s, back_started, back_pump, done)
        if layer:
            grad = r.state[...]
            net.drain()
    r.ffo_grad[0] = first.z_ffo.total()
    first.in_wait = send_inner(first)
    if layers > 1:
        place_qkv(1, r.layer[1], r.layer[1].qkv_wait)
    first.vec_wait = vectors_plane(first, first.vec_wait)
    first.z_out.poll()
    place_inner(0, first, first.in_wait)
    vectors_in(0, first, first.vec_wait)
    first.qkv_wait = send_qkv(first)
    r.out_grad_w[0] = first.z_out.total()
    swaps.back()
    unpack_vectors()
    place_qkv(0, first, first.qkv_wait)
    net.settle()


def plane_body(
    hidden_in,
    document_index,
    out_grad,
    qkv_weight,
    value_bias,
    attention_output_weight,
    ffn_in_weight,
    ffn_out_weight,
    biases,
    norm_gains,
):
    layers = qkv_weight.shape[0]
    width = hidden_in.shape[1]
    inner = ffn_in_weight.shape[2]
    share = inner // 8
    n_bias, n_gain, n_value = biases.shape[1], norm_gains.shape[1], value_bias.shape[1]

    ins = dict(
        hidden=hidden_in,
        docs=document_index,
        out_grad=out_grad,
        qkv_in=qkv_weight,
        out_in=attention_output_weight,
        inner_in=ffn_in_weight,
        ffo_in=ffn_out_weight,
        biases=biases,
        norm_gains=norm_gains,
        value_bias=value_bias,
    )
    outs = dict(
        out=((128, width), BF16),
        input_grad=((128, width), BF16),
        qkv_grad=(qkv_weight.shape, F32),
        out_grad_w=(attention_output_weight.shape, F32),
        in_grad=(ffn_in_weight.shape, F32),
        ffo_grad=(ffn_out_weight.shape, F32),
        bias_grad=((layers, n_bias), F32),
        gain_grad=((layers, n_gain), F32),
        value_grad=((layers, n_value), F32),
    )
    far = dict(hidden=1, out_grad=1, ffo_in=1, out_in=1, out=1, input_grad=1)
    whole = (1024, width)
    shared = dict(
        hidden_row=((128, width), BF16),
        grad_row=((128, width), BF16),
        docs_mine=((8, 128), F32),
        docs_own=((8, 128), F32),
        docs_all=((8, 8, 128), F32),
        docs_row=((8, 1024), F32),
        docs_col=((1024, 128), F32),
        vec_f=((16, 128), F32),
        vec_in=((16, 128), BF16),
        lined=((8, 384), F32),
        vectors=((layers * FLAT_ROWS, 128), F32),
        vec_z=((4, 16, 128), BF16),
        vec_all=((8, 4, 16, 128), BF16),
        flat=((layers * FLAT_ROWS, 128), F32),
        normed=((128, width), F32),
        state=((128, width), F32),
        state_low=((128, width), BF16),
        back_one=((128, width), F32),
        pre=((256, share), F32),
        all_second=(whole, BF16),
        all_branch=(whole, BF16),
        back_pre=((1024, share), BF16),
        back_context=((1024, 128), BF16),
        back_qkv=((1024, 384), BF16),
        sum_k=((1024, 128), F32),
        sum_v=((1024, 128), F32),
        g_out=((2, 2, 32, width), BF16),
        g_ffo=((4, 128, width), BF16),
        g_in=((4, 4, 64, share), BF16),
        core_out=((4, 128, width), BF16),
        core_in=((4, 128, width), BF16),
        keep=((4, 128, width), F32),
        across=((128, width), BF16),
        via_x=((64, width), BF16),
        via_y=((64, width), BF16),
        out_x=((128, width), BF16),
        out_y=((128, width), BF16),
        in_x=((128, width), BF16),
        in_y=((128, width), BF16),
    )
    each = dict(
        qkv_parts=((4, 2, 32, 384), BF16),
        qkv_piece=((4, 2, 32, 384), BF16),
        in_parts=((4, 2, 32, share), BF16),
        in_piece=((4, 2, 32, share), BF16),
        w_qkv=((4, 4, 2, 32, 384), BF16),
        w_in=((4, 4, 2, 32, share), BF16),
        w_ffo=((4, 128, width), BF16),
        out_z=((4, 32, width), BF16),
        w_out=((2, 2, 32, width), BF16),
        vec=((8, width), F32),
        part_bias=((8, width), F32),
        all_x=(whole, BF16),
        qkv=((1024, 384), BF16),
        context=((1024, 128), BF16),
        logs=((1024, 128), F32),
        all_n=(whole, BF16),
        inner=((1024, share), BF16),
        slope=((1024, share), BF16),
        hat_one=((128, width), F32),
        root_one=((128, 128), F32),
        hat_two=((128, width), F32),
        root_two=((128, 128), F32),
        g_qkv=((4, 4, 2, 32, 384), BF16),
        g_out_z=((4, 32, width), BF16),
        land_ffo=((4, 128, width), BF16),
        land_in=((4, 4, 64, share), BF16),
        land_qkv=((4, 4, 2, 32, 384), BF16),
        land_out=((4, 32, width), BF16),
        sums=((56, 128), F32),
        sums_z=((3, 56, 128), F32),
        sums_own=((56, 128), F32),
        sums_all=((8, 56, 128), F32),
    )

    def kernel(*refs):
        refs = list(refs)

        def take(names):
            return dict(zip(names, [refs.pop(0) for _ in names]))

        r = types.SimpleNamespace(
            width=width, share=share, n_bias=n_bias, n_gain=n_gain, n_value=n_value, **take(ins), **take(outs), **take(shared)
        )
        r.layer = [types.SimpleNamespace(**take(each)) for _ in range(layers)]
        r.ssem, r.rsem, r.lsem = refs
        whole_kernel(r)

    def held(items):
        return [VMEM(shape, dtype) for shape, dtype in items.values()]

    results = pl.pallas_call(
        kernel,
        out_shape=[jax.ShapeDtypeStruct(shape, dtype) for shape, dtype in outs.values()],
        in_specs=[pl.BlockSpec(memory_space=pl.ANY if name in far else VMEM) for name in ins],
        out_specs=[pl.BlockSpec(memory_space=pl.ANY if name in far else VMEM) for name in outs],
        scratch_shapes=[
            *held(shared),
            *(held(each) * layers),
            pltpu.SemaphoreType.DMA((COPIES,)),
            pltpu.SemaphoreType.DMA((COPIES,)),
            pltpu.SemaphoreType.DMA((48,)),
        ],
        compiler_params=pltpu.CompilerParams(
            collective_id=0, has_side_effects=True, vmem_limit_bytes=VMEM_LIMIT
        ),
    )(*ins.values())
    out, input_grad, g_qkv, g_out, g_in, g_ffo, g_bias, g_gain, g_value = results
    return in_place((out, input_grad, g_qkv, g_value, g_out, g_in, g_ffo, g_bias, g_gain))


def in_place(results):
    last = len(results)

    def kernel(*refs):
        sems = refs[-1]
        copies = [
            pltpu.make_async_copy(refs[k], refs[last + k], sems.at[k]) for k in range(last) if k != 1
        ]
        for copy in copies:
            copy.start()
        refs[last + 1][...] = refs[1][...].astype(F32)
        for copy in copies:
            copy.wait()

    return pl.pallas_call(
        kernel,
        out_shape=[jax.ShapeDtypeStruct(v.shape, F32 if k == 1 else v.dtype) for k, v in enumerate(results)],
        in_specs=[pl.BlockSpec(memory_space=VMEM)] * last,
        out_specs=[pl.BlockSpec(memory_space=VMEM if k == 1 else pl.ANY) for k in range(last)],
        scratch_shapes=[pltpu.SemaphoreType.DMA((last,))],
    )(*results)


def fits_plane(mesh):
    return mesh.shape[DP] == 4 and mesh.shape[CTX] == 8


def solution(mesh):
    return jax.shard_map(
        plane_body if fits_plane(mesh) else body,
        mesh=mesh,
        in_specs=(
            P(BOTH, None),
            P(DP, CTX),
            P(BOTH, None),
            P(None, BOTH, None),
            P(None, BOTH),
            P(None, BOTH, None),
            P(None, BOTH, None),
            P(None, BOTH, None),
            P(None, BOTH),
            P(None, BOTH),
        ),
        out_specs=(
            P(BOTH, None),
            P(BOTH, None),
            P(None, BOTH, None),
            P(None, BOTH),
            P(None, BOTH, None),
            P(None, BOTH, None),
            P(None, BOTH, None),
            P(None, BOTH),
            P(None, BOTH),
        ),
        check_vma=False,
    )
```
